32 devices in a mesh: fsdp: 2 (over core), expert: 16 (over z, y, x).
Axes of the slice: x: 2, y: 2, z: 4, core: 2. Of those that a mesh axis runs over, the one named last changes fastest.
Arguments:
- tokens: bfloat16 [16, 256, 2048], P('expert', 'fsdp'), may hold values from -6 to 6
- norm1_gain: bfloat16 [2048], P(('fsdp', 'expert')), may hold values from 0.5 to 1.5
- q_weight: bfloat16 [2048, 3072], P(('fsdp', 'expert')), may hold values from -0.125 to 0.125
- kv_down: bfloat16 [2048, 576], P(('fsdp', 'expert')), may hold values from -0.125 to 0.125
- latent_gain: bfloat16 [512], P(('fsdp', 'expert')), may hold values from 0.5 to 1.5
- kv_up: bfloat16 [512, 4096], P(('fsdp', 'expert')), may hold values from -0.25 to 0.25
- o_weight: bfloat16 [2048, 2048], P(('fsdp', 'expert')), may hold values from -1 to 1
- norm2_gain: bfloat16 [2048], P(('fsdp', 'expert')), may hold values from 0.5 to 1.5
- router: bfloat16 [2048, 16], P(('fsdp', 'expert')), may hold values from -0.0625 to 0.0625
- shared_gate_up: bfloat16 [2048, 5632], P(('fsdp', 'expert')), may hold values from -0.125 to 0.125
- shared_down: bfloat16 [2816, 2048], P(('fsdp', 'expert')), may hold values from -0.109375 to 0.109375
- expert_gate_up: bfloat16 [16, 2048, 2816], P('expert', 'fsdp'), may hold values from -0.125 to 0.125
- expert_down: bfloat16 [16, 1408, 2048], P('expert', None, 'fsdp'), may hold values from -0.4375 to 0.4375
- teacher: bfloat16 [16, 256, 2048], P('expert', 'fsdp'), may hold values from -10 to 10
- routes: int32 [16, 256, 6], P('expert', 'fsdp'), may hold values from 0 to 15, all different within a row; in each aligned block of 128 rows (0 to 127, 128 to 255, ..., all dimensions but the last counted through in order) at most 80 rows name the same one
- prefix: int32 [16], P('expert'), may hold values from 25 to 128
- token_count: int32 [1], replicated, may hold values from 2048 to 4096
Outputs:
- mixed: bfloat16 [16, 256, 2048], P('expert', 'fsdp')
- loss_value: float32 [1], replicated
- grad_tokens: float32 [16, 256, 2048], P('expert', 'fsdp')
- grad_norm1_gain: float32 [2048], P(('fsdp', 'expert'))
- grad_q_weight: float32 [2048, 3072], P(('fsdp', 'expert'))
- grad_kv_down: float32 [2048, 576], P(('fsdp', 'expert'))
- grad_latent_gain: float32 [512], P(('fsdp', 'expert'))
- grad_kv_up: float32 [512, 4096], P(('fsdp', 'expert'))
- grad_o_weight: float32 [2048, 2048], P(('fsdp', 'expert'))
- grad_norm2_gain: float32 [2048], P(('fsdp', 'expert'))
- grad_router: float32 [2048, 16], P(('fsdp', 'expert'))
- grad_shared_gate_up: float32 [2048, 5632], P(('fsdp', 'expert'))
- grad_shared_down: float32 [2816, 2048], P(('fsdp', 'expert'))
- grad_expert_gate_up: float32 [16, 2048, 2816], P('expert', 'fsdp')
- grad_expert_down: float32 [16, 1408, 2048], P('expert', None, 'fsdp')
The draws below stay inside these ranges and needn't reach their ends.
Inputs may be any that keep to these rules, and one draw needn't show every extreme that they name: `routes`: each token names 6 different experts. Among the 128 tokens of one device no expert is named by more than 80 tokens, and in every draw some expert is named by exactly 80 tokens of some device.
All inputs are finite; a program needn't handle non-finite values.
Results may differ from the reference program's by a relative error of at most 0.015.
Values may be sent and summed in bfloat16 or wider, within the bound.
No kernel may reach another device: no remote copies, remote signals or barrier semaphores. Data moves between devices by JAX's collectives and lax.ppermute only.
A program may use at most 448 MiB of HBM per device.

```python
import math
import jax
import jax.numpy as jnp
import numpy as np
from jax import lax

D = 2048
NH = 16
DN = 128
DR = 64
DV = 128
KVR = 512
FFE = 1408
FFS = 2816
TOP = 6
TOK_DEV = 128
EXPERTS = 16
LEN = 256
SEQS = 16
TOKENS = 4096
CAP = 80


def draw_teacher(key, part):
    key = jax.random.fold_in(key, 11)
    place = jnp.arange(LEN, dtype=jnp.float32).reshape(1, LEN, 1)
    which = jnp.arange(SEQS, dtype=jnp.float32).reshape(SEQS, 1, 1) / SEQS
    index = (place + which) / LEN
    growth = 0.25 + 2.25 * index
    samples = jnp.clip(jax.random.normal(key, (SEQS, LEN, D), jnp.float32), -4.0, 4.0)
    return (growth * samples).astype(jnp.bfloat16)


def plant(result, rng, smallest, high):
    longest = result.shape.index(max(result.shape))
    spots = []
    for shift in (0, 1):
        where = [jax.random.randint(jax.random.fold_in(rng, axis), (), 0, length) for axis, length in enumerate(result.shape)]
        where[longest] = (where[longest] + shift) % result.shape[longest]
        spots.append(tuple(where))
    return result.at[spots[0]].set(smallest).at[spots[1]].set(high)


def level_of(key, shape, shards, smallest, largest):
    level = 1.0
    for dim, shards_of in shards:
        draws = jax.random.uniform(jax.random.fold_in(jax.random.fold_in(key, 6), dim), (shards_of,), jnp.float32, smallest / len(shards), largest / len(shards))
        level = level * jnp.repeat(jnp.exp(draws), shape[dim] // shards_of).reshape((-1,) + (1,) * (len(shape) - 1 - dim))
    return level


def assign_block(key, own, number, rows, count, top, bound, lean):
    ranking = jax.random.permutation(key, count)
    heavy_load, ordinary = portions_of(count, rows * top, bound, lean, True), portions_of(count, rows * top, bound, lean, False)
    places = jnp.arange(count)

    def named(sizes, turn):
        used = int((sizes > 0).sum())
        fixed = max(1, used // 4)
        passed = fixed + (places - fixed + turn * (used - fixed)) % max(1, count - fixed)
        return jnp.zeros((count,), jnp.int32).at[ranking[jnp.where(places < fixed, places, passed)]].set(jnp.asarray(sizes, jnp.int32))

    sizes = jnp.where(number % 4 == 0, named(heavy_load, number // 4), named(ordinary, number - number // 4 - 1))
    mixed = jax.random.permutation(jax.random.fold_in(own, 3), count)
    donor, sink = mixed[0:count // 2 * 2:2], mixed[1:count // 2 * 2:2]
    slack = jnp.minimum(sizes[donor] - 1, bound - sizes[sink]) // 2
    slack = jnp.where((donor == ranking[0]) | (sink == ranking[0]) | (sizes[sink] == 0), 0, jnp.maximum(slack, 0))
    passed = jax.random.randint(jax.random.fold_in(own, 4), (count // 2,), 0, 1 << 20) % (slack + 1)
    sizes = sizes.at[donor].add(-passed).at[sink].add(passed)
    members = jnp.searchsorted(jnp.cumsum(sizes), jnp.arange(rows * top), side="right").astype(jnp.int32)
    table = members.reshape(top, rows).T
    table = table[jax.random.permutation(jax.random.fold_in(own, 1), rows)]
    turn = jax.random.randint(jax.random.fold_in(own, 2), (rows, 1), 0, top)
    return jnp.take_along_axis(table, (jnp.arange(top)[None, :] + turn) % top, axis=1)


def portions_of(number_of, total, limit, slope, full):
    loads = [(1 << 20) // math.isqrt(grade ** slope) + 1 for grade in range(1, number_of + 1)]
    largest = limit if full else min(limit, max(-(-total // number_of), total * loads[0] // sum(loads)))
    least = 1 if total - largest >= number_of - 1 else 0
    given, surplus = [largest] + [least] * (number_of - 1), total - largest - least * (number_of - 1)
    while surplus > 0:
        candidates = [i for i in range(1, number_of) if given[i] < largest] or [i for i in range(1, number_of) if given[i] < limit]
        whole, remaining = sum([loads[i] for i in candidates]), surplus
        for i in candidates:
            more = min(limit - given[i], max(1, remaining * loads[i] // whole), surplus)
            given[i] = given[i] + more
            surplus = surplus - more
    return np.array(given)


def gaussian(rng, shape, deviation, reach, cuts=(), kind=jnp.bfloat16):
    level = level_of(rng, shape, cuts, -0.22, 0.18) if cuts else 1.0
    array = jax.random.normal(rng, shape, jnp.float32) * deviation * level
    return jnp.minimum(jnp.maximum(array, -reach), reach).astype(kind)


def setup_inputs(seed: int = 0) -> dict:
    keys = jax.random.split(jax.random.key(seed), 18)
    tokens = gaussian(keys[0], (SEQS, LEN, D), 1.0, 6.0, ((0, 16), (1, 2)))
    norm1_gain = jnp.clip(1.0 + 0.1 * jax.random.normal(keys[1], (D,), jnp.float32), 0.5, 1.5).astype(jnp.bfloat16)
    q_weight = gaussian(keys[2], (D, NH * (DN + DR)), D ** -0.5, 0.125, ((0, 32),))
    kv_down = gaussian(keys[3], (D, KVR + DR), D ** -0.5, 0.125, ((0, 32),))
    latent_gain = jnp.clip(1.0 + 0.1 * jax.random.normal(keys[4], (KVR,), jnp.float32), 0.5, 1.5).astype(jnp.bfloat16)
    kv_up = gaussian(keys[5], (KVR, NH * (DN + DV)), KVR ** -0.5, 0.25, ((0, 32),))
    o_weight = gaussian(keys[6], (NH * DV, D), (NH * DV * 4 // LEN) ** -0.5, 1.0, ((0, 32),))
    norm2_gain = jnp.clip(1.0 + 0.1 * jax.random.normal(keys[7], (D,), jnp.float32), 0.5, 1.5).astype(jnp.bfloat16)
    router = gaussian(keys[8], (D, EXPERTS), (4 * D) ** -0.5, 0.0625, ((0, 32),))
    shared_gate_up = gaussian(keys[9], (D, 2 * FFS), D ** -0.5, 0.125, ((0, 32),))
    shared_down = gaussian(keys[10], (FFS, D), FFS ** -0.5, 0.109375, ((0, 32),))
    expert_gate_up = gaussian(keys[11], (EXPERTS, D, 2 * FFE), D ** -0.5, 0.125, ((0, 16), (1, 2)))
    expert_down = gaussian(keys[12], (EXPERTS, FFE, D), (FFE // 8) ** -0.5, 0.4375, ((0, 16), (2, 2)))
    teacher = draw_teacher(jax.random.fold_in(keys[17], 71), 0)
    routes_keys = jax.random.split(jax.random.fold_in(keys[14], 1), SEQS * LEN // TOK_DEV)
    routes_turns = jax.random.permutation(jax.random.fold_in(keys[14], 3), SEQS * LEN // TOK_DEV)
    routes = jax.vmap(lambda own, number: assign_block(jax.random.fold_in(keys[14], 2), own, number, TOK_DEV, EXPERTS, TOP, CAP, 1))(routes_keys, routes_turns).reshape((SEQS, LEN, TOP))
    prefix = plant(jax.random.randint(keys[15], (SEQS,), max(1, LEN // 10), LEN // 2 + 1), jax.random.fold_in(keys[15], 1), max(1, LEN // 10), (LEN // 2 + 1) - 1).astype(jnp.int32)
    token_count = jax.random.randint(keys[16], (1,), TOKENS // 2, TOKENS + 1).astype(jnp.int32)
    return dict(tokens=tokens, norm1_gain=norm1_gain, q_weight=q_weight, kv_down=kv_down, latent_gain=latent_gain, kv_up=kv_up, o_weight=o_weight, norm2_gain=norm2_gain, router=router, shared_gate_up=shared_gate_up, shared_down=shared_down, expert_gate_up=expert_gate_up, expert_down=expert_down, teacher=teacher, routes=routes, prefix=prefix, token_count=token_count)


highest = lax.Precision.HIGHEST
epsilon = 1e-06

@jax.custom_vjp
def low(v):
    return lax.optimization_barrier(v.astype(jnp.bfloat16)).astype(jnp.float32)

@jax.custom_vjp
def low_back(v):
    return v

def low_keep(v):
    return (low(v), None)

def low_pass(kept, grad):
    return (grad,)

def back_keep(v):
    return (v, None)

def back_low(kept, grad):
    return (low(grad),)
low.defvjp(low_keep, low_pass)
low_back.defvjp(back_keep, back_low)

def both_round(values):
    return low_back(low(values))

def matmul(left_side, right_side):
    return jnp.dot(left_side, right_side, precision=highest)

def rms_norm(values, gain_row):
    return values * lax.rsqrt(lax.optimization_barrier(jnp.mean(values * values, axis=-1, keepdims=True)) + epsilon) * gain_row

def tables(position, rot_width):
    half_width = rot_width // 2
    frequency = 10000.0 ** (-2.0 * jnp.arange(half_width, dtype=jnp.float32) / rot_width)
    angles = position.astype(jnp.float32)[:, None] * frequency[None, :]
    return (jnp.cos(angles), jnp.sin(angles))

def rotate(values, cosine, sine_table):
    half_width = values.shape[-1] // 2
    first_half = values[..., :half_width]
    second = values[..., half_width:]
    return jnp.concatenate([first_half * cosine - second * sine_table, first_half * sine_table + second * cosine], axis=-1)

def slot_select(route_rows):
    matches = (route_rows[:, :, None] == jnp.arange(EXPERTS, dtype=jnp.int32)[None, None, :]).astype(jnp.int32)
    owned_count = lax.optimization_barrier(jnp.sum(matches, axis=1)).astype(jnp.int32)
    before = (jnp.cumsum(owned_count, axis=0) - owned_count).astype(jnp.int32)
    rank_rows = lax.optimization_barrier(jnp.sum(matches * before[:, None, :], axis=2)).astype(jnp.int32)
    slot_index = (route_rows * CAP + rank_rows).astype(jnp.int32)
    return (matches, slot_index[:, :, None] == jnp.arange(EXPERTS * CAP, dtype=jnp.int32)[None, None, :])

def attend(queries, keyval, key_rope, prefix_len):
    length = queries.shape[0]
    scaling = (DN + DR) ** (-0.5)
    nope_part = jnp.einsum('qhd,khd->hqk', queries[..., :DN], keyval[..., :DN], precision=highest)
    rope_part = jnp.einsum('qhr,kr->hqk', queries[..., DN:], key_rope, precision=highest)
    scores = low_back((nope_part + rope_part) * scaling)
    row_index = jnp.arange(length, dtype=jnp.int32)[:, None]
    col_index = jnp.arange(length, dtype=jnp.int32)[None, :]
    visible = (col_index <= row_index) | (col_index < prefix_len)
    scores = jnp.where(visible[None], scores, -1e+30)
    attention = low(jax.nn.softmax(scores, axis=-1))
    context = jnp.einsum('hqk,khv->qhv', attention, keyval[..., DN:], precision=highest)
    return both_round(context.reshape(length, NH * DV))

def forward(params, routes, prefix):
    tokens, norm1_gain, q_weight, kv_down, latent_gain, kv_up, o_weight, norm2_gain, router, shared_gate_up, shared_down, expert_gate_up, expert_down = params
    flat_rows = tokens.reshape(TOKENS, D)
    normed = low(rms_norm(flat_rows, norm1_gain))
    position = jnp.tile(jnp.arange(LEN, dtype=jnp.int32), SEQS)
    cosine, sine_table = tables(position, DR)
    query_raw = low_back(matmul(normed, q_weight)).reshape(TOKENS, NH, DN + DR)
    queries = low(jnp.concatenate([query_raw[..., :DN], rotate(query_raw[..., DN:], cosine[:, None, :], sine_table[:, None, :])], axis=-1))
    latent = low_back(matmul(normed, kv_down))
    compressed = low(rms_norm(latent[:, :KVR], latent_gain))
    key_rope = low(rotate(latent[:, KVR:], cosine, sine_table))
    keyval = both_round(matmul(compressed, kv_up)).reshape(TOKENS, NH, DN + DV)

    def sequence_step(running, pieces):
        return (running, attend(pieces[0], pieces[1], pieces[2], pieces[3]))
    running, context = lax.scan(jax.checkpoint(sequence_step), jnp.zeros((), jnp.float32), (queries.reshape(SEQS, LEN, NH, DN + DR), keyval.reshape(SEQS, LEN, NH, DN + DV), key_rope.reshape(SEQS, LEN, DR), prefix))
    hidden = flat_rows + low_back(matmul(context.reshape(TOKENS, NH * DV), o_weight))
    normed2 = low(rms_norm(hidden, norm2_gain))
    shared_both = low_back(matmul(normed2, shared_gate_up))
    shared_act = low(jax.nn.silu(shared_both[:, :FFS]) * shared_both[:, FFS:])
    shared = low_back(matmul(shared_act, shared_down))
    logits = low_back(matmul(normed2, router))
    route_rows = routes.reshape(TOKENS, TOP)
    chosen = jnp.take_along_axis(logits, route_rows, axis=1)
    gate_values = jax.nn.softmax(chosen, axis=-1)

    def block_step(running, pieces):
        block_rows, block_routes, block_gates = pieces
        matches, select = slot_select(block_routes)
        select = select.astype(jnp.float32).reshape(TOK_DEV * TOP, EXPERTS * CAP)
        spread = lax.optimization_barrier(jnp.sum(select.reshape(TOK_DEV, TOP, EXPERTS * CAP), axis=1))
        arrived = low_back(matmul(spread.T, block_rows)).reshape(EXPERTS, CAP, D)
        expert_both = low_back(jnp.einsum('ecd,edf->ecf', arrived, expert_gate_up, precision=highest))
        expert_act = low(jax.nn.silu(expert_both[..., :FFE]) * expert_both[..., FFE:])
        returned = both_round(jnp.einsum('ecf,efd->ecd', expert_act, expert_down, precision=highest))
        picked = matmul(select, returned.reshape(EXPERTS * CAP, D)).reshape(TOK_DEV, TOP, D)
        return (running, lax.optimization_barrier(jnp.sum(block_gates[:, :, None] * picked, axis=1)))
    running, routed = lax.scan(jax.checkpoint(block_step), jnp.zeros((), jnp.float32), (normed2.reshape(-1, TOK_DEV, D), route_rows.reshape(-1, TOK_DEV, TOP), gate_values.reshape(-1, TOK_DEV, TOP)))
    output = hidden + shared + routed.reshape(TOKENS, D)
    return output.reshape(SEQS, LEN, D)

def reference(tokens, norm1_gain, q_weight, kv_down, latent_gain, kv_up, o_weight, norm2_gain, router, shared_gate_up, shared_down, expert_gate_up, expert_down, teacher, routes, prefix, token_count):
    params = tuple((argument.astype(jnp.float32) for argument in (tokens, norm1_gain, q_weight, kv_down, latent_gain, kv_up, o_weight, norm2_gain, router, shared_gate_up, shared_down, expert_gate_up, expert_down)))
    output, pullback = jax.vjp(lambda *weights: forward(weights, routes, prefix), *params)
    misfit = output - teacher.astype(jnp.float32)
    gradients = pullback(misfit)
    loss_value = jnp.sum(misfit * misfit) / (token_count.astype(jnp.float32) * D)
    return (output.astype(jnp.bfloat16), loss_value, gradients[0], gradients[1], gradients[2], gradients[3], gradients[4], gradients[5], gradients[6], gradients[7], gradients[8], gradients[9], gradients[10], gradients[11], gradients[12])
```

```python
import math

import jax
import jax.numpy as jnp
from jax import lax
from jax.sharding import Mesh
from jax.sharding import PartitionSpec as P

NH = 16
DN = 128
DR = 64
DV = 128
KVR = 512
FFE = 1408
FFS = 2816
TOP = 6
PLANE = 4

BF = jnp.bfloat16
F32 = jnp.float32

epsilon = 1e-06


def rms_norm(values, gain_row):
    return (
        values * lax.rsqrt(jnp.mean(values * values, axis=-1, keepdims=True) + epsilon) * gain_row
    )


def norm_back(values, gain_row, incoming):
    factor = lax.rsqrt(jnp.mean(values * values, axis=-1, keepdims=True) + epsilon)
    scaled = incoming * gain_row
    grad_values = factor * scaled - values * (factor * factor * factor) * jnp.mean(
        scaled * values, axis=-1, keepdims=True
    )
    grad_gain = jnp.sum(incoming * values * factor, axis=0)
    return (grad_values, grad_gain)


def tables(position, rot_width):
    half_width = rot_width // 2
    frequency = 10000.0 ** (-2.0 * jnp.arange(half_width, dtype=F32) / rot_width)
    angles = position.astype(F32)[:, None] * frequency[None, :]
    return (jnp.cos(angles), jnp.sin(angles))


def rotate(values, cosine, sine_table):
    half_width = values.shape[-1] // 2
    first_half = values[..., :half_width]
    second = values[..., half_width:]
    return jnp.concatenate(
        [first_half * cosine - second * sine_table, first_half * sine_table + second * cosine],
        axis=-1,
    )


def unrotate(values, cosine, sine_table):
    half_width = values.shape[-1] // 2
    first_half = values[..., :half_width]
    second = values[..., half_width:]
    return jnp.concatenate(
        [first_half * cosine + second * sine_table, second * cosine - first_half * sine_table],
        axis=-1,
    )


def dot_plain(left_side, right_side):
    return jnp.dot(left_side, right_side, preferred_element_type=F32)


def dot_last(left_side, right_side):
    return lax.dot_general(
        left_side, right_side, (((1,), (1,)), ((), ())), preferred_element_type=F32
    )


def dot_first(left_side, right_side):
    return lax.dot_general(
        left_side, right_side, (((0,), (0,)), ((), ())), preferred_element_type=F32
    )


def swiglu(gate_up, half_width):
    return (jax.nn.silu(gate_up[:, :half_width]) * gate_up[:, half_width:]).astype(BF)


def swiglu_back(gate_up, incoming, half_width):
    first_half = gate_up[:, :half_width]
    second = gate_up[:, half_width:]
    sigmoid = jax.nn.sigmoid(first_half)
    return jnp.concatenate(
        [
            incoming * second * sigmoid * (1.0 + first_half * (1.0 - sigmoid)),
            incoming * first_half * sigmoid,
        ],
        axis=1,
    ).astype(BF)


def hop(values, axis, distance):
    size = lax.axis_size(axis)
    return lax.ppermute(values, axis, [(i, i ^ distance) for i in range(size)])


def gather_plane(values):
    along = hop(values, "r", 1)
    across = hop(values, "r", 2)
    if values.shape[0] % 2 == 0:
        half = values.shape[0] // 2
        far = jnp.concatenate([hop(along[:half], "r", 2), hop(across[half:], "r", 1)], axis=0)
    else:
        half = values.shape[1] // 2
        far = jnp.concatenate([hop(along[:, :half], "r", 2), hop(across[:, half:], "r", 1)], axis=1)
    return jnp.stack([values, along, across, far], axis=1)


def scatter_plane(parts):
    near, along, across, far = (parts[:, j] for j in range(4))
    far = far.astype(BF)
    if parts.shape[0] % 2 == 0:
        half = parts.shape[0] // 2
        first = hop(far[:half], "r", 1).astype(F32)
        second = hop(far[half:], "r", 2).astype(F32)
        across = jnp.concatenate([across[:half] + first, across[half:]], axis=0)
        along = jnp.concatenate([along[:half], along[half:] + second], axis=0)
    else:
        half = parts.shape[2] // 2
        first = hop(far[:, :half], "r", 1).astype(F32)
        second = hop(far[:, half:], "r", 2).astype(F32)
        across = jnp.concatenate([across[:, :half] + first, across[:, half:]], axis=1)
        along = jnp.concatenate([along[:, :half], along[:, half:] + second], axis=1)
    return (
        near
        + hop(along.astype(BF), "r", 1).astype(F32)
        + hop(across.astype(BF), "r", 2).astype(F32)
    )


def gather_group(rows):
    plane = gather_plane(rows[None])[0]
    return jnp.stack([plane, hop(plane, "fsdp", 1)], axis=1)


def scatter_group(parts):
    other = hop(parts[:, 1].astype(BF), "fsdp", 1).astype(F32)
    return scatter_plane((parts[:, 0] + other)[None])[0]


def sum_columns(parts):
    moved = lax.all_to_all(parts.astype(BF), "z", split_axis=0, concat_axis=0, tiled=True)
    return jnp.sum(moved.astype(F32), axis=0)


def gather_columns(values):
    spread = jnp.broadcast_to(values[None], (lax.axis_size("z"),) + values.shape)
    return lax.all_to_all(spread, "z", split_axis=0, concat_axis=0, tiled=True)


def gather_rows(values):
    rows, width = values.shape
    column = gather_columns(values)
    spread = jnp.broadcast_to(column[None], (PLANE,) + column.shape)
    plane = lax.all_to_all(spread, "r", split_axis=0, concat_axis=0, tiled=True)
    whole = jnp.swapaxes(plane, 0, 1).reshape(-1, width)
    return lax.all_gather(whole, "fsdp", axis=0, tiled=True)


def scatter_rows(parts):
    cores = lax.axis_size("fsdp")
    depth = lax.axis_size("z")
    rows = parts.shape[0] // (cores * depth * PLANE)
    width = parts.shape[1]
    core = lax.axis_index("fsdp")
    halves = parts.reshape(cores, -1, width)
    kept = lax.dynamic_index_in_dim(halves, core, 0, keepdims=False)
    given = lax.dynamic_index_in_dim(halves, 1 - core, 0, keepdims=False)
    kept = kept + hop(given.astype(BF), "fsdp", 1).astype(F32)
    kept = kept.reshape(depth, PLANE, rows, width).swapaxes(0, 1)
    moved = lax.all_to_all(kept.astype(BF), "r", split_axis=0, concat_axis=0, tiled=True)
    return sum_columns(jnp.sum(moved.astype(F32), axis=0))


def on_device(
    tokens,
    norm1_gain,
    q_weight,
    kv_down,
    latent_gain,
    kv_up,
    o_weight,
    norm2_gain,
    router,
    shared_gate_up,
    shared_down,
    expert_gate_up,
    expert_down,
    teacher,
    routes,
    prefix,
    token_count,
):
    cores = lax.axis_size("fsdp")
    depth = lax.axis_size("z")
    experts = depth * PLANE
    group = cores * PLANE
    heads = NH // group
    core = lax.axis_index("fsdp")
    plane_index = lax.axis_index("z")
    spot = lax.axis_index("r")
    own_expert = plane_index * PLANE + spot
    token_rows = tokens.shape[1]
    model_width = tokens.shape[2]
    seq_length = token_rows * cores
    capacity = max(2, token_rows * TOP * 5 // (experts * 3))
    weight_rows = q_weight.shape[0]
    latent_rows = kv_up.shape[0]
    wide_q = heads * (DN + DR)
    wide_kv = heads * (DN + DV)
    scaling = (DN + DR) ** (-0.5)

    fold = weight_rows // latent_rows
    up_fold = wide_kv // fold
    up_packed = kv_up.reshape(latent_rows, group, fold, up_fold)
    up_packed = up_packed.swapaxes(1, 2).reshape(weight_rows, group, up_fold)
    packed = jnp.concatenate([q_weight.reshape(weight_rows, group, wide_q), up_packed], axis=2)
    packed = lax.all_to_all(
        packed.swapaxes(0, 1), ("fsdp", "r"), split_axis=0, concat_axis=0, tiled=True
    )
    packed = gather_columns(packed.reshape(cores, PLANE * weight_rows, wide_q + up_fold))
    packed = packed.swapaxes(0, 1).reshape(model_width, wide_q + up_fold)
    query_weight = packed[:, :wide_q]
    up_weight = packed[:, wide_q:].reshape(KVR, fold * up_fold)

    small = jnp.concatenate(
        [
            kv_down,
            router,
            norm1_gain[:, None],
            norm2_gain[:, None],
            jnp.pad(latent_gain, (0, weight_rows - latent_rows))[:, None],
        ],
        axis=1,
    )
    small_width = -(-small.shape[1] // 128) * 128
    small = gather_rows(jnp.pad(small, ((0, 0), (0, small_width - small.shape[1]))))
    down_weight = small[:, : KVR + DR]
    router_weight = small[:, KVR + DR : KVR + DR + experts]
    gains = small[:, KVR + DR + experts : KVR + DR + experts + 3].astype(F32).T
    gain_one_f = gains[0]
    gain_two_f = gains[1]
    latent_gain_f = gains[2].reshape(-1, weight_rows)[:, :latent_rows].reshape(KVR)

    sub = depth // PLANE
    shard_moves = [
        (z * PLANE + r, ((z % sub) * PLANE + r) * PLANE + z // sub)
        for z in range(depth)
        for r in range(PLANE)
    ]
    output_weight = gather_columns(lax.ppermute(o_weight, ("z", "r"), shard_moves)).reshape(
        heads * DV, model_width
    )

    expert_both_weight = lax.all_gather(expert_gate_up, "fsdp", axis=1, tiled=True)[0]
    expert_down_weight = lax.all_gather(expert_down, "fsdp", axis=2, tiled=True)[0]
    unit = shared_down.shape[0]
    shared_units = cores * unit
    shared_both = shared_gate_up.reshape(weight_rows, 2 * cores, experts, unit).transpose(
        2, 0, 1, 3
    )
    shared_both = lax.all_to_all(
        shared_both.reshape(experts, weight_rows, 2 * shared_units),
        ("z", "r"),
        split_axis=0,
        concat_axis=0,
        tiled=True,
    ).reshape(experts * weight_rows, 2 * shared_units)
    shared_both_weight = lax.all_gather(shared_both, "fsdp", axis=0, tiled=True)
    shared_down_weight = lax.all_gather(shared_down, "fsdp", axis=0, tiled=True)

    own_mask = jnp.any(
        routes[0][:, :, None] == jnp.arange(experts, dtype=jnp.int32)[None, None, :], axis=1
    )
    named = jnp.concatenate(
        [
            own_mask.T.astype(F32),
            jnp.broadcast_to(prefix.astype(F32)[None, :], (experts, 128)),
        ],
        axis=1,
    )
    named = lax.all_to_all(named, ("z", "r"), split_axis=0, concat_axis=0, tiled=True)
    order = jnp.array(
        [[z * PLANE + r for r in range(PLANE)] for z in range(depth)], dtype=jnp.int32
    )
    order = (order ^ own_expert).reshape(-1)
    named = jnp.take(named, order, axis=0)
    prefixes = named[:PLANE, token_rows]
    taken = named[:, :token_rows]
    rank = jnp.cumsum(taken, axis=1) - taken
    select = taken[:, None, :] * (
        rank[:, None, :] == jnp.arange(capacity, dtype=F32)[None, :, None]
    ).astype(F32)
    select_low = select.astype(BF)

    half = jnp.arange(token_rows, dtype=jnp.int32)
    position = jnp.concatenate([core * token_rows + half, (1 - core) * token_rows + half])
    cosine, sine_table = tables(position, DR)
    every = PLANE * seq_length
    rows = gather_group(tokens[0]).reshape(every, model_width)
    normed = rms_norm(rows.astype(F32), gain_one_f).astype(BF)
    latent = dot_plain(normed, down_weight)
    compressed = rms_norm(latent[:, :KVR], latent_gain_f).astype(BF)
    key_rope = rotate(
        latent[:, KVR:].reshape(PLANE, seq_length, DR), cosine, sine_table
    ).astype(BF)
    query_raw = dot_plain(normed, query_weight).reshape(PLANE, seq_length, heads, DN + DR)
    queries = jnp.concatenate(
        [
            query_raw[..., :DN],
            rotate(query_raw[..., DN:], cosine[:, None, :], sine_table[:, None, :]),
        ],
        axis=-1,
    ).astype(BF)
    keyval = dot_plain(compressed, up_weight).astype(BF)
    keyval = keyval.reshape(PLANE, seq_length, heads, DN + DV)
    key_part = keyval[..., :DN]
    value_part = keyval[..., DN:]
    visible = (position[None, :] <= position[:, None])[None] | (
        position[None, None, :].astype(F32) < prefixes[:, None, None]
    )
    scores = (
        jnp.einsum("sqhd,skhd->shqk", queries[..., :DN], key_part, preferred_element_type=F32)
        + jnp.einsum("sqhr,skr->shqk", queries[..., DN:], key_rope, preferred_element_type=F32)
    ) * scaling
    scores = jnp.where(visible[:, None], scores, -1e30)
    peak_score = jnp.max(scores, axis=-1, keepdims=True)
    weights = jnp.exp(scores - peak_score)
    attention = weights / jnp.sum(weights, axis=-1, keepdims=True)
    attention_low = attention.astype(BF)
    context = (
        jnp.einsum("shqk,skhv->sqhv", attention_low, value_part, preferred_element_type=F32)
        .reshape(every, heads * DV)
        .astype(BF)
    )
    projected = dot_plain(context, output_weight).reshape(PLANE, cores, token_rows, model_width)
    own_rows = tokens[0].astype(F32)
    hidden = own_rows + scatter_group(projected)
    normed2 = rms_norm(hidden, gain_two_f).astype(BF)

    def gates_of(some_rows, mask):
        logits = jnp.where(mask, dot_plain(some_rows, router_weight), -1e30)
        odds = jnp.where(mask, jnp.exp(logits - jnp.max(logits, axis=-1, keepdims=True)), 0.0)
        return odds / jnp.sum(odds, axis=-1, keepdims=True)

    own_gates = gates_of(normed2, own_mask)
    chunk = depth // 2
    chunks = [range(start, start + chunk) for start in range(0, depth, chunk)]

    def gather_chunk(values, planes):
        stacked = jnp.stack([hop(values, "z", k) if k else values for k in planes], axis=0)
        return gather_plane(stacked).reshape(-1, model_width)

    def own_gate_column(gates):
        moved = lax.all_to_all(gates.T, ("z", "r"), split_axis=0, concat_axis=0, tiled=True)
        return jnp.take(moved, order, axis=0)

    gate_slots = jnp.sum(select * own_gate_column(own_gates)[:, None, :], axis=2)

    arrived = [gather_chunk(normed2, planes) for planes in chunks]
    blocks = chunk * PLANE
    kept = []
    returned = []
    for number, planes in enumerate(chunks):
        some = arrived[number]
        chosen = select_low[number * blocks : (number + 1) * blocks]
        gate_slot = gate_slots[number * blocks : (number + 1) * blocks].reshape(-1, 1)
        expert_in = (
            jnp.einsum(
                "bst,btd->bsd",
                chosen,
                some.reshape(blocks, token_rows, model_width),
                preferred_element_type=F32,
            )
            .astype(BF)
            .reshape(blocks * capacity, model_width)
        )
        expert_gu = dot_plain(expert_in, expert_both_weight)
        expert_act = swiglu(expert_gu, FFE)
        expert_out = dot_plain(expert_act, expert_down_weight).astype(BF)
        gated = (gate_slot * expert_out.astype(F32)).astype(BF)
        shared_gu = dot_plain(some, shared_both_weight)
        shared_act = swiglu(shared_gu, shared_units)
        total = jnp.einsum(
            "bst,bsd->btd",
            chosen,
            gated.reshape(blocks, capacity, model_width),
            preferred_element_type=F32,
        ) + dot_plain(shared_act, shared_down_weight).reshape(blocks, token_rows, model_width)
        kept.append((some, chosen, gate_slot, expert_in, expert_gu, expert_act, expert_out, shared_gu, shared_act))
        summed = scatter_plane(total.reshape(chunk, PLANE, token_rows, model_width))
        for place, k in enumerate(planes):
            returned.append(hop(summed[place].astype(BF), "z", k).astype(F32) if k else summed[place])
    output = hidden + sum(returned)
    misfit = output - teacher[0].astype(F32)
    misfit_low = misfit.astype(BF)

    grad_arrived = [gather_chunk(misfit_low, planes) for planes in chunks]
    grad_returned = []
    pieces = []
    for number, planes in enumerate(chunks):
        some, chosen, gate_slot, expert_in, expert_gu, expert_act, expert_out, shared_gu, shared_act = kept[number]
        incoming = grad_arrived[number]
        slots = (
            jnp.einsum(
                "bst,btd->bsd",
                chosen,
                incoming.reshape(blocks, token_rows, model_width),
                preferred_element_type=F32,
            )
            .reshape(blocks * capacity, model_width)
        )
        grad_gate = jnp.sum(slots * expert_out.astype(F32), axis=1)
        grad_slots = (gate_slot * slots).astype(BF)
        grad_gu = swiglu_back(expert_gu, dot_last(grad_slots, expert_down_weight), FFE)
        grad_expert_in = dot_last(grad_gu, expert_both_weight).astype(BF)
        grad_shared_gu = swiglu_back(
            shared_gu, dot_last(incoming, shared_down_weight), shared_units
        )
        total = jnp.einsum(
            "bst,bsd->btd",
            chosen,
            grad_expert_in.reshape(blocks, capacity, model_width),
            preferred_element_type=F32,
        ) + dot_last(grad_shared_gu, shared_both_weight).reshape(blocks, token_rows, model_width)
        summed = scatter_plane(total.reshape(chunk, PLANE, token_rows, model_width))
        for place, k in enumerate(planes):
            grad_returned.append(hop(summed[place].astype(BF), "z", k).astype(F32) if k else summed[place])
        pieces.append((some, incoming, expert_in, expert_act, shared_act, grad_slots, grad_gu, grad_shared_gu, grad_gate))
    some, incoming, expert_in, expert_act, shared_act, grad_slots, grad_gu, grad_shared_gu, grad_gate = (
        jnp.concatenate(values, axis=0) for values in zip(*pieces)
    )
    grad_expert_down = lax.psum_scatter(
        dot_first(expert_act, grad_slots)[None], "fsdp", scatter_dimension=2, tiled=True
    )
    grad_expert_gate_up = lax.psum_scatter(
        dot_first(expert_in, grad_gu)[None], "fsdp", scatter_dimension=1, tiled=True
    )
    grad_shared_down = lax.psum_scatter(
        dot_first(shared_act, incoming), "fsdp", scatter_dimension=0, tiled=True
    )
    grad_shared_both = lax.psum_scatter(
        dot_first(some, grad_shared_gu), "fsdp", scatter_dimension=0, tiled=True
    )
    grad_shared_gate_up = (
        lax.all_to_all(
            grad_shared_both.astype(BF).reshape(experts, weight_rows, 2 * shared_units),
            ("z", "r"),
            split_axis=0,
            concat_axis=0,
            tiled=True,
        )
        .reshape(experts, weight_rows, 2 * cores, unit)
        .transpose(1, 2, 0, 3)
        .reshape(weight_rows, 2 * FFS)
        .astype(F32)
    )

    grad_gate = jnp.sum(select * grad_gate.reshape(experts, capacity)[:, :, None], axis=1)
    squares = jnp.broadcast_to(jnp.sum(misfit * misfit)[None, None], (experts, 128))
    notes = jnp.concatenate([jnp.take(grad_gate, order, axis=0), squares], axis=1)
    notes = lax.all_to_all(notes, ("z", "r"), split_axis=0, concat_axis=0, tiled=True)
    grad_gates = notes[:, :token_rows].T
    all_squares = jnp.sum(notes[:, token_rows])[None]
    all_squares = all_squares + hop(jnp.broadcast_to(all_squares, (8, 128)), "fsdp", 1)[0, :1]
    loss_value = all_squares / (token_count.astype(F32) * model_width)
    grad_logits = (
        own_gates * (grad_gates - jnp.sum(own_gates * grad_gates, axis=1, keepdims=True))
    ).astype(BF)
    grad_normed2 = sum(grad_returned) + dot_last(grad_logits, router_weight)
    grad_hidden_norm, grad_gain_two = norm_back(hidden, gain_two_f, grad_normed2)
    grad_hidden = misfit + grad_hidden_norm
    grad_attn = gather_group(grad_hidden.astype(BF)).reshape(every, model_width)

    grad_context = dot_last(grad_attn, output_weight).astype(BF)
    grad_context = grad_context.reshape(PLANE, seq_length, heads, DV)
    grad_output_weight = dot_first(context, grad_attn).reshape(depth, weight_rows, model_width)
    grad_output_weight = lax.ppermute(
        sum_columns(grad_output_weight), ("z", "r"), [(b, a) for a, b in shard_moves]
    )
    grad_attention = jnp.einsum(
        "sqhv,skhv->shqk", grad_context, value_part, preferred_element_type=F32
    )
    grad_scores = (
        attention * (grad_attention - jnp.sum(attention * grad_attention, axis=-1, keepdims=True))
    ).astype(BF)
    grad_query_nope = (
        jnp.einsum("shqk,skhd->sqhd", grad_scores, key_part, preferred_element_type=F32) * scaling
    )
    grad_query_rope = (
        jnp.einsum("shqk,skr->sqhr", grad_scores, key_rope, preferred_element_type=F32) * scaling
    )
    grad_key_nope = (
        jnp.einsum("shqk,sqhd->skhd", grad_scores, queries[..., :DN], preferred_element_type=F32)
        * scaling
    )
    grad_values = jnp.einsum(
        "shqk,sqhv->skhv", attention_low, grad_context, preferred_element_type=F32
    )
    grad_key_rope = (
        jnp.einsum("shqk,sqhr->skr", grad_scores, queries[..., DN:], preferred_element_type=F32)
        * scaling
    )
    grad_keyval = (
        jnp.concatenate([grad_key_nope, grad_values], axis=-1).astype(BF).reshape(every, wide_kv)
    )
    grad_query = (
        jnp.concatenate(
            [
                grad_query_nope,
                unrotate(grad_query_rope, cosine[:, None, :], sine_table[:, None, :]),
            ],
            axis=-1,
        )
        .astype(BF)
        .reshape(every, wide_q)
    )
    partial = jnp.concatenate(
        [
            dot_last(grad_query, query_weight),
            dot_last(grad_keyval, up_weight),
            grad_key_rope.reshape(every, DR),
        ],
        axis=1,
    )
    partial = scatter_group(partial.reshape(PLANE, cores, token_rows, -1))
    grad_up = dot_first(compressed, grad_keyval).reshape(model_width, up_fold)
    grad_packed = jnp.concatenate([dot_first(normed, grad_query), grad_up], axis=1)
    grad_packed = grad_packed.reshape(cores, depth, PLANE * weight_rows, wide_q + up_fold)
    grad_packed = sum_columns(grad_packed.swapaxes(0, 1)).astype(BF)
    grad_packed = lax.all_to_all(
        grad_packed.reshape(group, weight_rows, wide_q + up_fold),
        ("fsdp", "r"),
        split_axis=0,
        concat_axis=0,
        tiled=True,
    ).swapaxes(0, 1)
    grad_q_weight = grad_packed[:, :, :wide_q].reshape(weight_rows, -1).astype(F32)
    grad_kv_up = (
        grad_packed[:, :, wide_q:]
        .reshape(latent_rows, fold, group, up_fold)
        .swapaxes(1, 2)
        .reshape(latent_rows, -1)
        .astype(F32)
    )
    own_latent = latent[:token_rows]
    grad_latent_norm, grad_latent_gain = norm_back(
        own_latent[:, :KVR], latent_gain_f, partial[:, model_width : model_width + KVR]
    )
    grad_latent = jnp.concatenate(
        [
            grad_latent_norm,
            unrotate(
                partial[:, model_width + KVR :], cosine[:token_rows], sine_table[:token_rows]
            ),
        ],
        axis=1,
    ).astype(BF)
    own_normed = normed[:token_rows]
    grad_normed = partial[:, :model_width] + dot_last(grad_latent, down_weight)
    grad_flat_norm, grad_gain_one = norm_back(own_rows, gain_one_f, grad_normed)
    grad_tokens = grad_hidden + grad_flat_norm
    grad_latent_gain = jnp.pad(
        grad_latent_gain.reshape(-1, latent_rows), ((0, 0), (0, weight_rows - latent_rows))
    ).reshape(model_width)
    grad_small = jnp.concatenate(
        [
            dot_first(own_normed, grad_latent),
            dot_first(normed2, grad_logits),
            jnp.stack([grad_gain_one, grad_gain_two, grad_latent_gain], axis=1),
        ],
        axis=1,
    )
    grad_small = scatter_rows(
        jnp.pad(grad_small, ((0, 0), (0, small_width - grad_small.shape[1])))
    )
    base = KVR + DR + experts
    return (
        output.astype(BF)[None],
        loss_value,
        grad_tokens[None],
        grad_small[:, base],
        grad_q_weight,
        grad_small[:, : KVR + DR],
        grad_small[:latent_rows, base + 2],
        grad_kv_up,
        grad_output_weight,
        grad_small[:, base + 1],
        grad_small[:, KVR + DR : base],
        grad_shared_gate_up,
        grad_shared_down,
        grad_expert_gate_up,
        grad_expert_down,
    )


def solution(mesh):
    cores = mesh.shape["fsdp"]
    experts = mesh.shape["expert"]
    grid = Mesh(mesh.devices.reshape(cores, experts // PLANE, PLANE), ("fsdp", "z", "r"))
    expert = ("z", "r")
    every = ("fsdp", "z", "r")
    return jax.shard_map(
        on_device,
        mesh=grid,
        in_specs=(
            P(expert, "fsdp", None),
            P(every),
            P(every, None),
            P(every, None),
            P(every),
            P(every, None),
            P(every, None),
            P(every),
            P(every, None),
            P(every, None),
            P(every, None),
            P(expert, "fsdp", None),
            P(expert, None, "fsdp"),
            P(expert, "fsdp", None),
            P(expert, "fsdp", None),
            P(expert),
            P(),
        ),
        out_specs=(
            P(expert, "fsdp", None),
            P(),
            P(expert, "fsdp", None),
            P(every),
            P(every, None),
            P(every, None),
            P(every),
            P(every, None),
            P(every, None),
            P(every),
            P(every, None),
            P(every, None),
            P(every, None),
            P(expert, "fsdp", None),
            P(expert, None, "fsdp"),
        ),
        check_vma=False,
    )
```

```python
import math

import jax
import jax.numpy as jnp
import numpy as np
from jax import lax
from jax.experimental import pallas as pl
from jax.experimental.layout import Layout, with_layout_constraint
from jax.experimental.pallas import tpu as pltpu
from jax.sharding import Mesh
from jax.sharding import PartitionSpec as P

NH = 16
DN = 128
DR = 64
DV = 128
KVR = 512
FFE = 1408
FFS = 2816
TOP = 6
PLANE = 4

BF = jnp.bfloat16
F32 = jnp.float32

epsilon = 1e-06


def rms_norm(values, gain_row):
    return (
        values * lax.rsqrt(jnp.mean(values * values, axis=-1, keepdims=True) + epsilon) * gain_row
    )


def norm_back(values, gain_row, incoming):
    factor = lax.rsqrt(jnp.mean(values * values, axis=-1, keepdims=True) + epsilon)
    scaled = incoming * gain_row
    grad_values = factor * scaled - values * (factor * factor * factor) * jnp.mean(
        scaled * values, axis=-1, keepdims=True
    )
    grad_gain = jnp.sum(incoming * values * factor, axis=0)
    return (grad_values, grad_gain)


def tables(position, rot_width):
    half_width = rot_width // 2
    frequency = 10000.0 ** (-2.0 * jnp.arange(half_width, dtype=F32) / rot_width)
    angles = position.astype(F32)[:, None] * frequency[None, :]
    return (jnp.cos(angles), jnp.sin(angles))


def unrotate(values, cosine, sine_table):
    half_width = values.shape[-1] // 2
    first_half = values[..., :half_width]
    second = values[..., half_width:]
    return jnp.concatenate(
        [first_half * cosine + second * sine_table, second * cosine - first_half * sine_table],
        axis=-1,
    )


def dot_plain(left_side, right_side):
    return jnp.dot(left_side, right_side, preferred_element_type=F32)


def dot_last(left_side, right_side):
    return lax.dot_general(
        left_side, right_side, (((1,), (1,)), ((), ())), preferred_element_type=F32
    )


def dot_first(left_side, right_side):
    return lax.dot_general(
        left_side, right_side, (((0,), (0,)), ((), ())), preferred_element_type=F32
    )


def straight(values):
    return with_layout_constraint(values, Layout(tuple(range(values.ndim))))


def after(values, *others):
    return lax.optimization_barrier((values,) + others)[0]


def hop(values, axis, distance):
    size = lax.axis_size(axis)
    moves = [(i, i ^ distance) for i in range(size)]
    return straight(lax.ppermute(straight(values), axis, moves))


def gather_plane(values):
    return [values] + [hop(values, "r", j) for j in range(1, PLANE)]


def scatter_plane(parts):
    moved = [hop(parts[j].astype(BF), "r", j) for j in range(1, PLANE)]
    return parts[0].astype(F32) + sum(part.astype(F32) for part in moved)


def gather_group(rows):
    plane = jnp.stack(gather_plane(rows), axis=0)
    return plane, hop(plane, "fsdp", 1)


def scatter_group(own, given):
    return scatter_plane(list(own.astype(F32) + hop(given, "fsdp", 1).astype(F32)))


def column_order(axis):
    return jnp.arange(lax.axis_size(axis), dtype=jnp.int32) ^ lax.axis_index(axis)


def sum_columns(parts):
    parts = jnp.take(parts.astype(BF), column_order("z"), axis=0, mode="clip")
    moved = [hop(parts[k], "z", k) for k in range(1, lax.axis_size("z"))]
    return parts[0].astype(F32) + sum(part.astype(F32) for part in moved)


def gather_columns(values):
    spread = jnp.broadcast_to(values[None], (lax.axis_size("z"),) + values.shape)
    return lax.all_to_all(spread, "z", split_axis=0, concat_axis=0, tiled=True)


def gather_columns_apart(values):
    column = [values] + [hop(values, "z", k) for k in range(1, lax.axis_size("z"))]
    return jnp.take(jnp.stack(column, axis=0), column_order("z"), axis=0, mode="clip")


def all_order():
    return (column_order("z")[:, None] * PLANE + column_order("r")[None, :]).reshape(-1)


def swap_plane(parts):
    shape = parts.shape[1:]
    parts = jnp.take(parts, all_order(), axis=0, mode="clip")
    parts = parts.reshape((lax.axis_size("z"), PLANE) + shape)
    plane = [parts[:, 0]] + [hop(parts[:, j], "r", j) for j in range(1, PLANE)]
    return jnp.stack(plane, axis=1)


def swap_column(plane):
    depth = lax.axis_size("z")
    column = [plane[0]] + [hop(plane[k], "z", k) for k in range(1, depth)]
    column = jnp.stack(column, axis=0).reshape((depth * PLANE,) + plane.shape[2:])
    return jnp.take(column, all_order(), axis=0, mode="clip")


ROOM = 56 * 1024 * 1024


def whole(array):
    return pl.BlockSpec(array.shape, lambda *_: (0,) * array.ndim)


def sums_of_products(lefts, rights, tall, wide=None):
    pairs = len(lefts)
    depth, height = lefts[0].shape
    width = rights[0].shape[1]
    wide = width if wide is None else wide

    def body(*refs):
        out_ref, left_ref, right_ref = refs[-3:]

        @pl.when(pl.program_id(1) == 0)
        def _():
            for i in range(pairs):
                right_ref[i * depth : (i + 1) * depth, :] = refs[pairs + i][...]

        for i in range(pairs):
            left_ref[i * depth : (i + 1) * depth, :] = refs[i][...]
        out_ref[...] = dot_first(left_ref[...], right_ref[...])

    return pl.pallas_call(
        body,
        grid=(width // wide, height // tall),
        in_specs=[pl.BlockSpec((depth, tall), lambda j, i: (0, i))] * pairs
        + [pl.BlockSpec((depth, wide), lambda j, i: (0, j))] * pairs,
        out_specs=pl.BlockSpec((tall, wide), lambda j, i: (i, j)),
        out_shape=jax.ShapeDtypeStruct((height, width), F32),
        scratch_shapes=[pltpu.VMEM((pairs * depth, tall), BF), pltpu.VMEM((pairs * depth, wide), BF)],
        compiler_params=pltpu.CompilerParams(vmem_limit_bytes=ROOM),
        cost_estimate=pl.CostEstimate(
            flops=2 * pairs * depth * height * width,
            bytes_accessed=2 * pairs * depth * (height + width) + 4 * height * width,
            transcendentals=0,
        ),
    )(*lefts, *rights)


def swiglu_parts(gate, up, incoming):
    sigmoid = jax.nn.sigmoid(gate)
    return (
        (incoming * up * sigmoid * (1.0 + gate * (1.0 - sigmoid))).astype(BF),
        (incoming * gate * sigmoid).astype(BF),
    )


TILE = 128
STRIP = 256


def expert_forward(pieces, chosen, masks, mine, shared_router, both, down, shared_down):
    planes, rows, width = pieces[0].shape
    blocks, capacity = chosen.shape[:2]
    slots, flat_rows = blocks * capacity, blocks * rows
    hidden, units, experts = down.shape[0], shared_down.shape[0], mine.shape[1]
    tiles, strips = hidden // TILE, width // STRIP

    def body(
        piece_0, piece_1, piece_2, piece_3, chosen_ref, masks_ref, mine_ref, router_ref, gate_ref,
        up_ref, down_ref, shared_down_ref,
        flat_ref, in_ref, gu_ref, act_ref, picked_ref, gates_ref, shared_gu_ref, shared_act_ref,
        total_0, total_1, total_2, total_3,
    ):
        step = pl.program_id(0)

        @pl.when(step == 0)
        def _():
            for j, piece in enumerate((piece_0, piece_1, piece_2, piece_3)):
                for k in range(planes):
                    start = (j * planes + k) * rows
                    flat_ref[start : start + rows, :] = piece[k]
            for block in range(blocks):
                in_ref[block * capacity : (block + 1) * capacity, :] = dot_plain(
                    chosen_ref[block], flat_ref[block * rows : (block + 1) * rows, :]
                ).astype(BF)
            joined = dot_plain(flat_ref[...], router_ref[...])
            shared_gu_ref[...] = joined[:, : 2 * units]
            gate, up = joined[:, :units], joined[:, units : 2 * units]
            shared_act_ref[...] = (gate * jax.nn.sigmoid(gate) * up).astype(BF)
            mask = masks_ref[...] > 0.0
            logits = jnp.where(mask, joined[:, 2 * units : 2 * units + experts], -1e30)
            odds = jnp.exp(logits - jnp.max(logits, axis=1, keepdims=True))
            odds = jnp.where(mask, odds, 0.0)
            own = jnp.sum(odds * mine_ref[...], axis=1, keepdims=True)
            own = own / jnp.sum(odds, axis=1, keepdims=True)
            gates_ref[...] = jnp.broadcast_to(own, gates_ref.shape)

        @pl.when(step < tiles)
        def _():
            weights = jnp.concatenate([gate_ref[...], up_ref[...]], axis=1)
            both_parts = dot_plain(in_ref[...], weights)
            gate, up = both_parts[:, :TILE], both_parts[:, TILE:]
            place = pl.multiple_of(step * TILE, TILE)
            gu_ref[:, pl.ds(place, TILE)] = gate
            gu_ref[:, pl.ds(pl.multiple_of(hidden + step * TILE, TILE), TILE)] = up
            act_ref[:, pl.ds(place, TILE)] = (gate * jax.nn.sigmoid(gate) * up).astype(BF)

        @pl.when(step >= tiles)
        def _():
            out = dot_plain(act_ref[...], down_ref[...]).astype(BF)
            shared = dot_plain(shared_act_ref[...], shared_down_ref[...])
            for j, total in enumerate((total_0, total_1, total_2, total_3)):
                for k in range(planes):
                    block = j * planes + k
                    span = slice(block * rows, (block + 1) * rows)
                    picked = dot_first(
                        chosen_ref[block], out[block * capacity : (block + 1) * capacity, :]
                    )
                    picked_ref[block] = picked.astype(BF)
                    total[k] = (gates_ref[span, 0:1] * picked + shared[span, :]).astype(total.dtype)

    def tile_of(step):
        return jnp.minimum(step, tiles - 1)

    def strip_of(step):
        return jnp.maximum(step - tiles, 0)

    def total_spec():
        return pl.BlockSpec((planes, rows, STRIP), lambda s: (0, 0, strip_of(s)))

    shapes = [
        ((flat_rows, width), BF), ((slots, width), BF), ((slots, 2 * hidden), F32),
        ((slots, hidden), BF), ((blocks, rows, width), BF), ((flat_rows, 128), F32),
        ((flat_rows, 2 * units), F32), ((flat_rows, units), BF),
    ] + [((planes, rows, width), F32 if j == 0 else BF) for j in range(PLANE)]
    shapes = [jax.ShapeDtypeStruct(*shape) for shape in shapes]
    return pl.pallas_call(
        body,
        grid=(tiles + strips,),
        in_specs=[whole(piece) for piece in pieces]
        + [whole(chosen), whole(masks), whole(mine), whole(shared_router)]
        + [
            pl.BlockSpec((width, TILE), lambda s: (0, tile_of(s))),
            pl.BlockSpec((width, TILE), lambda s: (0, tiles + tile_of(s))),
            pl.BlockSpec((hidden, STRIP), lambda s: (0, strip_of(s))),
            pl.BlockSpec((units, STRIP), lambda s: (0, strip_of(s))),
        ],
        out_specs=[whole(shape) for shape in shapes[:4]]
        + [pl.BlockSpec((blocks, rows, STRIP), lambda s: (0, 0, strip_of(s)))]
        + [whole(shape) for shape in shapes[5:8]]
        + [total_spec() for _ in range(PLANE)],
        out_shape=shapes,
        compiler_params=pltpu.CompilerParams(vmem_limit_bytes=ROOM),
        cost_estimate=pl.CostEstimate(
            flops=2 * width * (3 * slots * hidden + flat_rows * 4 * units),
            bytes_accessed=2 * width * (3 * hidden + 4 * units + 4 * flat_rows) + 12 * slots * hidden,
            transcendentals=slots * hidden,
        ),
    )(*pieces, chosen, masks, mine, shared_router, both, both, down, shared_down)


def expert_backward(pieces, chosen, gates, picked, gu, shared_gu, shared_router, both, down, shared_down):
    planes, rows, width = pieces[0].shape
    blocks, capacity = chosen.shape[:2]
    slots, flat_rows = blocks * capacity, blocks * rows
    hidden, units = down.shape[0], shared_down.shape[0]
    tiles, strips = hidden // TILE, width // STRIP

    def body(
        piece_0, piece_1, piece_2, piece_3, chosen_ref, gates_ref, picked_ref, gate_ref, up_ref,
        shared_gu_ref, shared_down_ref, down_ref, both_ref, router_ref,
        flat_ref, slots_ref, grad_gu_ref, grad_shared_ref, grad_gate_ref,
        total_0, total_1, total_2, total_3,
    ):
        step = pl.program_id(0)

        @pl.when(step == 0)
        def _():
            for j, piece in enumerate((piece_0, piece_1, piece_2, piece_3)):
                for k in range(planes):
                    block = j * planes + k
                    span = slice(block * rows, (block + 1) * rows)
                    flat_ref[span, :] = piece[k]
                    values = piece[k].astype(F32)
                    slots_ref[block * capacity : (block + 1) * capacity, :] = dot_plain(
                        chosen_ref[block], (gates_ref[span, 0:1] * values).astype(BF)
                    ).astype(BF)
                    own = jnp.sum(values * picked_ref[block].astype(F32), axis=1, keepdims=True)
                    grad_gate_ref[span, :] = jnp.broadcast_to(own, (rows, 128))
            grad_gate, grad_up = swiglu_parts(
                shared_gu_ref[:, :units],
                shared_gu_ref[:, units:],
                dot_last(flat_ref[...], shared_down_ref[...]),
            )
            grad_shared_ref[:, :units] = grad_gate
            grad_shared_ref[:, units:] = grad_up

        @pl.when(step < tiles)
        def _():
            grad_gate, grad_up = swiglu_parts(
                gate_ref[...], up_ref[...], dot_last(slots_ref[...], down_ref[...])
            )
            grad_gu_ref[:, pl.ds(pl.multiple_of(step * TILE, TILE), TILE)] = grad_gate
            grad_gu_ref[:, pl.ds(pl.multiple_of(hidden + step * TILE, TILE), TILE)] = grad_up

        @pl.when(step >= tiles)
        def _():
            grad_in = dot_last(grad_gu_ref[...], both_ref[...]).astype(BF)
            shared = dot_last(grad_shared_ref[...], router_ref[:, : 2 * units])
            for j, total in enumerate((total_0, total_1, total_2, total_3)):
                for k in range(planes):
                    block = j * planes + k
                    moved = dot_first(
                        chosen_ref[block], grad_in[block * capacity : (block + 1) * capacity, :]
                    )
                    total[k] = (moved + shared[block * rows : (block + 1) * rows, :]).astype(total.dtype)

    def tile_of(step):
        return jnp.minimum(step, tiles - 1)

    def strip_of(step):
        return jnp.maximum(step - tiles, 0)

    shapes = [
        ((flat_rows, width), BF), ((slots, width), BF), ((slots, 2 * hidden), BF),
        ((flat_rows, 2 * units), BF), ((flat_rows, 128), F32),
    ] + [((planes, rows, width), F32 if j == 0 else BF) for j in range(PLANE)]
    shapes = [jax.ShapeDtypeStruct(*shape) for shape in shapes]
    return pl.pallas_call(
        body,
        grid=(tiles + strips,),
        in_specs=[whole(piece) for piece in pieces]
        + [whole(chosen), whole(gates), whole(picked)]
        + [
            pl.BlockSpec((slots, TILE), lambda s: (0, tile_of(s))),
            pl.BlockSpec((slots, TILE), lambda s: (0, tiles + tile_of(s))),
            whole(shared_gu),
            whole(shared_down),
            pl.BlockSpec((TILE, width), lambda s: (tile_of(s), 0)),
            pl.BlockSpec((STRIP, 2 * hidden), lambda s: (strip_of(s), 0)),
            pl.BlockSpec((STRIP, shared_router.shape[1]), lambda s: (strip_of(s), 0)),
        ],
        out_specs=[whole(shape) for shape in shapes[:5]]
        + [pl.BlockSpec((planes, rows, STRIP), lambda s: (0, 0, strip_of(s))) for _ in range(PLANE)],
        out_shape=shapes,
        compiler_params=pltpu.CompilerParams(vmem_limit_bytes=ROOM),
        cost_estimate=pl.CostEstimate(
            flops=2 * width * (3 * slots * hidden + flat_rows * 4 * units),
            bytes_accessed=2 * width * (3 * hidden + 4 * units + 6 * flat_rows) + 12 * slots * hidden,
            transcendentals=slots * hidden,
        ),
    )(*pieces, chosen, gates, picked, gu, gu, shared_gu, shared_down, down, both, shared_router)


def turn(values, cosine, sine_table):
    lane = lax.broadcasted_iota(jnp.int32, values.shape, 1)
    wide = values.shape[1]
    swapped = jnp.where(
        lane % DR < DR // 2,
        pltpu.roll(values, wide - DR // 2, 1),
        pltpu.roll(values, DR // 2, 1),
    )
    return values * cosine + swapped * sine_table


def head_lanes(values, head):
    lane = lax.broadcasted_iota(jnp.int32, values.shape, 1)
    return jnp.where(lane // DR == head, values, jnp.zeros_like(values))


def attend(near, away, gain, down, latent_gain, query, up, heads, cosine, sine_table, place, places, early):
    sequences, rows, width = near.shape
    length = 2 * rows
    nope = heads * DN
    span = KVR + 2 * DR
    scaling = (DN + DR) ** (-0.5)

    def body(
        near_ref, away_ref, gain_ref, down_ref, latent_gain_ref, query_ref, up_ref, cos_ref, sin_ref, place_ref, places_ref, early_ref,
        normed_ref, latent_ref, compressed_ref, queries_ref, rope_ref, keyval_ref,
        attention_ref, context_ref,
    ):
        for side, ref in enumerate((near_ref, away_ref)):
            values = ref[0].astype(F32)
            normed_ref[side * rows : (side + 1) * rows, :] = rms_norm(values, gain_ref[...]).astype(BF)
        normed = normed_ref[...]
        latent = dot_plain(normed, down_ref[:, :span])
        latent_ref[...] = latent
        compressed = rms_norm(latent[:, :KVR], latent_gain_ref[...]).astype(BF)
        compressed_ref[...] = compressed
        key_rope = head_lanes(turn(latent[:, KVR:], cos_ref[...], sin_ref[...]), 0)
        key_rope = (key_rope + pltpu.roll(key_rope, DR, 1)).astype(BF)
        rope_ref[...] = key_rope
        query_raw = dot_plain(normed, query_ref[...])
        queries_ref[:, :nope] = query_raw[:, :nope].astype(BF)
        query_rope = turn(query_raw[:, nope:], cos_ref[...], sin_ref[...]).astype(BF)
        queries_ref[:, nope:] = query_rope
        keyval_ref[...] = dot_plain(compressed, up_ref[...]).astype(BF)
        visible = (places_ref[0:1, :] <= place_ref[:, 0:1]) | (early_ref[0, 0:1, :] > 0.0)
        for head in range(heads):
            start = head * (DN + DV)
            scores = dot_last(
                queries_ref[:, head * DN : (head + 1) * DN], keyval_ref[:, start : start + DN]
            ) + dot_last(head_lanes(query_rope, head), key_rope)
            scores = jnp.where(visible, scores * scaling, -1e30)
            weights = jnp.exp(scores - jnp.max(scores, axis=1, keepdims=True))
            attention = weights / jnp.sum(weights, axis=1, keepdims=True)
            attention_ref[0, head] = attention
            context_ref[:, head * DV : (head + 1) * DV] = dot_plain(
                attention.astype(BF), keyval_ref[:, start + DN : start + DN + DV]
            ).astype(BF)

    def by_rows(columns):
        return pl.BlockSpec((length, columns), lambda s: (s, 0))

    def halves():
        return pl.BlockSpec((1, rows, width), lambda s: (s, 0, 0))

    every = sequences * length
    fixed = (gain, down, latent_gain, query, up, cosine, sine_table, place, places)
    columns = (width, span, KVR, query.shape[1], 2 * DR, up.shape[1])
    kinds = (BF, F32, BF, BF, BF, BF)
    return pl.pallas_call(
        body,
        grid=(sequences,),
        in_specs=[halves(), halves()]
        + [whole(array) for array in fixed]
        + [pl.BlockSpec((1,) + early.shape[1:], lambda s: (s, 0, 0))],
        out_specs=[by_rows(c) for c in columns]
        + [
            pl.BlockSpec((1, heads, length, length), lambda s: (s, 0, 0, 0)),
            by_rows(heads * DV),
        ],
        out_shape=[jax.ShapeDtypeStruct((every, c), k) for c, k in zip(columns, kinds)]
        + [
            jax.ShapeDtypeStruct((sequences, heads, length, length), F32),
            jax.ShapeDtypeStruct((every, heads * DV), BF),
        ],
        compiler_params=pltpu.CompilerParams(vmem_limit_bytes=ROOM),
        cost_estimate=pl.CostEstimate(
            flops=2 * every * (width * (span + query.shape[1]) + KVR * up.shape[1]),
            bytes_accessed=32 * 1024 * 1024,
            transcendentals=every * length * heads,
        ),
    )(near, away, *fixed, early)


def attend_back(
    near, away, out, queries, rope, keyval, attention, normed, compressed, query, up, cosine, sine_table
):
    sequences, rows, width = near.shape
    length = 2 * rows
    heads = out.shape[0] // DV
    nope = heads * DN
    span = KVR + 2 * DR
    scaling = (DN + DR) ** (-0.5)

    def body(
        near_ref, away_ref, queries_ref, rope_ref, keyval_ref, attention_ref,
        normed_ref, compressed_ref, out_ref, query_ref, up_ref, cos_ref, sin_ref,
        grad_query_ref, grad_up_ref, own_ref, given_ref, incoming_ref, columns_ref, pairs_ref,
    ):
        @pl.when(pl.program_id(0) == 0)
        def _():
            grad_query_ref[...] = jnp.zeros_like(grad_query_ref)
            grad_up_ref[...] = jnp.zeros_like(grad_up_ref)

        incoming_ref[:rows, :] = near_ref[0]
        incoming_ref[rows:, :] = away_ref[0]
        incoming = incoming_ref[...]
        grad_context = dot_last(incoming, out_ref[...]).astype(BF)
        key_rope = rope_ref[...]
        query_rope = queries_ref[:, nope:]
        grad_query_rope = jnp.zeros((length, 2 * DR), F32)
        grad_key_rope = jnp.zeros((length, 2 * DR), F32)
        for head in range(heads):
            start = head * (DN + DV)
            attention = attention_ref[0, head]
            grad_head = grad_context[:, head * DV : (head + 1) * DV]
            grad_attention = dot_last(grad_head, keyval_ref[:, start + DN : start + DN + DV])
            grad_scores = attention * (
                grad_attention - jnp.sum(attention * grad_attention, axis=1, keepdims=True)
            )
            grad_scores = grad_scores.astype(BF)
            columns_ref[:, head * DN : (head + 1) * DN] = (
                dot_plain(grad_scores, keyval_ref[:, start : start + DN]) * scaling
            ).astype(BF)
            grad_query_rope += head_lanes(dot_plain(grad_scores, key_rope) * scaling, head)
            pairs_ref[:, start : start + DN] = (
                dot_first(grad_scores, queries_ref[:, head * DN : (head + 1) * DN]) * scaling
            ).astype(BF)
            pairs_ref[:, start + DN : start + DN + DV] = dot_first(
                attention.astype(BF), grad_head
            ).astype(BF)
            grad_key_rope += dot_first(grad_scores, head_lanes(query_rope, head)) * scaling
        columns_ref[:, nope:] = turn(grad_query_rope, cos_ref[...], -sin_ref[...]).astype(BF)
        grad_key_rope += pltpu.roll(grad_key_rope, DR, 1)
        columns = columns_ref[...]
        pairs = pairs_ref[...]
        grad_query_ref[...] += dot_first(normed_ref[...], columns)
        grad_up_ref[...] += dot_first(compressed_ref[...], pairs)
        latent = dot_last(pairs, up_ref[...])
        total = dot_last(columns, query_ref[...])
        own_ref[0, :, :width] = total[:rows].astype(BF)
        given_ref[0, :, :width] = total[rows:].astype(BF)
        own_ref[0, :, width : width + KVR] = latent[:rows].astype(BF)
        given_ref[0, :, width : width + KVR] = latent[rows:].astype(BF)
        own_ref[0, :, width + KVR :] = grad_key_rope[:rows].astype(BF)
        given_ref[0, :, width + KVR :] = grad_key_rope[rows:].astype(BF)

    def by_rows(columns):
        return pl.BlockSpec((length, columns), lambda s: (s, 0))

    def halves(columns):
        return pl.BlockSpec((1, rows, columns), lambda s: (s, 0, 0))

    every = sequences * length
    moving = (queries, rope, keyval)
    fixed = (out, query, up, cosine, sine_table)
    shapes = (
        (query.shape, F32), (up.shape, F32),
        ((sequences, rows, width + span), BF), ((sequences, rows, width + span), BF),
    )
    return pl.pallas_call(
        body,
        grid=(sequences,),
        in_specs=[halves(width), halves(width)]
        + [by_rows(array.shape[1]) for array in moving]
        + [pl.BlockSpec((1, heads, length, length), lambda s: (s, 0, 0, 0))]
        + [by_rows(normed.shape[1]), by_rows(compressed.shape[1])]
        + [whole(array) for array in fixed],
        out_specs=[whole(query), whole(up)]
        + [halves(width + span), halves(width + span)],
        out_shape=[jax.ShapeDtypeStruct(shape, kind) for shape, kind in shapes],
        scratch_shapes=[
            pltpu.VMEM((length, width), BF),
            pltpu.VMEM((length, query.shape[1]), BF),
            pltpu.VMEM((length, up.shape[1]), BF),
        ],
        compiler_params=pltpu.CompilerParams(vmem_limit_bytes=ROOM),
        cost_estimate=pl.CostEstimate(
            flops=4 * every * (width * (query.shape[1] + heads * DV) + KVR * up.shape[1]),
            bytes_accessed=48 * 1024 * 1024,
            transcendentals=0,
        ),
    )(near, away, *moving, attention, normed, compressed, *fixed)


def on_device(
    tokens,
    norm1_gain,
    q_weight,
    kv_down,
    latent_gain,
    kv_up,
    o_weight,
    norm2_gain,
    router,
    shared_gate_up,
    shared_down,
    expert_gate_up,
    expert_down,
    teacher,
    routes,
    prefix,
    token_count,
):
    cores = lax.axis_size("fsdp")
    depth = lax.axis_size("z")
    experts = depth * PLANE
    group = cores * PLANE
    heads = NH // group
    core = lax.axis_index("fsdp")
    plane_index = lax.axis_index("z")
    spot = lax.axis_index("r")
    own_expert = plane_index * PLANE + spot
    token_rows = tokens.shape[1]
    model_width = tokens.shape[2]
    seq_length = token_rows * cores
    capacity = -(-max(2, token_rows * TOP * 5 // (experts * 3)) // 16) * 16
    weight_rows = q_weight.shape[0]
    latent_rows = kv_up.shape[0]
    wide_q = heads * (DN + DR)
    wide_kv = heads * (DN + DV)
    scaling = (DN + DR) ** (-0.5)
    devices = cores * experts
    every = PLANE * seq_length
    everywhere = jnp.arange(devices, dtype=jnp.int32) ^ (core * experts + own_expert)

    sub = depth // PLANE
    shard_moves = [
        (z * PLANE + r, ((z % sub) * PLANE + r) * PLANE + z // sub)
        for z in range(depth)
        for r in range(PLANE)
    ]

    fold = weight_rows // latent_rows
    up_fold = wide_kv // fold
    up_packed = kv_up.reshape(latent_rows, group, fold, up_fold)
    up_packed = up_packed.swapaxes(1, 2).reshape(weight_rows, group, up_fold)
    by_head = q_weight.reshape(weight_rows, group, heads, DN + DR)
    packed = jnp.concatenate(
        [
            by_head[..., :DN].reshape(weight_rows, group, heads * DN),
            by_head[..., DN:].reshape(weight_rows, group, heads * DR),
            up_packed,
        ],
        axis=2,
    )
    packed = lax.all_to_all(
        packed.swapaxes(0, 1), ("fsdp", "r"), split_axis=0, concat_axis=0, tiled=True
    )
    packed = packed.reshape(cores, PLANE * weight_rows, wide_q + up_fold)

    own_mask = jnp.any(
        routes[0][:, :, None] == jnp.arange(experts, dtype=jnp.int32)[None, None, :], axis=1
    )
    small = jnp.concatenate(
        [
            kv_down,
            router,
            norm1_gain[:, None],
            norm2_gain[:, None],
            jnp.pad(latent_gain, (0, weight_rows - latent_rows))[:, None],
            jnp.broadcast_to(prefix.astype(BF)[None, :], (weight_rows, 1)),
            own_mask.astype(BF).reshape(weight_rows, -1),
        ],
        axis=1,
    )
    small_width = -(-small.shape[1] // 128) * 128
    small = jnp.pad(small, ((0, 0), (0, small_width - small.shape[1])))
    small = jnp.stack([small] + [hop(small, "z", k) for k in range(1, depth)], axis=0)
    moved_o = lax.ppermute(o_weight, ("z", "r"), shard_moves)
    output_weight = gather_columns_apart(moved_o).reshape(heads * DV, model_width)
    first_rows = tokens[0]
    shared_both = shared_gate_up.reshape(weight_rows, 2 * cores, experts, shared_down.shape[0])
    shared_both = shared_both.transpose(2, 0, 1, 3).reshape(experts, weight_rows, -1)
    packed, small, output_weight, shared_both = lax.optimization_barrier(
        (packed, small, output_weight, shared_both)
    )
    packed = gather_columns(packed)
    first_rows = gather_plane(first_rows)
    small = jnp.stack(gather_plane(after(small, first_rows[-1])), axis=1)
    small = jnp.stack([small, hop(small, "fsdp", 1)], axis=0)
    near_rows = jnp.stack(first_rows, axis=0)
    away_rows = hop(near_rows, "fsdp", 1)

    shared_both = swap_plane(after(shared_both, small))
    packed, shared_both = lax.optimization_barrier((packed, shared_both, small, away_rows))[:2]
    small = small.reshape(devices, weight_rows, small_width)
    prefixes = small[:PLANE, 0, KVR + DR + experts + 3].astype(F32)
    masks = small[:experts, :, KVR + DR + experts + 4 :][:, :, : token_rows * experts // weight_rows]
    masks = masks.astype(F32).reshape(experts, token_rows, experts)
    small = jnp.take(small, everywhere, axis=0, mode="clip").reshape(model_width, small_width)
    down_weight = small[:, : KVR + DR]
    router_weight = small[:, KVR + DR : KVR + DR + experts]
    gains = small[:, KVR + DR + experts : KVR + DR + experts + 3].astype(F32).T
    gain_one_f = gains[0]
    gain_two_f = gains[1]
    latent_gain_f = gains[2].reshape(-1, weight_rows)[:, :latent_rows].reshape(KVR)

    half = jnp.arange(token_rows, dtype=jnp.int32)
    position = jnp.concatenate([core * token_rows + half, (1 - core) * token_rows + half])
    cosine, sine_table = tables(position, DR)
    spread_cos = jnp.tile(cosine, (1, 4))
    spread_sin = jnp.tile(jnp.concatenate([-sine_table, sine_table], axis=1), (1, 2))
    places = position.astype(F32)
    early = (places[None, :] < prefixes[:, None]).astype(F32)
    early = jnp.broadcast_to(early[:, None, :], (PLANE, 8, seq_length))
    packed = packed.swapaxes(0, 1).reshape(model_width, wide_q + up_fold)
    query_weight = packed[:, :wide_q]
    up_weight = packed[:, wide_q:].reshape(KVR, fold * up_fold)


    normed, latent, compressed, queries, key_rope, keyval, attention, context = attend(
        near_rows, away_rows, gain_one_f[None], small, latent_gain_f[None], query_weight,
        up_weight, heads, spread_cos, spread_sin,
        jnp.broadcast_to(places[:, None], (seq_length, 128)),
        jnp.broadcast_to(places[None, :], (8, seq_length)), early,
    )
    sides = context.reshape(PLANE, cores, token_rows, heads * DV)

    def project(side):
        flat = sides[:, side].reshape(PLANE * token_rows, heads * DV)
        return dot_plain(flat, output_weight).reshape(PLANE, token_rows, model_width)

    given_part = project(1).astype(BF)
    own_part = project(0).astype(BF)
    order = jnp.arange(experts, dtype=jnp.int32) ^ own_expert
    mine = (jnp.arange(experts, dtype=jnp.int32) == own_expert).astype(F32)
    taken = jnp.sum(masks * mine[None, None, :], axis=2)
    rank = jnp.cumsum(taken, axis=1) - taken
    select = taken[:, None, :] * (
        rank[:, None, :] == jnp.arange(capacity, dtype=F32)[None, :, None]
    ).astype(F32)
    select_low = select.astype(BF)

    expert_both_weight = lax.all_gather(expert_gate_up, "fsdp", axis=1, tiled=True)[0]
    expert_down_weight = lax.all_gather(expert_down, "fsdp", axis=2, tiled=True)[0]
    unit = shared_down.shape[0]
    shared_units = cores * unit
    shared_both = swap_column(after(shared_both, context)).reshape(
        experts * weight_rows, 2 * shared_units
    )
    shared_both = after(shared_both, expert_both_weight, expert_down_weight)
    shared_both_weight = lax.all_gather(shared_both, "fsdp", axis=0, tiled=True)
    shared_down_weight = lax.all_gather(shared_down, "fsdp", axis=0, tiled=True)

    own_rows = tokens[0].astype(F32)
    hidden = own_rows + scatter_group(own_part, given_part)
    normed2 = rms_norm(hidden, gain_two_f).astype(BF)

    def gates_of(logits, mask):
        logits = jnp.where(mask, logits, -1e30)
        odds = jnp.where(mask, jnp.exp(logits - jnp.max(logits, axis=-1, keepdims=True)), 0.0)
        return odds / jnp.sum(odds, axis=-1, keepdims=True)

    own_gates = gates_of(dot_plain(normed2, router_weight), own_mask)
    steps = depth
    lots = [[k] for k in range(depth)]
    lots = lots[:1] + lots[2:] + lots[1:2]
    block_order = np.array(
        [k * PLANE + j for planes in lots for j in range(PLANE) for k in planes], dtype=np.int32
    )
    chunk_select = jnp.take(select_low, block_order, axis=0, mode="clip")
    chunk_select = chunk_select.reshape(steps, PLANE, capacity, token_rows)
    chunk_masks = jnp.take(masks, block_order, axis=0, mode="clip")
    chunk_masks = chunk_masks.reshape(steps, PLANE * token_rows, experts)
    padded = -(-shared_units // 128) * 128

    def pad_columns(values, columns):
        return jnp.pad(values, ((0, 0), (0, columns - values.shape[1])))

    shared_router = jnp.concatenate(
        [
            pad_columns(shared_both_weight[:, :shared_units], padded),
            pad_columns(shared_both_weight[:, shared_units:], padded),
            pad_columns(router_weight, -(-experts // 128) * 128),
        ],
        axis=1,
    )
    shared_rows = jnp.pad(shared_down_weight, ((0, padded - shared_units), (0, 0)))

    def passes(values, compute, besides):
        def fetch(values, number):
            return jnp.stack([hop(values, "z", k) if k else values for k in lots[number]], axis=0)

        source, pieces, totals, summed = fetch(values, 0), None, None, None
        returned, results = [], []
        for step in range(steps + 3):
            later = [values, None, None, None, None, None]
            if step + 1 < steps:
                later[1] = fetch(values, step + 1)
            if source is not None and totals is not None:
                moved = [
                    hop(jnp.concatenate([source, totals[j]], axis=0), "r", j)
                    for j in range(1, PLANE)
                ]
                later[2] = [source] + [part[: source.shape[0]] for part in moved]
                later[4] = totals[0] + sum(part[source.shape[0] :].astype(F32) for part in moved)
            elif source is not None:
                later[2] = gather_plane(source)
            elif totals is not None:
                later[4] = scatter_plane(totals)
            if pieces is not None:
                later[3] = compute(step - 1, pieces)
            if summed is not None:
                later[5] = [
                    hop(summed[i].astype(BF), "z", k) if k else summed[i]
                    for i, k in enumerate(lots[step - 3])
                ]
            later.append(besides(step, summed if totals is None else totals[0]))
            values, source, pieces, totals, summed, back, beside = lax.optimization_barrier(later)
            if beside is not None:
                results.append(beside)
            if back is not None:
                returned += [part.astype(F32) for part in back]
        return sum(returned), results

    def forward_chunk(number, pieces):
        values = expert_forward(
            pieces, chunk_select[number], chunk_masks[number], mine[None], shared_router,
            expert_both_weight, expert_down_weight, shared_rows,
        )
        saved.append(values[:8])
        return list(values[8:])

    def backward_chunk(number, pieces):
        flat, expert_in, expert_gu, expert_act, picked, gates, shared_gu, shared_act = saved[number]
        values = expert_backward(
            pieces, chunk_select[number], gates, picked, expert_gu, shared_gu, shared_router,
            expert_both_weight, expert_down_weight, shared_rows,
        )
        grads.append(values[:5])
        return list(values[5:])

    saved, grads = [], []
    routed, _ = passes(normed2, forward_chunk, lambda step, behind: None)
    output = hidden + routed
    misfit = output - teacher[0].astype(F32)
    misfit_low = misfit.astype(BF)

    def products(left, right, behind, tall, wide=None):
        lefts = [after(values[left], behind) for values in saved]
        return sums_of_products(lefts, [values[right] for values in grads], tall, wide)

    def weight_grads(step, behind):
        if step == steps + 1:
            grad_gate = jnp.concatenate([values[4][:, 0] for values in grads], axis=0)
            grad_gate = jnp.take(
                after(grad_gate.reshape(experts, token_rows), behind),
                np.argsort(block_order), axis=0, mode="clip",
            )
            squares = jnp.broadcast_to(jnp.sum(misfit * misfit)[None, None], (experts, 128))
            notes = jnp.concatenate([jnp.take(grad_gate, order, axis=0, mode="clip"), squares], axis=1)
            notes = lax.all_to_all(notes, ("z", "r"), split_axis=0, concat_axis=0, tiled=True)
            grad_shared = products(0, 3, behind, 512)
            grad_shared = jnp.concatenate(
                [grad_shared[:, :shared_units], grad_shared[:, padded : padded + shared_units]], axis=1
            )
            return grad_shared, products(7, 0, behind, padded, 512)[:shared_units], notes
        if step == steps + 2:
            return products(3, 1, behind, 128)
        return None

    grad_returned, results = passes(misfit_low, backward_chunk, weight_grads)
    (grad_shared_both, grad_shared_down, notes), grad_expert_down = results
    grad_expert_down = lax.psum_scatter(
        grad_expert_down[None], "fsdp", scatter_dimension=2, tiled=True
    )
    grad_shared_down = lax.psum_scatter(
        grad_shared_down, "fsdp", scatter_dimension=0, tiled=True
    )
    grad_shared_both = lax.psum_scatter(
        grad_shared_both, "fsdp", scatter_dimension=0, tiled=True
    )
    grad_shared_gate_up = (
        lax.all_to_all(
            grad_shared_both.astype(BF).reshape(experts, weight_rows, 2 * shared_units),
            ("z", "r"),
            split_axis=0,
            concat_axis=0,
            tiled=True,
        )
        .reshape(experts, weight_rows, 2 * cores, unit)
        .transpose(1, 2, 0, 3)
        .reshape(weight_rows, 2 * FFS)
        .astype(F32)
    )

    grad_gates = notes[:, :token_rows].T
    all_squares = jnp.sum(notes[:, token_rows])[None]
    all_squares = all_squares + hop(jnp.broadcast_to(all_squares, (8, 128)), "fsdp", 1)[0, :1]
    loss_value = all_squares / (token_count.astype(F32) * model_width)
    grad_logits = (
        own_gates * (grad_gates - jnp.sum(own_gates * grad_gates, axis=1, keepdims=True))
    ).astype(BF)
    grad_normed2 = grad_returned + dot_last(grad_logits, router_weight)
    grad_hidden_norm, grad_gain_two = norm_back(hidden, gain_two_f, grad_normed2)
    grad_hidden = misfit + grad_hidden_norm
    near_grad, away_grad = gather_group(grad_hidden.astype(BF))
    grad_expert_gate_up = products(1, 2, grad_hidden, 256)
    near_grad, away_grad, grad_expert_gate_up, grad_shared_gate_up = lax.optimization_barrier(
        (near_grad, away_grad, grad_expert_gate_up, grad_shared_gate_up)
    )
    grad_expert_gate_up = lax.psum_scatter(
        grad_expert_gate_up[None], "fsdp", scatter_dimension=1, tiled=True
    )

    incoming_rows = jnp.stack([near_grad, away_grad], axis=1).reshape(every, model_width)
    grad_output_weight = sum_columns(
        sums_of_products([context], [incoming_rows], heads * DV).reshape(
            depth, weight_rows, model_width
        )
    )
    grad_query_weight, grad_up, own_part, given_part = attend_back(
        near_grad, away_grad, output_weight, queries, key_rope, keyval, attention,
        normed, compressed, query_weight, up_weight, spread_cos, spread_sin,
    )
    grad_packed = jnp.concatenate([grad_query_weight, grad_up.reshape(model_width, up_fold)], axis=1)
    grad_packed = grad_packed.reshape(cores, depth, PLANE * weight_rows, wide_q + up_fold)
    grad_packed = grad_packed.swapaxes(0, 1).astype(BF)
    grad_output_weight, given_part, grad_packed = lax.optimization_barrier(
        (grad_output_weight, given_part, grad_packed)
    )
    grad_packed = lax.all_to_all(grad_packed, "z", split_axis=0, concat_axis=0, tiled=True)
    grad_packed = jnp.sum(grad_packed.astype(F32), axis=0).astype(BF)
    normed_sum = scatter_group(own_part, given_part)
    latent_sum = normed_sum[:, model_width:]
    grad_output_weight = lax.ppermute(
        grad_output_weight,
        ("z", "r"),
        [(b, a) for a, b in shard_moves],
    )
    own_latent = latent[:token_rows]
    grad_latent_norm, grad_latent_gain = norm_back(
        own_latent[:, :KVR], latent_gain_f, latent_sum[:, :KVR]
    )
    grad_latent = jnp.concatenate(
        [
            grad_latent_norm,
            unrotate(latent_sum[:, KVR : KVR + DR], cosine[:token_rows], sine_table[:token_rows]),
        ],
        axis=1,
    ).astype(BF)
    own_normed = normed[:token_rows]
    grad_normed = normed_sum[:, :model_width] + dot_last(grad_latent, down_weight)
    grad_flat_norm, grad_gain_one = norm_back(own_rows, gain_one_f, grad_normed)
    grad_tokens = grad_hidden + grad_flat_norm
    grad_latent_gain = jnp.pad(
        grad_latent_gain.reshape(-1, latent_rows), ((0, 0), (0, weight_rows - latent_rows))
    ).reshape(model_width)
    base = KVR + DR + experts
    columns = jnp.arange(small_width, dtype=jnp.int32)[None, :]

    def widen(values, start):
        return jnp.pad(values, ((0, 0), (start, small_width - start - values.shape[1])))

    grad_small = (
        dot_first(own_normed, widen(grad_latent, 0))
        + dot_first(normed2, widen(grad_logits, KVR + DR))
        + jnp.where(columns == base, grad_gain_one[:, None], 0.0)
        + jnp.where(columns == base + 1, grad_gain_two[:, None], 0.0)
        + jnp.where(columns == base + 2, grad_latent_gain[:, None], 0.0)
    )
    grad_small = straight(grad_small.astype(BF)).reshape(devices, weight_rows, small_width)
    grad_small = jnp.take(grad_small, everywhere, axis=0, mode="clip")
    grad_small = grad_small.reshape(cores, depth, PLANE, weight_rows, small_width)
    grad_tail = grad_small[0].astype(F32) + hop(grad_small[1], "fsdp", 1).astype(F32)
    grad_small = scatter_plane([grad_tail[:, j] for j in range(PLANE)])
    grad_small = grad_small[0] + sum(
        hop(grad_small[k].astype(BF), "z", k).astype(F32) for k in range(1, depth)
    )
    grad_packed = lax.all_to_all(
        after(grad_packed, grad_tail).reshape(group, weight_rows, wide_q + up_fold),
        ("fsdp", "r"),
        split_axis=0,
        concat_axis=0,
        tiled=True,
    ).swapaxes(0, 1)
    grad_q_weight = jnp.concatenate(
        [
            grad_packed[:, :, : heads * DN].reshape(weight_rows, group, heads, DN),
            grad_packed[:, :, heads * DN : wide_q].reshape(weight_rows, group, heads, DR),
        ],
        axis=3,
    )
    grad_q_weight = grad_q_weight.reshape(weight_rows, -1).astype(F32)
    grad_kv_up = (
        grad_packed[:, :, wide_q:]
        .reshape(latent_rows, fold, group, up_fold)
        .swapaxes(1, 2)
        .reshape(latent_rows, -1)
        .astype(F32)
    )
    return (
        output.astype(BF)[None],
        loss_value,
        grad_tokens[None],
        grad_small[:, base],
        grad_q_weight,
        grad_small[:, : KVR + DR],
        grad_small[:latent_rows, base + 2],
        grad_kv_up,
        grad_output_weight,
        grad_small[:, base + 1],
        grad_small[:, KVR + DR : base],
        grad_shared_gate_up,
        grad_shared_down,
        grad_expert_gate_up,
        grad_expert_down,
    )


def solution(mesh):
    cores = mesh.shape["fsdp"]
    experts = mesh.shape["expert"]
    grid = Mesh(mesh.devices.reshape(cores, experts // PLANE, PLANE), ("fsdp", "z", "r"))
    expert = ("z", "r")
    every = ("fsdp", "z", "r")
    return jax.shard_map(
        on_device,
        mesh=grid,
        in_specs=(
            P(expert, "fsdp", None),
            P(every),
            P(every, None),
            P(every, None),
            P(every),
            P(every, None),
            P(every, None),
            P(every),
            P(every, None),
            P(every, None),
            P(every, None),
            P(expert, "fsdp", None),
            P(expert, None, "fsdp"),
            P(expert, "fsdp", None),
            P(expert, "fsdp", None),
            P(expert),
            P(),
        ),
        out_specs=(
            P(expert, "fsdp", None),
            P(),
            P(expert, "fsdp", None),
            P(every),
            P(every, None),
            P(every, None),
            P(every),
            P(every, None),
            P(every, None),
            P(every),
            P(every, None),
            P(every, None),
            P(every, None),
            P(expert, "fsdp", None),
            P(expert, None, "fsdp"),
        ),
        check_vma=False,
    )
```

```python
import math

import jax
import jax.numpy as jnp
import numpy as np
from jax import lax
from jax.experimental import pallas as pl
from jax.experimental.layout import Layout, with_layout_constraint
from jax.experimental.pallas import tpu as pltpu
from jax.sharding import Mesh
from jax.sharding import PartitionSpec as P

NH = 16
DN = 128
DR = 64
DV = 128
KVR = 512
FFE = 1408
FFS = 2816
TOP = 6
PLANE = 4

BF = jnp.bfloat16
F32 = jnp.float32

epsilon = 1e-06


def rms_norm(values, gain_row):
    return (
        values * lax.rsqrt(jnp.mean(values * values, axis=-1, keepdims=True) + epsilon) * gain_row
    )


def norm_back(values, gain_row, incoming):
    factor = lax.rsqrt(jnp.mean(values * values, axis=-1, keepdims=True) + epsilon)
    scaled = incoming * gain_row
    grad_values = factor * scaled - values * (factor * factor * factor) * jnp.mean(
        scaled * values, axis=-1, keepdims=True
    )
    grad_gain = jnp.sum(incoming * values * factor, axis=0)
    return (grad_values, grad_gain)


def tables(position, rot_width):
    half_width = rot_width // 2
    frequency = 10000.0 ** (-2.0 * jnp.arange(half_width, dtype=F32) / rot_width)
    angles = position.astype(F32)[:, None] * frequency[None, :]
    return (jnp.cos(angles), jnp.sin(angles))


def unrotate(values, cosine, sine_table):
    half_width = values.shape[-1] // 2
    first_half = values[..., :half_width]
    second = values[..., half_width:]
    return jnp.concatenate(
        [first_half * cosine + second * sine_table, second * cosine - first_half * sine_table],
        axis=-1,
    )


def dot_plain(left_side, right_side):
    return jnp.dot(left_side, right_side, preferred_element_type=F32)


def dot_last(left_side, right_side):
    return lax.dot_general(
        left_side, right_side, (((1,), (1,)), ((), ())), preferred_element_type=F32
    )


def dot_first(left_side, right_side):
    return lax.dot_general(
        left_side, right_side, (((0,), (0,)), ((), ())), preferred_element_type=F32
    )


def straight(values):
    return with_layout_constraint(values, Layout(tuple(range(values.ndim))))


def after(values, *others):
    return lax.optimization_barrier((values,) + others)[0]


def stage(*values):
    return lax.optimization_barrier(values)


def hop(values, axis, distance):
    size = lax.axis_size(axis)
    moves = [(i, i ^ distance) for i in range(size)]
    return straight(lax.ppermute(straight(values), axis, moves))


def gather_plane(values):
    return [values] + [hop(values, "r", j) for j in range(1, PLANE)]


def scatter_plane(parts):
    moved = [hop(parts[j].astype(BF), "r", j) for j in range(1, PLANE)]
    return parts[0].astype(F32) + sum(part.astype(F32) for part in moved)


def scatter_sides(own, given):
    total = straight((own.astype(F32) + given.astype(F32)).astype(BF))
    return scatter_plane([total[j] for j in range(PLANE)])


def column_order(axis):
    return jnp.arange(lax.axis_size(axis), dtype=jnp.int32) ^ lax.axis_index(axis)


def both_cores(values):
    other = hop(values, "fsdp", 1)
    first = lax.axis_index("fsdp") == 0
    return jnp.concatenate(
        [jnp.where(first, values, other), jnp.where(first, other, values)], axis=0
    )


def by_column(parts):
    return jnp.take(parts.astype(BF), column_order("z"), axis=0, mode="clip")


def sum_columns(parts):
    moved = [hop(parts[k], "z", k) for k in range(1, lax.axis_size("z"))]
    return parts[0].astype(F32) + sum(part.astype(F32) for part in moved)


def gather_columns(values):
    spread = jnp.broadcast_to(values[None], (lax.axis_size("z"),) + values.shape)
    return lax.all_to_all(spread, "z", split_axis=0, concat_axis=0, tiled=True)


def gather_columns_apart(values):
    column = [values] + [hop(values, "z", k) for k in range(1, lax.axis_size("z"))]
    return jnp.take(jnp.stack(column, axis=0), column_order("z"), axis=0, mode="clip")


def all_order():
    return (column_order("z")[:, None] * PLANE + column_order("r")[None, :]).reshape(-1)


def swap_plane(parts):
    shape = parts.shape[1:]
    parts = jnp.take(parts, all_order(), axis=0, mode="clip")
    parts = parts.reshape((lax.axis_size("z"), PLANE) + shape)
    plane = [parts[:, 0]] + [hop(parts[:, j], "r", j) for j in range(1, PLANE)]
    return jnp.stack(plane, axis=1)


def swap_column(plane):
    depth = lax.axis_size("z")
    column = [plane[0]] + [hop(plane[k], "z", k) for k in range(1, depth)]
    column = jnp.stack(column, axis=0).reshape((depth * PLANE,) + plane.shape[2:])
    return jnp.take(column, all_order(), axis=0, mode="clip")


ROOM = 56 * 1024 * 1024


def whole(array):
    return pl.BlockSpec(array.shape, lambda *_: (0,) * array.ndim)


def sums_of_products(lefts, rights, tall, wide=None, more=None):
    height, width = lefts[0].shape[1], rights[0].shape[1]
    depth = sum(left.shape[0] for left in lefts)
    wide = width if wide is None else wide

    def stack(refs, into):
        start = 0
        for ref in refs:
            into[start : start + ref.shape[0], :] = ref[...]
            start += ref.shape[0]

    def body(*refs):
        out_ref, left_ref, right_ref = refs[-3:]

        @pl.when(pl.program_id(1) == 0)
        def _():
            stack(refs[len(lefts) : len(lefts) + len(rights)], right_ref)

        stack(refs[: len(lefts)], left_ref)
        out_ref[...] = dot_first(left_ref[...], right_ref[...])
        if more is not None:
            out_ref[...] += refs[-4][...]

    return pl.pallas_call(
        body,
        grid=(width // wide, height // tall),
        in_specs=[pl.BlockSpec((left.shape[0], tall), lambda j, i: (0, i)) for left in lefts]
        + [pl.BlockSpec((right.shape[0], wide), lambda j, i: (0, j)) for right in rights]
        + ([] if more is None else [pl.BlockSpec((tall, wide), lambda j, i: (i, j))]),
        out_specs=pl.BlockSpec((tall, wide), lambda j, i: (i, j)),
        out_shape=jax.ShapeDtypeStruct((height, width), F32),
        scratch_shapes=[pltpu.VMEM((depth, tall), BF), pltpu.VMEM((depth, wide), BF)],
        compiler_params=pltpu.CompilerParams(vmem_limit_bytes=ROOM),
        cost_estimate=pl.CostEstimate(
            flops=2 * depth * height * width,
            bytes_accessed=2 * depth * (height + width) + 4 * height * width,
            transcendentals=0,
        ),
    )(*lefts, *rights, *([] if more is None else [more]))


def swiglu_parts(gate, up, incoming):
    sigmoid = jax.nn.sigmoid(gate)
    return (
        (incoming * up * sigmoid * (1.0 + gate * (1.0 - sigmoid))).astype(BF),
        (incoming * gate * sigmoid).astype(BF),
    )


TILE = 256
STRIP = 512
PARTS = 4


def spans(size, width):
    return [slice(start, min(start + width, size)) for start in range(0, size, width)]


class Copies:
    def __init__(self, semaphores):
        self.semaphores = semaphores
        self.used = 0

    def start(self, source, target):
        copy = pltpu.make_async_copy(source, target, self.semaphores.at[self.used])
        self.used += 1
        copy.start()
        return [copy]

    def start_rows(self, source, target):
        rows = source.shape[0]
        step = rows // PARTS
        copies = []
        for part in range(PARTS):
            span = pl.ds(part * step, step)
            copies += self.start(source.at[span, :], target.at[span, :])
        return copies


def wait(copies):
    for copy in copies:
        copy.wait()


def expert_forward(pieces, chosen, masks, mine, shared_router, both, down, shared_down):
    planes, rows, width = pieces[0].shape
    blocks, capacity = chosen.shape[:2]
    slots, flat_rows = blocks * capacity, blocks * rows
    hidden, units, experts = down.shape[0], shared_down.shape[0], mine.shape[1]
    strips = spans(width, STRIP)
    shapes = [
        ((slots, width), BF), ((slots, 2 * hidden), BF), ((slots, hidden), BF), ((slots, width), BF),
        ((flat_rows, 2 * units), BF), ((flat_rows, units), BF),
    ] + [((planes, rows, width), F32 if j == 0 else BF) for j in range(PLANE)]
    gate_shape = jax.ShapeDtypeStruct((flat_rows, 128), F32)

    def body(
        chosen_ref, masks_ref, mine_ref, piece_0, piece_1, piece_2, piece_3, router_hbm, both_hbm,
        down_hbm, shared_down_hbm,
        gates_ref, in_hbm, gu_hbm, act_hbm, out_hbm, shared_gu_hbm, shared_act_hbm,
        total_0, total_1, total_2, total_3,
        rows_ref, router_ref, both_ref, down_ref, shared_down_ref,
        in_ref, gu_ref, act_ref, out_ref, shared_gu_ref, shared_act_ref,
        sum_0, sum_1, sum_2, sum_3, semaphores,
    ):
        copies = Copies(semaphores)
        totals, sums = (total_0, total_1, total_2, total_3), (sum_0, sum_1, sum_2, sum_3)
        coming = []
        for j, piece in enumerate((piece_0, piece_1, piece_2, piece_3)):
            for k in range(planes):
                target = rows_ref.at[pl.ds((j * planes + k) * rows, rows), :]
                coming.append(copies.start(piece.at[k], target))
        router_in = copies.start_rows(router_hbm, router_ref)
        both_in = copies.start_rows(both_hbm, both_ref)
        down_in = copies.start_rows(down_hbm, down_ref)
        down_in += copies.start(shared_down_hbm, shared_down_ref)
        for block in range(blocks):
            wait(coming[block])
            in_ref[block * capacity : (block + 1) * capacity, :] = dot_plain(
                chosen_ref[block], rows_ref[block * rows : (block + 1) * rows, :]
            ).astype(BF)
        leaving = copies.start(in_ref, in_hbm)
        wait(router_in)
        joined = dot_plain(rows_ref[...], router_ref[...])
        gate, up = joined[:, :units], joined[:, units : 2 * units]
        shared_gu_ref[...] = joined[:, : 2 * units].astype(BF)
        shared_act_ref[...] = (gate * jax.nn.sigmoid(gate) * up).astype(BF)
        leaving += copies.start(shared_gu_ref, shared_gu_hbm)
        leaving += copies.start(shared_act_ref, shared_act_hbm)
        mask = masks_ref[...] > 0.0
        logits = jnp.where(mask, joined[:, 2 * units : 2 * units + experts], -1e30)
        odds = jnp.exp(logits - jnp.max(logits, axis=1, keepdims=True))
        odds = jnp.where(mask, odds, 0.0)
        own = jnp.sum(odds * mine_ref[...], axis=1, keepdims=True)
        own = own / jnp.sum(odds, axis=1, keepdims=True)
        gates_ref[...] = jnp.broadcast_to(own, gates_ref.shape)
        wait(both_in)
        for span in spans(hidden, TILE):
            above = slice(hidden + span.start, hidden + span.stop)
            gate = dot_plain(in_ref[...], both_ref[:, span])
            up = dot_plain(in_ref[...], both_ref[:, above])
            gu_ref[:, span] = gate.astype(BF)
            gu_ref[:, above] = up.astype(BF)
            act_ref[:, span] = (gate * jax.nn.sigmoid(gate) * up).astype(BF)
        leaving += copies.start(gu_ref, gu_hbm)
        leaving += copies.start(act_ref, act_hbm)
        wait(down_in)
        for strip in strips:
            out_ref[:, strip] = dot_plain(act_ref[...], down_ref[:, strip]).astype(BF)
            shared = dot_plain(shared_act_ref[...], shared_down_ref[:, strip])
            for j in range(PLANE):
                for k in range(planes):
                    block = j * planes + k
                    span = slice(block * rows, (block + 1) * rows)
                    picked = dot_first(
                        chosen_ref[block], out_ref[block * capacity : (block + 1) * capacity, strip]
                    )
                    sums[j][k, :, strip] = (gates_ref[span, 0:1] * picked + shared[span, :]).astype(
                        sums[j].dtype
                    )
                place = pl.ds(strip.start, strip.stop - strip.start)
                leaving += copies.start(sums[j].at[:, :, place], totals[j].at[:, :, place])
        leaving += copies.start(out_ref, out_hbm)
        wait(leaving)

    anywhere = pl.BlockSpec(memory_space=pl.ANY)
    moved = [shared_router, both, down, shared_down]
    scratch = [pltpu.VMEM((flat_rows, width), BF)]
    scratch += [pltpu.VMEM(array.shape, BF) for array in moved]
    scratch += [pltpu.VMEM(*shape) for shape in shapes]
    count = blocks + 3 * PARTS + 1 + 6 + PLANE * len(strips)
    return pl.pallas_call(
        body,
        in_specs=[pl.BlockSpec(memory_space=pltpu.VMEM)] * 3 + [anywhere] * (PLANE + len(moved)),
        out_specs=[pl.BlockSpec(memory_space=pltpu.VMEM)] + [anywhere] * len(shapes),
        out_shape=[gate_shape] + [jax.ShapeDtypeStruct(*shape) for shape in shapes],
        scratch_shapes=scratch + [pltpu.SemaphoreType.DMA((count,))],
        compiler_params=pltpu.CompilerParams(vmem_limit_bytes=ROOM),
        cost_estimate=pl.CostEstimate(
            flops=2 * width * (3 * slots * hidden + flat_rows * 4 * units),
            bytes_accessed=2 * width * (3 * hidden + 4 * units + 4 * flat_rows) + 12 * slots * hidden,
            transcendentals=slots * hidden,
        ),
    )(chosen, masks, mine, *pieces, *moved)


def expert_backward(pieces, chosen, gates, gu, out, shared_gu, shared_router, both, down, shared_down):
    planes, rows, width = pieces[0].shape
    blocks, capacity = chosen.shape[:2]
    slots, flat_rows = blocks * capacity, blocks * rows
    hidden, units = down.shape[0], shared_down.shape[0]
    strips = spans(width, STRIP)
    shapes = [
        ((slots, width), BF), ((slots, 2 * hidden), BF), ((flat_rows, 2 * units), BF),
    ] + [((planes, rows, width), F32 if j == 0 else BF) for j in range(PLANE)]
    gate_shape = jax.ShapeDtypeStruct((flat_rows, 128), F32)

    def body(
        chosen_ref, gates_ref, piece_0, piece_1, piece_2, piece_3, out_hbm, shared_gu_hbm, shared_down_hbm,
        gu_hbm, down_hbm, router_hbm, both_hbm,
        grad_gate_ref, slots_hbm, grad_gu_hbm, grad_shared_hbm, total_0, total_1, total_2, total_3,
        rows_ref, out_ref, shared_gu_ref, shared_down_ref, gu_ref, down_ref, router_ref, both_ref,
        slots_ref, grad_gu_ref, grad_shared_ref, sum_0, sum_1, sum_2, sum_3, semaphores,
    ):
        copies = Copies(semaphores)
        totals, sums = (total_0, total_1, total_2, total_3), (sum_0, sum_1, sum_2, sum_3)
        coming = []
        for j, piece in enumerate((piece_0, piece_1, piece_2, piece_3)):
            for k in range(planes):
                target = rows_ref.at[pl.ds((j * planes + k) * rows, rows), :]
                coming.append(copies.start(piece.at[k], target))
        out_in = copies.start_rows(out_hbm, out_ref)
        shared_in = copies.start(shared_gu_hbm, shared_gu_ref)
        shared_in += copies.start(shared_down_hbm, shared_down_ref)
        down_in = copies.start_rows(down_hbm, down_ref)
        down_in += copies.start(gu_hbm, gu_ref)
        both_in = copies.start_rows(both_hbm, both_ref)
        both_in += copies.start_rows(router_hbm, router_ref)
        wait(out_in)
        for block in range(blocks):
            wait(coming[block])
            span = slice(block * rows, (block + 1) * rows)
            part = slice(block * capacity, (block + 1) * capacity)
            values = rows_ref[span, :].astype(F32)
            slots_ref[part, :] = dot_plain(
                chosen_ref[block], (gates_ref[span, 0:1] * values).astype(BF)
            ).astype(BF)
            picked = dot_first(chosen_ref[block], out_ref[part, :])
            own = jnp.sum(values * picked, axis=1, keepdims=True)
            grad_gate_ref[span, :] = jnp.broadcast_to(own, (rows, 128))
        leaving = copies.start(slots_ref, slots_hbm)
        wait(shared_in)
        grad_gate, grad_up = swiglu_parts(
            shared_gu_ref[:, :units].astype(F32),
            shared_gu_ref[:, units:].astype(F32),
            dot_last(rows_ref[...], shared_down_ref[...]),
        )
        grad_shared_ref[:, :units] = grad_gate
        grad_shared_ref[:, units:] = grad_up
        leaving += copies.start(grad_shared_ref, grad_shared_hbm)
        wait(down_in)
        for span in spans(hidden, TILE):
            above = slice(hidden + span.start, hidden + span.stop)
            grad_gate, grad_up = swiglu_parts(
                gu_ref[:, span].astype(F32),
                gu_ref[:, above].astype(F32),
                dot_last(slots_ref[...], down_ref[span, :]),
            )
            grad_gu_ref[:, span] = grad_gate
            grad_gu_ref[:, above] = grad_up
        leaving += copies.start(grad_gu_ref, grad_gu_hbm)
        wait(both_in)
        for strip in strips:
            grad_in = dot_last(grad_gu_ref[...], both_ref[strip, :]).astype(BF)
            shared = dot_last(grad_shared_ref[...], router_ref[strip, : 2 * units])
            for j in range(PLANE):
                for k in range(planes):
                    block = j * planes + k
                    moved = dot_first(
                        chosen_ref[block], grad_in[block * capacity : (block + 1) * capacity, :]
                    )
                    sums[j][k, :, strip] = (moved + shared[block * rows : (block + 1) * rows, :]).astype(
                        sums[j].dtype
                    )
                place = pl.ds(strip.start, strip.stop - strip.start)
                leaving += copies.start(sums[j].at[:, :, place], totals[j].at[:, :, place])
        wait(leaving)

    anywhere = pl.BlockSpec(memory_space=pl.ANY)
    moved = [out, shared_gu, shared_down, gu, down, shared_router, both]
    scratch = [pltpu.VMEM((flat_rows, width), BF)]
    scratch += [pltpu.VMEM(array.shape, BF) for array in moved]
    scratch += [pltpu.VMEM(*shape) for shape in shapes]
    count = blocks + 4 * PARTS + 3 + 3 + PLANE * len(strips)
    return pl.pallas_call(
        body,
        in_specs=[pl.BlockSpec(memory_space=pltpu.VMEM)] * 2 + [anywhere] * (PLANE + len(moved)),
        out_specs=[pl.BlockSpec(memory_space=pltpu.VMEM)] + [anywhere] * len(shapes),
        out_shape=[gate_shape] + [jax.ShapeDtypeStruct(*shape) for shape in shapes],
        scratch_shapes=scratch + [pltpu.SemaphoreType.DMA((count,))],
        compiler_params=pltpu.CompilerParams(vmem_limit_bytes=ROOM),
        cost_estimate=pl.CostEstimate(
            flops=2 * width * (3 * slots * hidden + flat_rows * 4 * units),
            bytes_accessed=2 * width * (3 * hidden + 4 * units + 6 * flat_rows) + 12 * slots * hidden,
            transcendentals=slots * hidden,
        ),
    )(chosen, gates, *pieces, *moved)


def turn(values, cosine, sine_table):
    lane = lax.broadcasted_iota(jnp.int32, values.shape, 1)
    wide = values.shape[1]
    swapped = jnp.where(
        lane % DR < DR // 2,
        pltpu.roll(values, wide - DR // 2, 1),
        pltpu.roll(values, DR // 2, 1),
    )
    return values * cosine + swapped * sine_table


def head_lanes(values, head):
    lane = lax.broadcasted_iota(jnp.int32, values.shape, 1)
    return jnp.where(lane // DR == head, values, jnp.zeros_like(values))


def attend(near, away, gain, down, latent_gain, query, up, heads, cosine, sine_table, place, places, early):
    sequences, rows, width = near.shape
    length = 2 * rows
    nope = heads * DN
    span = KVR + 2 * DR
    scaling = (DN + DR) ** (-0.5)

    def body(
        near_ref, away_ref, gain_ref, down_ref, latent_gain_ref, query_ref, up_ref, cos_ref, sin_ref, place_ref, places_ref, early_ref,
        normed_ref, latent_ref, compressed_ref, queries_ref, rope_ref, keyval_ref,
        attention_ref, context_ref,
    ):
        for side, ref in enumerate((near_ref, away_ref)):
            values = ref[0].astype(F32)
            normed_ref[side * rows : (side + 1) * rows, :] = rms_norm(values, gain_ref[...]).astype(BF)
        normed = normed_ref[...]
        latent = dot_plain(normed, down_ref[:, :span])
        latent_ref[...] = latent
        compressed = rms_norm(latent[:, :KVR], latent_gain_ref[...]).astype(BF)
        compressed_ref[...] = compressed
        key_rope = head_lanes(turn(latent[:, KVR:], cos_ref[...], sin_ref[...]), 0)
        key_rope = (key_rope + pltpu.roll(key_rope, DR, 1)).astype(BF)
        rope_ref[...] = key_rope
        query_raw = dot_plain(normed, query_ref[...])
        queries_ref[:, :nope] = query_raw[:, :nope].astype(BF)
        query_rope = turn(query_raw[:, nope:], cos_ref[...], sin_ref[...]).astype(BF)
        queries_ref[:, nope:] = query_rope
        keyval_ref[...] = dot_plain(compressed, up_ref[...]).astype(BF)
        visible = (places_ref[0:1, :] <= place_ref[:, 0:1]) | (early_ref[0, 0:1, :] > 0.0)
        for head in range(heads):
            start = head * (DN + DV)
            scores = dot_last(
                queries_ref[:, head * DN : (head + 1) * DN], keyval_ref[:, start : start + DN]
            ) + dot_last(head_lanes(query_rope, head), key_rope)
            scores = jnp.where(visible, scores * scaling, -1e30)
            weights = jnp.exp(scores - jnp.max(scores, axis=1, keepdims=True))
            attention = weights / jnp.sum(weights, axis=1, keepdims=True)
            attention_ref[0, head] = attention
            context_ref[:, head * DV : (head + 1) * DV] = dot_plain(
                attention.astype(BF), keyval_ref[:, start + DN : start + DN + DV]
            ).astype(BF)

    def by_rows(columns):
        return pl.BlockSpec((length, columns), lambda s: (s, 0))

    def halves():
        return pl.BlockSpec((1, rows, width), lambda s: (s, 0, 0))

    every = sequences * length
    fixed = (gain, down, latent_gain, query, up, cosine, sine_table, place, places)
    columns = (width, span, KVR, query.shape[1], 2 * DR, up.shape[1])
    kinds = (BF, F32, BF, BF, BF, BF)
    return pl.pallas_call(
        body,
        grid=(sequences,),
        in_specs=[halves(), halves()]
        + [whole(array) for array in fixed]
        + [pl.BlockSpec((1,) + early.shape[1:], lambda s: (s, 0, 0))],
        out_specs=[by_rows(c) for c in columns]
        + [
            pl.BlockSpec((1, heads, length, length), lambda s: (s, 0, 0, 0)),
            by_rows(heads * DV),
        ],
        out_shape=[jax.ShapeDtypeStruct((every, c), k) for c, k in zip(columns, kinds)]
        + [
            jax.ShapeDtypeStruct((sequences, heads, length, length), F32),
            jax.ShapeDtypeStruct((every, heads * DV), BF),
        ],
        compiler_params=pltpu.CompilerParams(vmem_limit_bytes=ROOM),
        cost_estimate=pl.CostEstimate(
            flops=2 * every * (width * (span + query.shape[1]) + KVR * up.shape[1]),
            bytes_accessed=32 * 1024 * 1024,
            transcendentals=every * length * heads,
        ),
    )(near, away, *fixed, early)


def attend_back(
    near, away, out, queries, rope, keyval, attention, normed, compressed, query, up, cosine, sine_table
):
    sequences, rows, width = near.shape
    length = 2 * rows
    heads = out.shape[0] // DV
    nope = heads * DN
    span = KVR + 2 * DR
    scaling = (DN + DR) ** (-0.5)

    def body(
        near_ref, away_ref, queries_ref, rope_ref, keyval_ref, attention_ref,
        normed_ref, compressed_ref, out_ref, query_ref, up_ref, cos_ref, sin_ref,
        grad_query_out, grad_up_out, own_ref, given_ref,
        grad_query_ref, grad_up_ref, incoming_ref, columns_ref, pairs_ref,
    ):
        @pl.when(pl.program_id(0) == 0)
        def _():
            grad_query_ref[...] = jnp.zeros_like(grad_query_ref)
            grad_up_ref[...] = jnp.zeros_like(grad_up_ref)

        incoming_ref[:rows, :] = near_ref[0]
        incoming_ref[rows:, :] = away_ref[0]
        incoming = incoming_ref[...]
        grad_context = dot_last(incoming, out_ref[...]).astype(BF)
        key_rope = rope_ref[...]
        query_rope = queries_ref[:, nope:]
        grad_query_rope = jnp.zeros((length, 2 * DR), F32)
        grad_key_rope = jnp.zeros((length, 2 * DR), F32)
        for head in range(heads):
            start = head * (DN + DV)
            attention = attention_ref[0, head]
            grad_head = grad_context[:, head * DV : (head + 1) * DV]
            grad_attention = dot_last(grad_head, keyval_ref[:, start + DN : start + DN + DV])
            grad_scores = attention * (
                grad_attention - jnp.sum(attention * grad_attention, axis=1, keepdims=True)
            )
            grad_scores = grad_scores.astype(BF)
            columns_ref[:, head * DN : (head + 1) * DN] = (
                dot_plain(grad_scores, keyval_ref[:, start : start + DN]) * scaling
            ).astype(BF)
            grad_query_rope += head_lanes(dot_plain(grad_scores, key_rope) * scaling, head)
            pairs_ref[:, start : start + DN] = (
                dot_first(grad_scores, queries_ref[:, head * DN : (head + 1) * DN]) * scaling
            ).astype(BF)
            pairs_ref[:, start + DN : start + DN + DV] = dot_first(
                attention.astype(BF), grad_head
            ).astype(BF)
            grad_key_rope += dot_first(grad_scores, head_lanes(query_rope, head)) * scaling
        columns_ref[:, nope:] = turn(grad_query_rope, cos_ref[...], -sin_ref[...]).astype(BF)
        grad_key_rope += pltpu.roll(grad_key_rope, DR, 1)
        columns = columns_ref[...]
        pairs = pairs_ref[...]
        grad_query_ref[...] += dot_first(normed_ref[...], columns)
        grad_up_ref[...] += dot_first(compressed_ref[...], pairs)
        latent = dot_last(pairs, up_ref[...])
        total = dot_last(columns, query_ref[...])
        own_ref[0, :, :width] = total[:rows].astype(BF)
        given_ref[0, :, :width] = total[rows:].astype(BF)
        own_ref[0, :, width : width + KVR] = latent[:rows].astype(BF)
        given_ref[0, :, width : width + KVR] = latent[rows:].astype(BF)
        own_ref[0, :, width + KVR :] = grad_key_rope[:rows].astype(BF)

        @pl.when(pl.program_id(0) == sequences - 1)
        def _():
            grad_query_out[...] = grad_query_ref[...].astype(BF)
            grad_up_out[...] = grad_up_ref[...].astype(BF)

        given_ref[0, :, width + KVR :] = grad_key_rope[rows:].astype(BF)

    def by_rows(columns):
        return pl.BlockSpec((length, columns), lambda s: (s, 0))

    def halves(columns):
        return pl.BlockSpec((1, rows, columns), lambda s: (s, 0, 0))

    every = sequences * length
    moving = (queries, rope, keyval)
    fixed = (out, query, up, cosine, sine_table)
    shapes = (
        (query.shape, BF), (up.shape, BF),
        ((sequences, rows, width + span), BF), ((sequences, rows, width + span), BF),
    )
    return pl.pallas_call(
        body,
        grid=(sequences,),
        in_specs=[halves(width), halves(width)]
        + [by_rows(array.shape[1]) for array in moving]
        + [pl.BlockSpec((1, heads, length, length), lambda s: (s, 0, 0, 0))]
        + [by_rows(normed.shape[1]), by_rows(compressed.shape[1])]
        + [whole(array) for array in fixed],
        out_specs=[whole(query), whole(up)]
        + [halves(width + span), halves(width + span)],
        out_shape=[jax.ShapeDtypeStruct(shape, kind) for shape, kind in shapes],
        scratch_shapes=[
            pltpu.VMEM(query.shape, F32),
            pltpu.VMEM(up.shape, F32),
            pltpu.VMEM((length, width), BF),
            pltpu.VMEM((length, query.shape[1]), BF),
            pltpu.VMEM((length, up.shape[1]), BF),
        ],
        compiler_params=pltpu.CompilerParams(vmem_limit_bytes=ROOM),
        cost_estimate=pl.CostEstimate(
            flops=4 * every * (width * (query.shape[1] + heads * DV) + KVR * up.shape[1]),
            bytes_accessed=48 * 1024 * 1024,
            transcendentals=0,
        ),
    )(near, away, *moving, attention, normed, compressed, *fixed)


def on_device(
    tokens,
    norm1_gain,
    q_weight,
    kv_down,
    latent_gain,
    kv_up,
    o_weight,
    norm2_gain,
    router,
    shared_gate_up,
    shared_down,
    expert_gate_up,
    expert_down,
    teacher,
    routes,
    prefix,
    token_count,
):
    cores = lax.axis_size("fsdp")
    depth = lax.axis_size("z")
    experts = depth * PLANE
    group = cores * PLANE
    heads = NH // group
    core = lax.axis_index("fsdp")
    plane_index = lax.axis_index("z")
    spot = lax.axis_index("r")
    own_expert = plane_index * PLANE + spot
    token_rows = tokens.shape[1]
    model_width = tokens.shape[2]
    seq_length = token_rows * cores
    capacity = -(-max(2, token_rows * TOP * 5 // (experts * 3)) // 16) * 16
    weight_rows = q_weight.shape[0]
    latent_rows = kv_up.shape[0]
    wide_q = heads * (DN + DR)
    wide_kv = heads * (DN + DV)
    scaling = (DN + DR) ** (-0.5)
    devices = cores * experts
    every = PLANE * seq_length
    everywhere = jnp.arange(devices, dtype=jnp.int32) ^ (core * experts + own_expert)

    sub = depth // PLANE
    shard_moves = [
        (z * PLANE + r, ((z % sub) * PLANE + r) * PLANE + z // sub)
        for z in range(depth)
        for r in range(PLANE)
    ]

    moved_o = lax.ppermute(o_weight, ("z", "r"), shard_moves)
    first_rows = tokens[0]

    fold = weight_rows // latent_rows
    up_fold = wide_kv // fold
    up_packed = kv_up.reshape(latent_rows, group, fold, up_fold)
    up_packed = up_packed.swapaxes(1, 2).reshape(weight_rows, group, up_fold)
    by_head = q_weight.reshape(weight_rows, group, heads, DN + DR)
    packed = jnp.concatenate(
        [
            by_head[..., :DN].reshape(weight_rows, group, heads * DN),
            by_head[..., DN:].reshape(weight_rows, group, heads * DR),
            up_packed,
        ],
        axis=2,
    )
    packed = lax.all_to_all(
        packed.swapaxes(0, 1), ("fsdp", "r"), split_axis=0, concat_axis=0, tiled=True
    )
    packed = packed.reshape(cores, PLANE * weight_rows, wide_q + up_fold)

    own_mask = jnp.any(
        routes[0][:, :, None] == jnp.arange(experts, dtype=jnp.int32)[None, None, :], axis=1
    )
    small = jnp.concatenate(
        [
            kv_down,
            router,
            norm1_gain[:, None],
            norm2_gain[:, None],
            jnp.pad(latent_gain, (0, weight_rows - latent_rows))[:, None],
            jnp.broadcast_to(prefix.astype(BF)[None, :], (weight_rows, 1)),
            own_mask.astype(BF).reshape(weight_rows, -1),
        ],
        axis=1,
    )
    small_width = -(-small.shape[1] // 128) * 128
    small = jnp.pad(small, ((0, 0), (0, small_width - small.shape[1])))
    small = jnp.stack([small] + [hop(small, "z", k) for k in range(1, depth)], axis=0)
    shared_both = shared_gate_up.reshape(weight_rows, 2 * cores, experts, shared_down.shape[0])
    shared_both = shared_both.transpose(2, 0, 1, 3).reshape(experts, weight_rows, -1)
    near_rows = jnp.stack(gather_plane(first_rows), axis=0)
    packed, small, near_rows, shared_both = stage(packed, small, near_rows, shared_both)
    packed = gather_columns(packed)
    away_rows = hop(near_rows, "fsdp", 1)
    small = jnp.stack(gather_plane(small), axis=1)
    small = jnp.stack([small, hop(small, "fsdp", 1)], axis=0)
    shared_both = swap_plane(after(shared_both, small))
    packed, shared_both, moved_o = stage(packed, shared_both, moved_o, small, away_rows)[:3]
    output_weight = gather_columns_apart(moved_o).reshape(heads * DV, model_width)
    small = small.reshape(devices, weight_rows, small_width)
    prefixes = small[:PLANE, 0, KVR + DR + experts + 3].astype(F32)
    masks = small[:experts, :, KVR + DR + experts + 4 :][:, :, : token_rows * experts // weight_rows]
    masks = masks.astype(F32).reshape(experts, token_rows, experts)
    order = jnp.arange(experts, dtype=jnp.int32) ^ own_expert
    mine = (jnp.arange(experts, dtype=jnp.int32) == own_expert).astype(F32)
    taken = jnp.sum(masks * mine[None, None, :], axis=2)
    rank = jnp.cumsum(taken, axis=1) - taken
    select = taken[:, None, :] * (
        rank[:, None, :] == jnp.arange(capacity, dtype=F32)[None, :, None]
    ).astype(F32)
    select_low = select.astype(BF)
    steps = depth
    lots = [[k] for k in range(depth)]
    lots = lots[:1] + lots[2:] + lots[1:2]
    block_order = np.array(
        [k * PLANE + j for planes in lots for j in range(PLANE) for k in planes], dtype=np.int32
    )
    chunk_select = jnp.take(select_low, block_order, axis=0, mode="clip")
    chunk_select = chunk_select.reshape(steps, PLANE, capacity, token_rows)
    chunk_masks = jnp.take(masks, block_order, axis=0, mode="clip")
    chunk_masks = chunk_masks.reshape(steps, PLANE * token_rows, experts)

    small = jnp.take(small, everywhere, axis=0, mode="clip").reshape(model_width, small_width)
    down_weight = small[:, : KVR + DR]
    router_weight = small[:, KVR + DR : KVR + DR + experts]
    gains = small[:, KVR + DR + experts : KVR + DR + experts + 3].astype(F32).T
    gain_one_f = gains[0]
    gain_two_f = gains[1]
    latent_gain_f = gains[2].reshape(-1, weight_rows)[:, :latent_rows].reshape(KVR)

    half = jnp.arange(token_rows, dtype=jnp.int32)
    position = jnp.concatenate([core * token_rows + half, (1 - core) * token_rows + half])
    cosine, sine_table = tables(position, DR)
    spread_cos = jnp.tile(cosine, (1, 4))
    spread_sin = jnp.tile(jnp.concatenate([-sine_table, sine_table], axis=1), (1, 2))
    places = position.astype(F32)
    early = (places[None, :] < prefixes[:, None]).astype(F32)
    early = jnp.broadcast_to(early[:, None, :], (PLANE, 8, seq_length))
    packed = packed.swapaxes(0, 1).reshape(model_width, wide_q + up_fold)
    query_weight = packed[:, :wide_q]
    up_weight = packed[:, wide_q:].reshape(KVR, fold * up_fold)


    normed, latent, compressed, queries, key_rope, keyval, attention, context = attend(
        near_rows, away_rows, gain_one_f[None], small, latent_gain_f[None], query_weight,
        up_weight, heads, spread_cos, spread_sin,
        jnp.broadcast_to(places[:, None], (seq_length, 128)),
        jnp.broadcast_to(places[None, :], (8, seq_length)), early,
    )
    expert_both_weight = lax.all_gather(expert_gate_up, "fsdp", axis=1, tiled=True)[0]
    expert_down_weight = lax.all_gather(expert_down, "fsdp", axis=2, tiled=True)[0]
    unit = shared_down.shape[0]
    shared_units = cores * unit
    context, output_weight, chunk_select, chunk_masks = stage(
        context, output_weight, chunk_select, chunk_masks
    )
    sides = context.reshape(PLANE, cores, token_rows, heads * DV)

    def project(side):
        flat = sides[:, side].reshape(PLANE * token_rows, heads * DV)
        return dot_plain(flat, output_weight).reshape(PLANE, token_rows, model_width)

    given_part = hop(project(1).astype(BF), "fsdp", 1)
    own_part = project(0).astype(BF)
    shared_down_weight = both_cores(shared_down)
    own_part, given_part, shared_both, shared_down_weight = stage(
        own_part, given_part, shared_both, shared_down_weight
    )
    shared_both = swap_column(shared_both).reshape(experts * weight_rows, 2 * shared_units)
    own_rows = tokens[0].astype(F32)
    hidden = own_rows + scatter_sides(own_part, given_part)
    hidden, shared_both = stage(hidden, shared_both)
    shared_both_weight = both_cores(shared_both)
    normed2 = rms_norm(hidden, gain_two_f).astype(BF)

    def gates_of(logits, mask):
        logits = jnp.where(mask, logits, -1e30)
        odds = jnp.where(mask, jnp.exp(logits - jnp.max(logits, axis=-1, keepdims=True)), 0.0)
        return odds / jnp.sum(odds, axis=-1, keepdims=True)

    own_gates = gates_of(dot_plain(normed2, router_weight), own_mask)
    padded = -(-shared_units // 128) * 128

    def pad_columns(values, columns):
        return jnp.pad(values, ((0, 0), (0, columns - values.shape[1])))

    shared_router = jnp.concatenate(
        [
            pad_columns(shared_both_weight[:, :shared_units], padded),
            pad_columns(shared_both_weight[:, shared_units:], padded),
            pad_columns(router_weight, -(-experts // 128) * 128),
        ],
        axis=1,
    )
    shared_rows = jnp.pad(shared_down_weight, ((0, padded - shared_units), (0, 0)))

    def passes(values, compute, besides):
        def fetch(values, number):
            return jnp.stack([hop(values, "z", k) if k else values for k in lots[number]], axis=0)

        source, pieces, totals, summed = fetch(values, 0), None, None, None
        returned, results = [], []
        for step in range(steps + 3):
            later = [values, None, None, None, None, None]
            if step + 1 < steps:
                later[1] = fetch(values, step + 1)
            if source is not None and totals is not None:
                moved = [
                    hop(jnp.concatenate([source, totals[j]], axis=0), "r", j)
                    for j in range(1, PLANE)
                ]
                later[2] = [source] + [part[: source.shape[0]] for part in moved]
                later[4] = totals[0] + sum(part[source.shape[0] :].astype(F32) for part in moved)
            elif source is not None:
                later[2] = gather_plane(source)
            elif totals is not None:
                later[4] = scatter_plane(totals)
            if pieces is not None:
                later[3] = compute(step - 1, pieces, results)
            if summed is not None:
                later[5] = [
                    hop(summed[i].astype(BF), "z", k) if k else summed[i]
                    for i, k in enumerate(lots[step - 3])
                ]
            later.append(besides(step, summed if totals is None else totals[0], results))
            values, source, pieces, totals, summed, back, beside = lax.optimization_barrier(later)
            if beside is not None:
                results.append(beside)
            if back is not None:
                returned += [part.astype(F32) for part in back]
        return sum(returned), results

    def forward_chunk(number, pieces, results):
        values = expert_forward(
            pieces, chunk_select[number], chunk_masks[number], mine[None], results[0][0],
            expert_both_weight, expert_down_weight, results[0][1],
        )
        arrived.append([piece.reshape(-1, model_width) for piece in pieces])
        saved.append(values[:7])
        return list(values[7:])

    def backward_chunk(number, pieces, results):
        gates, expert_in, expert_gu, expert_act, expert_out, shared_gu, shared_act = saved[number]
        values = expert_backward(
            pieces, chunk_select[number], gates, expert_gu, expert_out, shared_gu, shared_router,
            expert_both_weight, expert_down_weight, shared_rows,
        )
        grad_arrived.append([piece.reshape(-1, model_width) for piece in pieces])
        grads.append(values[:4])
        return list(values[4:])

    arrived, saved, grad_arrived, grads = [], [], [], []
    routed, results = passes(
        normed2,
        forward_chunk,
        lambda step, behind, results: (shared_router, shared_rows, chunk_select, chunk_masks)
        if step == 0
        else None,
    )
    shared_router, shared_rows = results[0][:2]
    output = hidden + routed
    misfit = output - teacher[0].astype(F32)
    misfit_low = misfit.astype(BF)

    def products(lefts, rights, behind, tall, wide=None):
        return sums_of_products([after(lefts[0], behind)] + lefts[1:], rights, tall, wide)

    def kept(lists, entry):
        return [values[entry] for values in lists]

    def joined(lists):
        return [piece for pieces in lists for piece in pieces]

    def weight_grads(step, behind, results):
        if step == steps + 1:
            grad_gate = jnp.concatenate([values[0][:, 0] for values in grads], axis=0)
            grad_gate = jnp.take(
                after(grad_gate.reshape(experts, token_rows), behind),
                np.argsort(block_order), axis=0, mode="clip",
            )
            squares = jnp.broadcast_to(jnp.sum(misfit * misfit)[None, None], (experts, 128))
            notes = jnp.concatenate([jnp.take(grad_gate, order, axis=0, mode="clip"), squares], axis=1)
            notes = lax.all_to_all(notes, ("z", "r"), split_axis=0, concat_axis=0, tiled=True)
            return (
                products(joined(arrived), kept(grads, 3), behind, 512),
                products(kept(saved, 6), joined(grad_arrived), behind, padded, 512),
                notes,
            )
        if step == steps + 2:
            return products(kept(saved, 3), kept(grads, 1), behind, FFE, 512)
        return None

    grad_returned, results = passes(misfit_low, backward_chunk, weight_grads)
    (*grad_shared, notes), grad_expert_down = results
    grad_shared_both = jnp.concatenate(
        [grad_shared[0][:, :shared_units], grad_shared[0][:, padded : padded + shared_units]], axis=1
    )
    grad_shared_down = grad_shared[1][:shared_units]
    grad_expert_down = lax.psum_scatter(
        grad_expert_down[None], "fsdp", scatter_dimension=2, tiled=True
    )
    grad_shared_down = lax.psum_scatter(
        grad_shared_down, "fsdp", scatter_dimension=0, tiled=True
    )
    grad_shared_both = lax.psum_scatter(
        grad_shared_both, "fsdp", scatter_dimension=0, tiled=True
    )
    grad_shared_both = lax.all_to_all(
        grad_shared_both.astype(BF).reshape(experts, weight_rows, 2 * shared_units),
        ("z", "r"),
        split_axis=0,
        concat_axis=0,
        tiled=True,
    )

    grad_gates = notes[:, :token_rows].T
    all_squares = jnp.sum(notes[:, token_rows])[None]
    all_squares = all_squares + hop(jnp.broadcast_to(all_squares, (8, 128)), "fsdp", 1)[0, :1]
    loss_value = all_squares / (token_count.astype(F32) * model_width)
    grad_logits = (
        own_gates * (grad_gates - jnp.sum(own_gates * grad_gates, axis=1, keepdims=True))
    ).astype(BF)
    grad_normed2 = grad_returned + dot_last(grad_logits, router_weight)
    grad_hidden_norm, grad_gain_two = norm_back(hidden, gain_two_f, grad_normed2)
    grad_hidden = misfit + grad_hidden_norm
    near_grad = jnp.stack(gather_plane(grad_hidden.astype(BF)), axis=0)
    grad_expert_gate_up = products(kept(saved, 1), kept(grads, 2), grad_hidden, 256)
    near_grad, grad_expert_gate_up, grad_shared_both = stage(
        near_grad, grad_expert_gate_up, grad_shared_both
    )
    grad_expert_gate_up = lax.psum_scatter(
        grad_expert_gate_up[None], "fsdp", scatter_dimension=1, tiled=True
    )
    away_grad = hop(near_grad, "fsdp", 1)
    flat = (PLANE * token_rows, model_width)
    grad_output_weight = sums_of_products(
        [sides[:, 0].reshape(flat[0], -1), sides[:, 1].reshape(flat[0], -1)],
        [near_grad.reshape(flat), away_grad.reshape(flat)],
        heads * DV,
        512,
    )
    grad_output_weight = by_column(grad_output_weight.reshape(depth, weight_rows, model_width))
    grad_output_weight, away_grad = stage(grad_output_weight, away_grad)
    grad_output_weight = sum_columns(grad_output_weight).astype(BF)
    grad_query_weight, grad_up, own_part, given_part = attend_back(
        near_grad, away_grad, output_weight, queries, key_rope, keyval, attention,
        normed, compressed, query_weight, up_weight, spread_cos, spread_sin,
    )
    grad_query_weight, grad_up, own_part, given_part, grad_output_weight = stage(
        grad_query_weight, grad_up, own_part, given_part, grad_output_weight
    )
    grad_output_weight = lax.ppermute(
        grad_output_weight, ("z", "r"), [(b, a) for a, b in shard_moves]
    )
    grad_packed = jnp.concatenate([grad_query_weight, grad_up.reshape(model_width, up_fold)], axis=1)
    grad_packed = grad_packed.reshape(cores, depth, PLANE * weight_rows, wide_q + up_fold)
    grad_packed = grad_packed.swapaxes(0, 1)
    given_part = hop(given_part, "fsdp", 1)
    own_part, given_part, grad_packed = stage(own_part, given_part, grad_packed)
    grad_packed = lax.all_to_all(grad_packed, "z", split_axis=0, concat_axis=0, tiled=True)
    normed_sum = scatter_sides(own_part, given_part)
    normed_sum, grad_output_weight = stage(normed_sum, grad_output_weight)
    latent_sum = normed_sum[:, model_width:]
    own_latent = latent[:token_rows]
    grad_latent_norm, grad_latent_gain = norm_back(
        own_latent[:, :KVR], latent_gain_f, latent_sum[:, :KVR]
    )
    grad_latent = jnp.concatenate(
        [
            grad_latent_norm,
            unrotate(latent_sum[:, KVR : KVR + DR], cosine[:token_rows], sine_table[:token_rows]),
        ],
        axis=1,
    ).astype(BF)
    own_normed = normed[:token_rows]
    grad_normed = normed_sum[:, :model_width] + dot_last(grad_latent, down_weight)
    grad_flat_norm, grad_gain_one = norm_back(own_rows, gain_one_f, grad_normed)
    grad_tokens = grad_hidden + grad_flat_norm
    grad_latent_gain = jnp.pad(
        grad_latent_gain.reshape(-1, latent_rows), ((0, 0), (0, weight_rows - latent_rows))
    ).reshape(model_width)
    base = KVR + DR + experts
    columns = jnp.arange(small_width, dtype=jnp.int32)[None, :]

    def widen(values, start):
        return jnp.pad(values, ((0, 0), (start, small_width - start - values.shape[1])))

    grad_small = (
        dot_first(own_normed, widen(grad_latent, 0))
        + dot_first(normed2, widen(grad_logits, KVR + DR))
        + jnp.where(columns == base, grad_gain_one[:, None], 0.0)
        + jnp.where(columns == base + 1, grad_gain_two[:, None], 0.0)
        + jnp.where(columns == base + 2, grad_latent_gain[:, None], 0.0)
    )
    grad_small = straight(grad_small.astype(BF)).reshape(devices, weight_rows, small_width)
    grad_small = jnp.take(grad_small, everywhere, axis=0, mode="clip")
    grad_small = grad_small.reshape(cores, depth, PLANE, weight_rows, small_width)
    grad_tail = grad_small[0].astype(F32) + hop(grad_small[1], "fsdp", 1).astype(F32)
    grad_tail, grad_packed, grad_output_weight = stage(
        straight(grad_tail.astype(BF)), grad_packed, grad_output_weight
    )
    grad_packed = jnp.sum(grad_packed.astype(F32), axis=0).astype(BF)
    grad_output_weight = grad_output_weight.astype(F32)
    grad_shared_gate_up = (
        after(grad_shared_both, grad_tail)
        .reshape(experts, weight_rows, 2 * cores, unit)
        .transpose(1, 2, 0, 3)
        .reshape(weight_rows, 2 * FFS)
        .astype(F32)
    )
    grad_packed = lax.all_to_all(
        grad_packed.reshape(group, weight_rows, wide_q + up_fold),
        ("fsdp", "r"),
        split_axis=0,
        concat_axis=0,
        tiled=True,
    )
    grad_small = scatter_plane([grad_tail[:, j] for j in range(PLANE)])
    grad_small, grad_packed = stage(grad_small, grad_packed)
    grad_packed = grad_packed.swapaxes(0, 1)
    grad_small = grad_small[0] + sum(
        hop(grad_small[k].astype(BF), "z", k).astype(F32) for k in range(1, depth)
    )
    grad_q_weight = jnp.concatenate(
        [
            grad_packed[:, :, : heads * DN].reshape(weight_rows, group, heads, DN),
            grad_packed[:, :, heads * DN : wide_q].reshape(weight_rows, group, heads, DR),
        ],
        axis=3,
    )
    grad_q_weight = grad_q_weight.reshape(weight_rows, -1).astype(F32)
    grad_kv_up = (
        grad_packed[:, :, wide_q:]
        .reshape(latent_rows, fold, group, up_fold)
        .swapaxes(1, 2)
        .reshape(latent_rows, -1)
        .astype(F32)
    )
    return (
        output.astype(BF)[None],
        loss_value,
        grad_tokens[None],
        grad_small[:, base],
        grad_q_weight,
        grad_small[:, : KVR + DR],
        grad_small[:latent_rows, base + 2],
        grad_kv_up,
        grad_output_weight,
        grad_small[:, base + 1],
        grad_small[:, KVR + DR : base],
        grad_shared_gate_up,
        grad_shared_down,
        grad_expert_gate_up,
        grad_expert_down,
    )


def solution(mesh):
    cores = mesh.shape["fsdp"]
    experts = mesh.shape["expert"]
    grid = Mesh(mesh.devices.reshape(cores, experts // PLANE, PLANE), ("fsdp", "z", "r"))
    expert = ("z", "r")
    every = ("fsdp", "z", "r")
    return jax.shard_map(
        on_device,
        mesh=grid,
        in_specs=(
            P(expert, "fsdp", None),
            P(every),
            P(every, None),
            P(every, None),
            P(every),
            P(every, None),
            P(every, None),
            P(every),
            P(every, None),
            P(every, None),
            P(every, None),
            P(expert, "fsdp", None),
            P(expert, None, "fsdp"),
            P(expert, "fsdp", None),
            P(expert, "fsdp", None),
            P(expert),
            P(),
        ),
        out_specs=(
            P(expert, "fsdp", None),
            P(),
            P(expert, "fsdp", None),
            P(every),
            P(every, None),
            P(every, None),
            P(every),
            P(every, None),
            P(every, None),
            P(every),
            P(every, None),
            P(every, None),
            P(every, None),
            P(expert, "fsdp", None),
            P(expert, None, "fsdp"),
        ),
        check_vma=False,
    )
```

```python
import math

import jax
import jax.numpy as jnp
import numpy as np
from jax import lax
from jax.experimental import pallas as pl
from jax.experimental.layout import Layout, with_layout_constraint
from jax.experimental.pallas import tpu as pltpu
from jax.sharding import Mesh
from jax.sharding import PartitionSpec as P

NH = 16
DN = 128
DR = 64
DV = 128
KVR = 512
FFE = 1408
FFS = 2816
TOP = 6
PLANE = 4

BF = jnp.bfloat16
F32 = jnp.float32

epsilon = 1e-06


def rms_norm(values, gain_row):
    return (
        values * lax.rsqrt(jnp.mean(values * values, axis=-1, keepdims=True) + epsilon) * gain_row
    )


def norm_back(values, gain_row, incoming):
    factor = lax.rsqrt(jnp.mean(values * values, axis=-1, keepdims=True) + epsilon)
    scaled = incoming * gain_row
    grad_values = factor * scaled - values * (factor * factor * factor) * jnp.mean(
        scaled * values, axis=-1, keepdims=True
    )
    grad_gain = jnp.sum(incoming * values * factor, axis=0)
    return (grad_values, grad_gain)


def tables(position, rot_width):
    half_width = rot_width // 2
    frequency = 10000.0 ** (-2.0 * jnp.arange(half_width, dtype=F32) / rot_width)
    angles = position.astype(F32)[:, None] * frequency[None, :]
    return (jnp.cos(angles), jnp.sin(angles))


def unrotate(values, cosine, sine_table):
    half_width = values.shape[-1] // 2
    first_half = values[..., :half_width]
    second = values[..., half_width:]
    return jnp.concatenate(
        [first_half * cosine + second * sine_table, second * cosine - first_half * sine_table],
        axis=-1,
    )


def dot_plain(left_side, right_side):
    return jnp.dot(left_side, right_side, preferred_element_type=F32)


def dot_last(left_side, right_side):
    return lax.dot_general(
        left_side, right_side, (((1,), (1,)), ((), ())), preferred_element_type=F32
    )


def dot_first(left_side, right_side):
    return lax.dot_general(
        left_side, right_side, (((0,), (0,)), ((), ())), preferred_element_type=F32
    )


def straight(values):
    return with_layout_constraint(values, Layout(tuple(range(values.ndim))))


def after(values, *others):
    return lax.optimization_barrier((values,) + others)[0]


def stage(*values):
    return lax.optimization_barrier(values)


def hop(values, axis, distance):
    size = lax.axis_size(axis)
    moves = [(i, i ^ distance) for i in range(size)]
    return straight(lax.ppermute(straight(values), axis, moves))


def gather_plane(values):
    return [values] + [hop(values, "r", j) for j in range(1, PLANE)]


def scatter_plane(parts):
    moved = [hop(parts[j].astype(BF), "r", j) for j in range(1, PLANE)]
    return parts[0].astype(F32) + sum(part.astype(F32) for part in moved)


def scatter_sides(own, given):
    total = straight((own.astype(F32) + given.astype(F32)).astype(BF))
    return scatter_plane([total[j] for j in range(PLANE)])


def column_order(axis):
    return jnp.arange(lax.axis_size(axis), dtype=jnp.int32) ^ lax.axis_index(axis)


def both_cores(values):
    other = hop(values, "fsdp", 1)
    first = lax.axis_index("fsdp") == 0
    return jnp.concatenate(
        [jnp.where(first, values, other), jnp.where(first, other, values)], axis=0
    )


def by_column(parts):
    return jnp.take(parts.astype(BF), column_order("z"), axis=0, mode="clip")


def sum_columns(parts):
    moved = [hop(parts[k], "z", k) for k in range(1, lax.axis_size("z"))]
    return parts[0].astype(F32) + sum(part.astype(F32) for part in moved)


def gather_columns(values):
    spread = jnp.broadcast_to(values[None], (lax.axis_size("z"),) + values.shape)
    return lax.all_to_all(spread, "z", split_axis=0, concat_axis=0, tiled=True)


def gather_columns_apart(values):
    column = [values] + [hop(values, "z", k) for k in range(1, lax.axis_size("z"))]
    return jnp.take(jnp.stack(column, axis=0), column_order("z"), axis=0, mode="clip")


def all_order():
    return (column_order("z")[:, None] * PLANE + column_order("r")[None, :]).reshape(-1)


def swap_plane(parts):
    shape = parts.shape[1:]
    parts = jnp.take(parts, all_order(), axis=0, mode="clip")
    parts = parts.reshape((lax.axis_size("z"), PLANE) + shape)
    plane = [parts[:, 0]] + [hop(parts[:, j], "r", j) for j in range(1, PLANE)]
    return jnp.stack(plane, axis=1)


def swap_column(plane):
    depth = lax.axis_size("z")
    column = [plane[0]] + [hop(plane[k], "z", k) for k in range(1, depth)]
    column = jnp.stack(column, axis=0).reshape((depth * PLANE,) + plane.shape[2:])
    return jnp.take(column, all_order(), axis=0, mode="clip")


ROOM = 56 * 1024 * 1024


def whole(array):
    return pl.BlockSpec(array.shape, lambda *_: (0,) * array.ndim)


def sums_of_products(lefts, rights, tall, wide=None, kind=F32):
    height, width = lefts[0].shape[1], rights[0].shape[1]
    depth = sum(left.shape[0] for left in lefts)
    wide = width if wide is None else wide

    def stack(refs, into):
        start = 0
        for ref in refs:
            into[start : start + ref.shape[0], :] = ref[...]
            start += ref.shape[0]

    def body(*refs):
        out_ref, left_ref, right_ref = refs[-3:]

        @pl.when(pl.program_id(1) == 0)
        def _():
            stack(refs[len(lefts) : len(lefts) + len(rights)], right_ref)

        stack(refs[: len(lefts)], left_ref)
        out_ref[...] = dot_first(left_ref[...], right_ref[...]).astype(kind)

    return pl.pallas_call(
        body,
        grid=(width // wide, height // tall),
        in_specs=[pl.BlockSpec((left.shape[0], tall), lambda j, i: (0, i)) for left in lefts]
        + [pl.BlockSpec((right.shape[0], wide), lambda j, i: (0, j)) for right in rights],
        out_specs=pl.BlockSpec((tall, wide), lambda j, i: (i, j)),
        out_shape=jax.ShapeDtypeStruct((height, width), kind),
        scratch_shapes=[pltpu.VMEM((depth, tall), BF), pltpu.VMEM((depth, wide), BF)],
        compiler_params=pltpu.CompilerParams(vmem_limit_bytes=ROOM),
        cost_estimate=pl.CostEstimate(
            flops=2 * depth * height * width,
            bytes_accessed=2 * depth * (height + width) + 4 * height * width,
            transcendentals=0,
        ),
    )(*lefts, *rights)


def swiglu_parts(gate, up, incoming):
    sigmoid = jax.nn.sigmoid(gate)
    return (
        (incoming * up * sigmoid * (1.0 + gate * (1.0 - sigmoid))).astype(BF),
        (incoming * gate * sigmoid).astype(BF),
    )


TILE = 256
STRIP = 512
PARTS = 4


def spans(size, width):
    return [slice(start, min(start + width, size)) for start in range(0, size, width)]


class Copies:
    def __init__(self, semaphores):
        self.semaphores = semaphores
        self.used = 0

    def start(self, source, target):
        copy = pltpu.make_async_copy(source, target, self.semaphores.at[self.used])
        self.used += 1
        copy.start()
        return [copy]

    def start_rows(self, source, target):
        rows = source.shape[0]
        step = rows // PARTS
        copies = []
        for part in range(PARTS):
            span = pl.ds(part * step, step)
            copies += self.start(source.at[span, :], target.at[span, :])
        return copies


def wait(copies):
    for copy in copies:
        copy.wait()


def expert_forward(pieces, chosen, masks, mine, shared_router, both, down, shared_down):
    planes, rows, width = pieces[0].shape
    blocks, capacity = chosen.shape[:2]
    slots, flat_rows = blocks * capacity, blocks * rows
    hidden, units, experts = down.shape[0], shared_down.shape[0], mine.shape[1]
    strips = spans(width, STRIP)
    shapes = [
        ((slots, width), BF), ((slots, 2 * hidden), BF), ((slots, hidden), BF), ((slots, width), BF),
        ((flat_rows, 2 * units), BF), ((flat_rows, units), BF),
    ] + [((planes, rows, width), F32 if j == 0 else BF) for j in range(PLANE)]
    gate_shape = jax.ShapeDtypeStruct((flat_rows, 128), F32)

    def body(
        chosen_ref, masks_ref, mine_ref, piece_0, piece_1, piece_2, piece_3, router_hbm, both_hbm,
        down_hbm, shared_down_hbm,
        gates_ref, in_hbm, gu_hbm, act_hbm, out_hbm, shared_gu_hbm, shared_act_hbm,
        total_0, total_1, total_2, total_3,
        rows_ref, router_ref, both_ref, down_ref, shared_down_ref,
        in_ref, gu_ref, act_ref, out_ref, shared_gu_ref, shared_act_ref,
        sum_0, sum_1, sum_2, sum_3, semaphores,
    ):
        copies = Copies(semaphores)
        totals, sums = (total_0, total_1, total_2, total_3), (sum_0, sum_1, sum_2, sum_3)
        coming = []
        for j, piece in enumerate((piece_0, piece_1, piece_2, piece_3)):
            for k in range(planes):
                target = rows_ref.at[pl.ds((j * planes + k) * rows, rows), :]
                coming.append(copies.start(piece.at[k], target))
        router_in = copies.start_rows(router_hbm, router_ref)
        both_in = copies.start_rows(both_hbm, both_ref)
        down_in = copies.start_rows(down_hbm, down_ref)
        down_in += copies.start(shared_down_hbm, shared_down_ref)
        for block in range(blocks):
            wait(coming[block])
            in_ref[block * capacity : (block + 1) * capacity, :] = dot_plain(
                chosen_ref[block], rows_ref[block * rows : (block + 1) * rows, :]
            ).astype(BF)
        leaving = copies.start(in_ref, in_hbm)
        wait(router_in)
        joined = dot_plain(rows_ref[...], router_ref[...])
        gate, up = joined[:, :units], joined[:, units : 2 * units]
        shared_gu_ref[...] = joined[:, : 2 * units].astype(BF)
        shared_act_ref[...] = (gate * jax.nn.sigmoid(gate) * up).astype(BF)
        leaving += copies.start(shared_gu_ref, shared_gu_hbm)
        leaving += copies.start(shared_act_ref, shared_act_hbm)
        mask = masks_ref[...] > 0.0
        logits = jnp.where(mask, joined[:, 2 * units : 2 * units + experts], -1e30)
        odds = jnp.exp(logits - jnp.max(logits, axis=1, keepdims=True))
        odds = jnp.where(mask, odds, 0.0)
        own = jnp.sum(odds * mine_ref[...], axis=1, keepdims=True)
        own = own / jnp.sum(odds, axis=1, keepdims=True)
        gates_ref[...] = jnp.broadcast_to(own, gates_ref.shape)
        wait(both_in)
        for span in spans(hidden, TILE):
            above = slice(hidden + span.start, hidden + span.stop)
            gate = dot_plain(in_ref[...], both_ref[:, span])
            up = dot_plain(in_ref[...], both_ref[:, above])
            gu_ref[:, span] = gate.astype(BF)
            gu_ref[:, above] = up.astype(BF)
            act_ref[:, span] = (gate * jax.nn.sigmoid(gate) * up).astype(BF)
        leaving += copies.start(gu_ref, gu_hbm)
        leaving += copies.start(act_ref, act_hbm)
        wait(down_in)
        for strip in strips:
            out_ref[:, strip] = dot_plain(act_ref[...], down_ref[:, strip]).astype(BF)
            shared = dot_plain(shared_act_ref[...], shared_down_ref[:, strip])
            for j in range(PLANE):
                for k in range(planes):
                    block = j * planes + k
                    span = slice(block * rows, (block + 1) * rows)
                    picked = dot_first(
                        chosen_ref[block], out_ref[block * capacity : (block + 1) * capacity, strip]
                    )
                    sums[j][k, :, strip] = (gates_ref[span, 0:1] * picked + shared[span, :]).astype(
                        sums[j].dtype
                    )
                place = pl.ds(strip.start, strip.stop - strip.start)
                leaving += copies.start(sums[j].at[:, :, place], totals[j].at[:, :, place])
        leaving += copies.start(out_ref, out_hbm)
        wait(leaving)

    anywhere = pl.BlockSpec(memory_space=pl.ANY)
    moved = [shared_router, both, down, shared_down]
    scratch = [pltpu.VMEM((flat_rows, width), BF)]
    scratch += [pltpu.VMEM(array.shape, BF) for array in moved]
    scratch += [pltpu.VMEM(*shape) for shape in shapes]
    count = blocks + 3 * PARTS + 1 + 6 + PLANE * len(strips)
    return pl.pallas_call(
        body,
        in_specs=[pl.BlockSpec(memory_space=pltpu.VMEM)] * 3 + [anywhere] * (PLANE + len(moved)),
        out_specs=[pl.BlockSpec(memory_space=pltpu.VMEM)] + [anywhere] * len(shapes),
        out_shape=[gate_shape] + [jax.ShapeDtypeStruct(*shape) for shape in shapes],
        scratch_shapes=scratch + [pltpu.SemaphoreType.DMA((count,))],
        compiler_params=pltpu.CompilerParams(vmem_limit_bytes=ROOM),
        cost_estimate=pl.CostEstimate(
            flops=2 * width * (3 * slots * hidden + flat_rows * 4 * units),
            bytes_accessed=2 * width * (3 * hidden + 4 * units + 4 * flat_rows) + 12 * slots * hidden,
            transcendentals=slots * hidden,
        ),
    )(chosen, masks, mine, *pieces, *moved)


def expert_backward(pieces, chosen, gates, gu, out, shared_gu, shared_router, both, down, shared_down):
    planes, rows, width = pieces[0].shape
    blocks, capacity = chosen.shape[:2]
    slots, flat_rows = blocks * capacity, blocks * rows
    hidden, units = down.shape[0], shared_down.shape[0]
    strips = spans(width, STRIP)
    shapes = [
        ((slots, width), BF), ((slots, 2 * hidden), BF), ((flat_rows, 2 * units), BF),
    ] + [((planes, rows, width), F32 if j == 0 else BF) for j in range(PLANE)]
    gate_shape = jax.ShapeDtypeStruct((flat_rows, 128), F32)

    def body(
        chosen_ref, gates_ref, piece_0, piece_1, piece_2, piece_3, out_hbm, shared_gu_hbm, shared_down_hbm,
        gu_hbm, down_hbm, router_hbm, both_hbm,
        grad_gate_ref, slots_hbm, grad_gu_hbm, grad_shared_hbm, total_0, total_1, total_2, total_3,
        rows_ref, out_ref, shared_gu_ref, shared_down_ref, gu_ref, down_ref, router_ref, both_ref,
        slots_ref, grad_gu_ref, grad_shared_ref, sum_0, sum_1, sum_2, sum_3, semaphores,
    ):
        copies = Copies(semaphores)
        totals, sums = (total_0, total_1, total_2, total_3), (sum_0, sum_1, sum_2, sum_3)
        coming = []
        for j, piece in enumerate((piece_0, piece_1, piece_2, piece_3)):
            for k in range(planes):
                target = rows_ref.at[pl.ds((j * planes + k) * rows, rows), :]
                coming.append(copies.start(piece.at[k], target))
        out_in = copies.start_rows(out_hbm, out_ref)
        shared_in = copies.start(shared_gu_hbm, shared_gu_ref)
        shared_in += copies.start(shared_down_hbm, shared_down_ref)
        down_in = copies.start_rows(down_hbm, down_ref)
        down_in += copies.start(gu_hbm, gu_ref)
        both_in = copies.start_rows(both_hbm, both_ref)
        both_in += copies.start_rows(router_hbm, router_ref)
        wait(out_in)
        for block in range(blocks):
            wait(coming[block])
            span = slice(block * rows, (block + 1) * rows)
            part = slice(block * capacity, (block + 1) * capacity)
            values = rows_ref[span, :].astype(F32)
            slots_ref[part, :] = dot_plain(
                chosen_ref[block], (gates_ref[span, 0:1] * values).astype(BF)
            ).astype(BF)
            picked = dot_first(chosen_ref[block], out_ref[part, :])
            own = jnp.sum(values * picked, axis=1, keepdims=True)
            grad_gate_ref[span, :] = jnp.broadcast_to(own, (rows, 128))
        leaving = copies.start(slots_ref, slots_hbm)
        wait(shared_in)
        grad_gate, grad_up = swiglu_parts(
            shared_gu_ref[:, :units].astype(F32),
            shared_gu_ref[:, units:].astype(F32),
            dot_last(rows_ref[...], shared_down_ref[...]),
        )
        grad_shared_ref[:, :units] = grad_gate
        grad_shared_ref[:, units:] = grad_up
        leaving += copies.start(grad_shared_ref, grad_shared_hbm)
        wait(down_in)
        for span in spans(hidden, TILE):
            above = slice(hidden + span.start, hidden + span.stop)
            grad_gate, grad_up = swiglu_parts(
                gu_ref[:, span].astype(F32),
                gu_ref[:, above].astype(F32),
                dot_last(slots_ref[...], down_ref[span, :]),
            )
            grad_gu_ref[:, span] = grad_gate
            grad_gu_ref[:, above] = grad_up
        leaving += copies.start(grad_gu_ref, grad_gu_hbm)
        wait(both_in)
        for strip in strips:
            grad_in = dot_last(grad_gu_ref[...], both_ref[strip, :]).astype(BF)
            shared = dot_last(grad_shared_ref[...], router_ref[strip, : 2 * units])
            for j in range(PLANE):
                for k in range(planes):
                    block = j * planes + k
                    moved = dot_first(
                        chosen_ref[block], grad_in[block * capacity : (block + 1) * capacity, :]
                    )
                    sums[j][k, :, strip] = (moved + shared[block * rows : (block + 1) * rows, :]).astype(
                        sums[j].dtype
                    )
                place = pl.ds(strip.start, strip.stop - strip.start)
                leaving += copies.start(sums[j].at[:, :, place], totals[j].at[:, :, place])
        wait(leaving)

    anywhere = pl.BlockSpec(memory_space=pl.ANY)
    moved = [out, shared_gu, shared_down, gu, down, shared_router, both]
    scratch = [pltpu.VMEM((flat_rows, width), BF)]
    scratch += [pltpu.VMEM(array.shape, BF) for array in moved]
    scratch += [pltpu.VMEM(*shape) for shape in shapes]
    count = blocks + 4 * PARTS + 3 + 3 + PLANE * len(strips)
    return pl.pallas_call(
        body,
        in_specs=[pl.BlockSpec(memory_space=pltpu.VMEM)] * 2 + [anywhere] * (PLANE + len(moved)),
        out_specs=[pl.BlockSpec(memory_space=pltpu.VMEM)] + [anywhere] * len(shapes),
        out_shape=[gate_shape] + [jax.ShapeDtypeStruct(*shape) for shape in shapes],
        scratch_shapes=scratch + [pltpu.SemaphoreType.DMA((count,))],
        compiler_params=pltpu.CompilerParams(vmem_limit_bytes=ROOM),
        cost_estimate=pl.CostEstimate(
            flops=2 * width * (3 * slots * hidden + flat_rows * 4 * units),
            bytes_accessed=2 * width * (3 * hidden + 4 * units + 6 * flat_rows) + 12 * slots * hidden,
            transcendentals=slots * hidden,
        ),
    )(chosen, gates, *pieces, *moved)


def turn(values, cosine, sine_table):
    lane = lax.broadcasted_iota(jnp.int32, values.shape, 1)
    wide = values.shape[1]
    swapped = jnp.where(
        lane % DR < DR // 2,
        pltpu.roll(values, wide - DR // 2, 1),
        pltpu.roll(values, DR // 2, 1),
    )
    return values * cosine + swapped * sine_table


def head_lanes(values, head):
    lane = lax.broadcasted_iota(jnp.int32, values.shape, 1)
    return jnp.where(lane // DR == head, values, jnp.zeros_like(values))


def attend(near, away, gain, down, latent_gain, query, up, heads, cosine, sine_table, place, places, early):
    sequences, rows, width = near.shape
    length = 2 * rows
    nope = heads * DN
    span = KVR + 2 * DR
    scaling = (DN + DR) ** (-0.5)

    def body(
        near_ref, away_ref, gain_ref, down_ref, latent_gain_ref, query_ref, up_ref, cos_ref, sin_ref, place_ref, places_ref, early_ref,
        normed_ref, latent_ref, compressed_ref, queries_ref, rope_ref, keyval_ref,
        attention_ref, context_ref,
    ):
        for side, ref in enumerate((near_ref, away_ref)):
            values = ref[0].astype(F32)
            normed_ref[side * rows : (side + 1) * rows, :] = rms_norm(values, gain_ref[...]).astype(BF)
        normed = normed_ref[...]
        latent = dot_plain(normed, down_ref[:, :span])
        latent_ref[...] = latent
        compressed = rms_norm(latent[:, :KVR], latent_gain_ref[...]).astype(BF)
        compressed_ref[...] = compressed
        key_rope = head_lanes(turn(latent[:, KVR:], cos_ref[...], sin_ref[...]), 0)
        key_rope = (key_rope + pltpu.roll(key_rope, DR, 1)).astype(BF)
        rope_ref[...] = key_rope
        query_raw = dot_plain(normed, query_ref[...])
        queries_ref[:, :nope] = query_raw[:, :nope].astype(BF)
        query_rope = turn(query_raw[:, nope:], cos_ref[...], sin_ref[...]).astype(BF)
        queries_ref[:, nope:] = query_rope
        keyval_ref[...] = dot_plain(compressed, up_ref[...]).astype(BF)
        visible = (places_ref[0:1, :] <= place_ref[:, 0:1]) | (early_ref[0, 0:1, :] > 0.0)
        for head in range(heads):
            start = head * (DN + DV)
            scores = dot_last(
                queries_ref[:, head * DN : (head + 1) * DN], keyval_ref[:, start : start + DN]
            ) + dot_last(head_lanes(query_rope, head), key_rope)
            scores = jnp.where(visible, scores * scaling, -1e30)
            weights = jnp.exp(scores - jnp.max(scores, axis=1, keepdims=True))
            attention = weights / jnp.sum(weights, axis=1, keepdims=True)
            attention_ref[0, head] = attention
            context_ref[:, head * DV : (head + 1) * DV] = dot_plain(
                attention.astype(BF), keyval_ref[:, start + DN : start + DN + DV]
            ).astype(BF)

    def by_rows(columns):
        return pl.BlockSpec((length, columns), lambda s: (s, 0))

    def halves():
        return pl.BlockSpec((1, rows, width), lambda s: (s, 0, 0))

    every = sequences * length
    fixed = (gain, down, latent_gain, query, up, cosine, sine_table, place, places)
    columns = (width, span, KVR, query.shape[1], 2 * DR, up.shape[1])
    kinds = (BF, F32, BF, BF, BF, BF)
    return pl.pallas_call(
        body,
        grid=(sequences,),
        in_specs=[halves(), halves()]
        + [whole(array) for array in fixed]
        + [pl.BlockSpec((1,) + early.shape[1:], lambda s: (s, 0, 0))],
        out_specs=[by_rows(c) for c in columns]
        + [
            pl.BlockSpec((1, heads, length, length), lambda s: (s, 0, 0, 0)),
            by_rows(heads * DV),
        ],
        out_shape=[jax.ShapeDtypeStruct((every, c), k) for c, k in zip(columns, kinds)]
        + [
            jax.ShapeDtypeStruct((sequences, heads, length, length), F32),
            jax.ShapeDtypeStruct((every, heads * DV), BF),
        ],
        compiler_params=pltpu.CompilerParams(vmem_limit_bytes=ROOM),
        cost_estimate=pl.CostEstimate(
            flops=2 * every * (width * (span + query.shape[1]) + KVR * up.shape[1]),
            bytes_accessed=32 * 1024 * 1024,
            transcendentals=every * length * heads,
        ),
    )(near, away, *fixed, early)


def attend_back(
    near, away, out, queries, rope, keyval, attention, normed, compressed, query, up, cosine, sine_table
):
    sequences, rows, width = near.shape
    length = 2 * rows
    heads = out.shape[0] // DV
    nope = heads * DN
    span = KVR + 2 * DR
    scaling = (DN + DR) ** (-0.5)

    def body(
        near_ref, away_ref, queries_ref, rope_ref, keyval_ref, attention_ref,
        normed_ref, compressed_ref, out_ref, query_ref, up_ref, cos_ref, sin_ref,
        grad_query_out, grad_up_out, own_ref, given_ref,
        grad_query_ref, grad_up_ref, incoming_ref, columns_ref, pairs_ref,
    ):
        @pl.when(pl.program_id(0) == 0)
        def _():
            grad_query_ref[...] = jnp.zeros_like(grad_query_ref)
            grad_up_ref[...] = jnp.zeros_like(grad_up_ref)

        incoming_ref[:rows, :] = near_ref[0]
        incoming_ref[rows:, :] = away_ref[0]
        incoming = incoming_ref[...]
        grad_context = dot_last(incoming, out_ref[...]).astype(BF)
        key_rope = rope_ref[...]
        query_rope = queries_ref[:, nope:]
        grad_query_rope = jnp.zeros((length, 2 * DR), F32)
        grad_key_rope = jnp.zeros((length, 2 * DR), F32)
        for head in range(heads):
            start = head * (DN + DV)
            attention = attention_ref[0, head]
            grad_head = grad_context[:, head * DV : (head + 1) * DV]
            grad_attention = dot_last(grad_head, keyval_ref[:, start + DN : start + DN + DV])
            grad_scores = attention * (
                grad_attention - jnp.sum(attention * grad_attention, axis=1, keepdims=True)
            )
            grad_scores = grad_scores.astype(BF)
            columns_ref[:, head * DN : (head + 1) * DN] = (
                dot_plain(grad_scores, keyval_ref[:, start : start + DN]) * scaling
            ).astype(BF)
            grad_query_rope += head_lanes(dot_plain(grad_scores, key_rope) * scaling, head)
            pairs_ref[:, start : start + DN] = (
                dot_first(grad_scores, queries_ref[:, head * DN : (head + 1) * DN]) * scaling
            ).astype(BF)
            pairs_ref[:, start + DN : start + DN + DV] = dot_first(
                attention.astype(BF), grad_head
            ).astype(BF)
            grad_key_rope += dot_first(grad_scores, head_lanes(query_rope, head)) * scaling
        columns_ref[:, nope:] = turn(grad_query_rope, cos_ref[...], -sin_ref[...]).astype(BF)
        grad_key_rope += pltpu.roll(grad_key_rope, DR, 1)
        columns = columns_ref[...]
        pairs = pairs_ref[...]
        grad_query_ref[...] += dot_first(normed_ref[...], columns)
        grad_up_ref[...] += dot_first(compressed_ref[...], pairs)
        latent = dot_last(pairs, up_ref[...])
        total = dot_last(columns, query_ref[...])
        own_ref[0, :, :width] = total[:rows].astype(BF)
        given_ref[0, :, :width] = total[rows:].astype(BF)
        own_ref[0, :, width : width + KVR] = latent[:rows].astype(BF)
        given_ref[0, :, width : width + KVR] = latent[rows:].astype(BF)
        own_ref[0, :, width + KVR :] = grad_key_rope[:rows].astype(BF)

        @pl.when(pl.program_id(0) == sequences - 1)
        def _():
            grad_query_out[...] = grad_query_ref[...].astype(BF)
            grad_up_out[...] = grad_up_ref[...].astype(BF)

        given_ref[0, :, width + KVR :] = grad_key_rope[rows:].astype(BF)

    def by_rows(columns):
        return pl.BlockSpec((length, columns), lambda s: (s, 0))

    def halves(columns):
        return pl.BlockSpec((1, rows, columns), lambda s: (s, 0, 0))

    every = sequences * length
    moving = (queries, rope, keyval)
    fixed = (out, query, up, cosine, sine_table)
    shapes = (
        (query.shape, BF), (up.shape, BF),
        ((sequences, rows, width + span), BF), ((sequences, rows, width + span), BF),
    )
    return pl.pallas_call(
        body,
        grid=(sequences,),
        in_specs=[halves(width), halves(width)]
        + [by_rows(array.shape[1]) for array in moving]
        + [pl.BlockSpec((1, heads, length, length), lambda s: (s, 0, 0, 0))]
        + [by_rows(normed.shape[1]), by_rows(compressed.shape[1])]
        + [whole(array) for array in fixed],
        out_specs=[whole(query), whole(up)]
        + [halves(width + span), halves(width + span)],
        out_shape=[jax.ShapeDtypeStruct(shape, kind) for shape, kind in shapes],
        scratch_shapes=[
            pltpu.VMEM(query.shape, F32),
            pltpu.VMEM(up.shape, F32),
            pltpu.VMEM((length, width), BF),
            pltpu.VMEM((length, query.shape[1]), BF),
            pltpu.VMEM((length, up.shape[1]), BF),
        ],
        compiler_params=pltpu.CompilerParams(vmem_limit_bytes=ROOM),
        cost_estimate=pl.CostEstimate(
            flops=4 * every * (width * (query.shape[1] + heads * DV) + KVR * up.shape[1]),
            bytes_accessed=48 * 1024 * 1024,
            transcendentals=0,
        ),
    )(near, away, *moving, attention, normed, compressed, *fixed)


def on_device(
    tokens,
    norm1_gain,
    q_weight,
    kv_down,
    latent_gain,
    kv_up,
    o_weight,
    norm2_gain,
    router,
    shared_gate_up,
    shared_down,
    expert_gate_up,
    expert_down,
    teacher,
    routes,
    prefix,
    token_count,
):
    cores = lax.axis_size("fsdp")
    depth = lax.axis_size("z")
    experts = depth * PLANE
    group = cores * PLANE
    heads = NH // group
    core = lax.axis_index("fsdp")
    plane_index = lax.axis_index("z")
    spot = lax.axis_index("r")
    own_expert = plane_index * PLANE + spot
    token_rows = tokens.shape[1]
    model_width = tokens.shape[2]
    seq_length = token_rows * cores
    capacity = -(-max(2, token_rows * TOP * 5 // (experts * 3)) // 16) * 16
    weight_rows = q_weight.shape[0]
    latent_rows = kv_up.shape[0]
    wide_q = heads * (DN + DR)
    wide_kv = heads * (DN + DV)
    scaling = (DN + DR) ** (-0.5)
    devices = cores * experts
    every = PLANE * seq_length
    everywhere = jnp.arange(devices, dtype=jnp.int32) ^ (core * experts + own_expert)

    sub = depth // PLANE
    shard_moves = [
        (z * PLANE + r, ((z % sub) * PLANE + r) * PLANE + z // sub)
        for z in range(depth)
        for r in range(PLANE)
    ]

    moved_o = lax.ppermute(o_weight, ("z", "r"), shard_moves)
    first_rows = tokens[0]

    fold = weight_rows // latent_rows
    up_fold = wide_kv // fold
    up_packed = kv_up.reshape(latent_rows, group, fold, up_fold)
    up_packed = up_packed.swapaxes(1, 2).reshape(weight_rows, group, up_fold)
    by_head = q_weight.reshape(weight_rows, group, heads, DN + DR)
    packed = jnp.concatenate(
        [
            by_head[..., :DN].reshape(weight_rows, group, heads * DN),
            by_head[..., DN:].reshape(weight_rows, group, heads * DR),
            up_packed,
        ],
        axis=2,
    )
    packed = lax.all_to_all(
        packed.swapaxes(0, 1), ("fsdp", "r"), split_axis=0, concat_axis=0, tiled=True
    )
    packed = packed.reshape(cores, PLANE * weight_rows, wide_q + up_fold)

    own_mask = jnp.any(
        routes[0][:, :, None] == jnp.arange(experts, dtype=jnp.int32)[None, None, :], axis=1
    )
    small = jnp.concatenate(
        [
            kv_down,
            router,
            norm1_gain[:, None],
            norm2_gain[:, None],
            jnp.pad(latent_gain, (0, weight_rows - latent_rows))[:, None],
            jnp.broadcast_to(prefix.astype(BF)[None, :], (weight_rows, 1)),
            own_mask.astype(BF).reshape(weight_rows, -1),
        ],
        axis=1,
    )
    small_width = -(-small.shape[1] // 128) * 128
    small = jnp.pad(small, ((0, 0), (0, small_width - small.shape[1])))
    small = jnp.stack([small] + [hop(small, "z", k) for k in range(1, depth)], axis=0)
    shared_both = shared_gate_up.reshape(weight_rows, 2 * cores, experts, shared_down.shape[0])
    shared_both = shared_both.transpose(2, 0, 1, 3).reshape(experts, weight_rows, -1)
    near_rows = jnp.stack(gather_plane(first_rows), axis=0)
    packed, small, near_rows, shared_both = stage(packed, small, near_rows, shared_both)
    packed = gather_columns(packed)
    away_rows = hop(near_rows, "fsdp", 1)
    small = jnp.stack(gather_plane(small), axis=1)
    small = jnp.stack([small, hop(small, "fsdp", 1)], axis=0)
    shared_both = swap_plane(after(shared_both, small))
    packed, shared_both, moved_o = stage(packed, shared_both, moved_o, small, away_rows)[:3]
    output_weight = gather_columns_apart(moved_o).reshape(heads * DV, model_width)
    small = small.reshape(devices, weight_rows, small_width)
    prefixes = small[:PLANE, 0, KVR + DR + experts + 3].astype(F32)
    masks = small[:experts, :, KVR + DR + experts + 4 :][:, :, : token_rows * experts // weight_rows]
    masks = masks.astype(F32).reshape(experts, token_rows, experts)
    small = jnp.take(small, everywhere, axis=0, mode="clip").reshape(model_width, small_width)
    down_weight = small[:, : KVR + DR]
    router_weight = small[:, KVR + DR : KVR + DR + experts]
    gains = small[:, KVR + DR + experts : KVR + DR + experts + 3].astype(F32).T
    gain_one_f = gains[0]
    gain_two_f = gains[1]
    latent_gain_f = gains[2].reshape(-1, weight_rows)[:, :latent_rows].reshape(KVR)

    half = jnp.arange(token_rows, dtype=jnp.int32)
    position = jnp.concatenate([core * token_rows + half, (1 - core) * token_rows + half])
    cosine, sine_table = tables(position, DR)
    spread_cos = jnp.tile(cosine, (1, 4))
    spread_sin = jnp.tile(jnp.concatenate([-sine_table, sine_table], axis=1), (1, 2))
    places = position.astype(F32)
    early = (places[None, :] < prefixes[:, None]).astype(F32)
    early = jnp.broadcast_to(early[:, None, :], (PLANE, 8, seq_length))
    packed = packed.swapaxes(0, 1).reshape(model_width, wide_q + up_fold)
    query_weight = packed[:, :wide_q]
    up_weight = packed[:, wide_q:].reshape(KVR, fold * up_fold)


    normed, latent, compressed, queries, key_rope, keyval, attention, context = attend(
        near_rows, away_rows, gain_one_f[None], small, latent_gain_f[None], query_weight,
        up_weight, heads, spread_cos, spread_sin,
        jnp.broadcast_to(places[:, None], (seq_length, 128)),
        jnp.broadcast_to(places[None, :], (8, seq_length)), early,
    )
    expert_both_weight = lax.all_gather(expert_gate_up, "fsdp", axis=1, tiled=True)[0]
    expert_down_weight = lax.all_gather(expert_down, "fsdp", axis=2, tiled=True)[0]
    unit = shared_down.shape[0]
    shared_units = cores * unit
    masks = after(masks, packed)
    order = jnp.arange(experts, dtype=jnp.int32) ^ own_expert
    mine = (jnp.arange(experts, dtype=jnp.int32) == own_expert).astype(F32)
    taken = jnp.sum(masks * mine[None, None, :], axis=2)
    rank = jnp.cumsum(taken, axis=1) - taken
    select = taken[:, None, :] * (
        rank[:, None, :] == jnp.arange(capacity, dtype=F32)[None, :, None]
    ).astype(F32)
    select_low = select.astype(BF)
    steps = depth
    lots = [[k] for k in range(depth)]
    lots = lots[:1] + lots[2:] + lots[1:2]
    block_order = np.array(
        [k * PLANE + j for planes in lots for j in range(PLANE) for k in planes], dtype=np.int32
    )
    chunk_select = jnp.take(select_low, block_order, axis=0, mode="clip")
    chunk_select = chunk_select.reshape(steps, PLANE, capacity, token_rows)
    chunk_masks = jnp.take(masks, block_order, axis=0, mode="clip")
    chunk_masks = chunk_masks.reshape(steps, PLANE * token_rows, experts)
    context, output_weight, chunk_select, chunk_masks = stage(
        context, output_weight, chunk_select, chunk_masks
    )
    sides = context.reshape(PLANE, cores, token_rows, heads * DV)

    def project(side):
        flat = sides[:, side].reshape(PLANE * token_rows, heads * DV)
        return dot_plain(flat, output_weight).reshape(PLANE, token_rows, model_width)

    given_part = hop(project(1).astype(BF), "fsdp", 1)
    own_part = project(0).astype(BF)
    shared_down_weight = both_cores(shared_down)
    own_part, given_part, shared_both, shared_down_weight = stage(
        own_part, given_part, shared_both, shared_down_weight
    )
    shared_both = swap_column(shared_both).reshape(experts * weight_rows, 2 * shared_units)
    own_rows = tokens[0].astype(F32)
    hidden = own_rows + scatter_sides(own_part, given_part)
    hidden, shared_both = stage(hidden, shared_both)
    shared_both_weight = both_cores(shared_both)
    normed2 = rms_norm(hidden, gain_two_f).astype(BF)

    def gates_of(logits, mask):
        logits = jnp.where(mask, logits, -1e30)
        odds = jnp.where(mask, jnp.exp(logits - jnp.max(logits, axis=-1, keepdims=True)), 0.0)
        return odds / jnp.sum(odds, axis=-1, keepdims=True)

    own_gates = gates_of(dot_plain(normed2, router_weight), own_mask)
    padded = -(-shared_units // 128) * 128

    def pad_columns(values, columns):
        return jnp.pad(values, ((0, 0), (0, columns - values.shape[1])))

    shared_router = jnp.concatenate(
        [
            pad_columns(shared_both_weight[:, :shared_units], padded),
            pad_columns(shared_both_weight[:, shared_units:], padded),
            pad_columns(router_weight, -(-experts // 128) * 128),
        ],
        axis=1,
    )
    shared_rows = jnp.pad(shared_down_weight, ((0, padded - shared_units), (0, 0)))

    def passes(values, compute, besides):
        def fetch(values, number):
            return jnp.stack([hop(values, "z", k) if k else values for k in lots[number]], axis=0)

        source, pieces, totals, summed = fetch(values, 0), None, None, None
        returned, results = [], []
        for step in range(steps + 3):
            later = [values, None, None, None, None, None]
            if step + 1 < steps:
                later[1] = fetch(values, step + 1)
            if pieces is not None:
                later[3] = compute(step - 1, pieces, results)
            if source is not None and totals is not None:
                count, half = source.shape[0], source.shape[1] // 2
                along, across = [
                    hop(jnp.concatenate([source, totals[j]], axis=0), "r", j) for j in (1, 2)
                ]
                opposite = hop(totals[3], "r", 3)
                behind = later[3][1]
                far = jnp.concatenate(
                    [
                        hop(after(along[:count, :half], behind), "r", 2),
                        hop(after(across[:count, half:], behind), "r", 1),
                    ],
                    axis=1,
                )
                later[2] = [source, along[:count], across[:count], far]
                later[4] = totals[0] + sum(
                    part.astype(F32) for part in (along[count:], across[count:], opposite)
                )
            elif source is not None:
                later[2] = gather_plane(source)
            elif totals is not None:
                later[4] = scatter_plane(totals)
            if summed is not None:
                later[5] = [
                    hop(summed[i].astype(BF), "z", k) if k else summed[i]
                    for i, k in enumerate(lots[step - 3])
                ]
            later.append(besides(step, summed if totals is None else totals[0], results))
            values, source, pieces, totals, summed, back, beside = lax.optimization_barrier(later)
            if beside is not None:
                results.append(beside)
            if back is not None:
                returned += [part.astype(F32) for part in back]
        return sum(returned), results

    def forward_chunk(number, pieces, results):
        values = expert_forward(
            pieces, chunk_select[number], chunk_masks[number], mine[None], results[0][0],
            expert_both_weight, expert_down_weight, results[0][1],
        )
        arrived.append([piece.reshape(-1, model_width) for piece in pieces])
        saved.append(values[:7])
        return list(values[7:])

    def backward_chunk(number, pieces, results):
        gates, expert_in, expert_gu, expert_act, expert_out, shared_gu, shared_act = saved[number]
        values = expert_backward(
            pieces, chunk_select[number], gates, expert_gu, expert_out, shared_gu, shared_router,
            expert_both_weight, expert_down_weight, shared_rows,
        )
        grad_arrived.append([piece.reshape(-1, model_width) for piece in pieces])
        grads.append(values[:4])
        return list(values[4:])

    arrived, saved, grad_arrived, grads = [], [], [], []
    routed, results = passes(
        normed2,
        forward_chunk,
        lambda step, behind, results: (shared_router, shared_rows, chunk_select, chunk_masks)
        if step == 0
        else None,
    )
    shared_router, shared_rows = results[0][:2]
    output = hidden + routed
    misfit = output - teacher[0].astype(F32)
    misfit_low = misfit.astype(BF)

    def products(lefts, rights, behind, tall, wide=None):
        return sums_of_products([after(lefts[0], behind)] + lefts[1:], rights, tall, wide)

    def kept(lists, entry):
        return [values[entry] for values in lists]

    def joined(lists):
        return [piece for pieces in lists for piece in pieces]

    def weight_grads(step, behind, results):
        if step == steps + 1:
            grad_gate = jnp.concatenate([values[0][:, 0] for values in grads], axis=0)
            grad_gate = jnp.take(
                after(grad_gate.reshape(experts, token_rows), behind),
                np.argsort(block_order), axis=0, mode="clip",
            )
            squares = jnp.broadcast_to(jnp.sum(misfit * misfit)[None, None], (experts, 128))
            notes = jnp.concatenate([jnp.take(grad_gate, order, axis=0, mode="clip"), squares], axis=1)
            notes = lax.all_to_all(notes, ("z", "r"), split_axis=0, concat_axis=0, tiled=True)
            return (
                products(joined(arrived), kept(grads, 3), behind, 512),
                products(kept(saved, 6), joined(grad_arrived), behind, padded, 512),
                notes,
            )
        if step == steps + 2:
            return products(kept(saved, 3), kept(grads, 1), behind, FFE, 512)
        return None

    grad_returned, results = passes(misfit_low, backward_chunk, weight_grads)
    (*grad_shared, notes), grad_expert_down = results
    grad_shared_both = jnp.concatenate(
        [grad_shared[0][:, :shared_units], grad_shared[0][:, padded : padded + shared_units]], axis=1
    )
    grad_shared_down = grad_shared[1][:shared_units]
    grad_expert_down = lax.psum_scatter(
        grad_expert_down[None], "fsdp", scatter_dimension=2, tiled=True
    )
    grad_shared_down = lax.psum_scatter(
        grad_shared_down, "fsdp", scatter_dimension=0, tiled=True
    )
    grad_shared_both = lax.psum_scatter(
        grad_shared_both, "fsdp", scatter_dimension=0, tiled=True
    )
    grad_shared_both = lax.all_to_all(
        grad_shared_both.astype(BF).reshape(experts, weight_rows, 2 * shared_units),
        ("z", "r"),
        split_axis=0,
        concat_axis=0,
        tiled=True,
    )

    grad_gates = notes[:, :token_rows].T
    all_squares = jnp.sum(notes[:, token_rows])[None]
    all_squares = all_squares + hop(jnp.broadcast_to(all_squares, (8, 128)), "fsdp", 1)[0, :1]
    loss_value = all_squares / (token_count.astype(F32) * model_width)
    grad_logits = (
        own_gates * (grad_gates - jnp.sum(own_gates * grad_gates, axis=1, keepdims=True))
    ).astype(BF)
    grad_normed2 = grad_returned + dot_last(grad_logits, router_weight)
    grad_hidden_norm, grad_gain_two = norm_back(hidden, gain_two_f, grad_normed2)
    grad_hidden = misfit + grad_hidden_norm
    near_grad = jnp.stack(gather_plane(grad_hidden.astype(BF)), axis=0)
    grad_expert_gate_up = products(kept(saved, 1), kept(grads, 2), grad_hidden, 256)
    near_grad, grad_expert_gate_up, grad_shared_both = stage(
        near_grad, grad_expert_gate_up, grad_shared_both
    )
    grad_expert_gate_up = lax.psum_scatter(
        grad_expert_gate_up[None], "fsdp", scatter_dimension=1, tiled=True
    )
    away_grad = hop(near_grad, "fsdp", 1)
    flat = (PLANE * token_rows, model_width)
    grad_output_weight = sums_of_products(
        [sides[:, 0].reshape(flat[0], -1), sides[:, 1].reshape(flat[0], -1)],
        [near_grad.reshape(flat), away_grad.reshape(flat)],
        heads * DV,
        512,
        BF,
    )
    grad_output_weight = by_column(grad_output_weight.reshape(depth, weight_rows, model_width))
    grad_router = dot_first(normed2, grad_logits)
    grad_output_weight, away_grad, grad_router = stage(grad_output_weight, away_grad, grad_router)
    grad_output_weight = sum_columns(grad_output_weight).astype(BF)
    grad_query_weight, grad_up, own_part, given_part = attend_back(
        near_grad, away_grad, output_weight, queries, key_rope, keyval, attention,
        normed, compressed, query_weight, up_weight, spread_cos, spread_sin,
    )
    grad_query_weight, grad_up, own_part, given_part, grad_output_weight = stage(
        grad_query_weight, grad_up, own_part, given_part, grad_output_weight
    )
    grad_packed = jnp.concatenate([grad_query_weight, grad_up.reshape(model_width, up_fold)], axis=1)
    grad_packed = grad_packed.reshape(cores, depth, PLANE * weight_rows, wide_q + up_fold)
    grad_packed = grad_packed.swapaxes(0, 1)
    given_part = hop(given_part, "fsdp", 1)
    own_part, given_part, grad_packed = stage(own_part, given_part, grad_packed)
    grad_packed = lax.all_to_all(grad_packed, "z", split_axis=0, concat_axis=0, tiled=True)
    normed_sum = scatter_sides(own_part, given_part)
    latent_sum = normed_sum[:, model_width:]
    own_latent = latent[:token_rows]
    grad_latent_norm, grad_latent_gain = norm_back(
        own_latent[:, :KVR], latent_gain_f, latent_sum[:, :KVR]
    )
    grad_latent = jnp.concatenate(
        [
            grad_latent_norm,
            unrotate(latent_sum[:, KVR : KVR + DR], cosine[:token_rows], sine_table[:token_rows]),
        ],
        axis=1,
    ).astype(BF)
    own_normed = normed[:token_rows]
    grad_normed = normed_sum[:, :model_width] + dot_last(grad_latent, down_weight)
    grad_flat_norm, grad_gain_one = norm_back(own_rows, gain_one_f, grad_normed)
    grad_tokens = grad_hidden + grad_flat_norm
    grad_latent_gain = jnp.pad(
        grad_latent_gain.reshape(-1, latent_rows), ((0, 0), (0, weight_rows - latent_rows))
    ).reshape(model_width)
    base = KVR + DR + experts
    columns = jnp.arange(small_width, dtype=jnp.int32)[None, :]

    def widen(values, start):
        return jnp.pad(values, ((0, 0), (start, small_width - start - values.shape[1])))

    grad_small = (
        dot_first(own_normed, widen(grad_latent, 0))
        + widen(grad_router, KVR + DR)
        + jnp.where(columns == base, grad_gain_one[:, None], 0.0)
        + jnp.where(columns == base + 1, grad_gain_two[:, None], 0.0)
        + jnp.where(columns == base + 2, grad_latent_gain[:, None], 0.0)
    )
    grad_small = straight(grad_small.astype(BF)).reshape(devices, weight_rows, small_width)
    grad_small = jnp.take(grad_small, everywhere, axis=0, mode="clip")
    grad_small = grad_small.reshape(cores, depth, PLANE, weight_rows, small_width)
    grad_tail = grad_small[0].astype(F32) + hop(grad_small[1], "fsdp", 1).astype(F32)
    grad_tail, grad_packed, grad_output_weight = stage(
        straight(grad_tail.astype(BF)), grad_packed, grad_output_weight
    )
    grad_packed = jnp.sum(grad_packed.astype(F32), axis=0).astype(BF)
    grad_shared_gate_up = (
        after(grad_shared_both, grad_tail)
        .reshape(experts, weight_rows, 2 * cores, unit)
        .transpose(1, 2, 0, 3)
        .reshape(weight_rows, 2 * FFS)
        .astype(F32)
    )
    grad_packed = lax.all_to_all(
        grad_packed.reshape(group, weight_rows, wide_q + up_fold),
        ("fsdp", "r"),
        split_axis=0,
        concat_axis=0,
        tiled=True,
    )
    grad_small = scatter_plane([grad_tail[:, j] for j in range(PLANE)])
    grad_output_weight = lax.ppermute(
        grad_output_weight, ("z", "r"), [(b, a) for a, b in shard_moves]
    )
    grad_small, grad_packed, grad_output_weight = stage(
        grad_small, grad_packed, grad_output_weight
    )
    grad_output_weight = grad_output_weight.astype(F32)
    grad_packed = grad_packed.swapaxes(0, 1)
    grad_small = grad_small[0] + sum(
        hop(grad_small[k].astype(BF), "z", k).astype(F32) for k in range(1, depth)
    )
    grad_q_weight = jnp.concatenate(
        [
            grad_packed[:, :, : heads * DN].reshape(weight_rows, group, heads, DN),
            grad_packed[:, :, heads * DN : wide_q].reshape(weight_rows, group, heads, DR),
        ],
        axis=3,
    )
    grad_q_weight = grad_q_weight.reshape(weight_rows, -1).astype(F32)
    grad_kv_up = (
        grad_packed[:, :, wide_q:]
        .reshape(latent_rows, fold, group, up_fold)
        .swapaxes(1, 2)
        .reshape(latent_rows, -1)
        .astype(F32)
    )
    return (
        output.astype(BF)[None],
        loss_value,
        grad_tokens[None],
        grad_small[:, base],
        grad_q_weight,
        grad_small[:, : KVR + DR],
        grad_small[:latent_rows, base + 2],
        grad_kv_up,
        grad_output_weight,
        grad_small[:, base + 1],
        grad_small[:, KVR + DR : base],
        grad_shared_gate_up,
        grad_shared_down,
        grad_expert_gate_up,
        grad_expert_down,
    )


def solution(mesh):
    cores = mesh.shape["fsdp"]
    experts = mesh.shape["expert"]
    grid = Mesh(mesh.devices.reshape(cores, experts // PLANE, PLANE), ("fsdp", "z", "r"))
    expert = ("z", "r")
    every = ("fsdp", "z", "r")
    return jax.shard_map(
        on_device,
        mesh=grid,
        in_specs=(
            P(expert, "fsdp", None),
            P(every),
            P(every, None),
            P(every, None),
            P(every),
            P(every, None),
            P(every, None),
            P(every),
            P(every, None),
            P(every, None),
            P(every, None),
            P(expert, "fsdp", None),
            P(expert, None, "fsdp"),
            P(expert, "fsdp", None),
            P(expert, "fsdp", None),
            P(expert),
            P(),
        ),
        out_specs=(
            P(expert, "fsdp", None),
            P(),
            P(expert, "fsdp", None),
            P(every),
            P(every, None),
            P(every, None),
            P(every),
            P(every, None),
            P(every, None),
            P(every),
            P(every, None),
            P(every, None),
            P(every, None),
            P(expert, "fsdp", None),
            P(expert, None, "fsdp"),
        ),
        check_vma=False,
    )
```

```python
import math

import jax
import jax.numpy as jnp
import numpy as np
from jax import lax
from jax.experimental import pallas as pl
from jax.experimental.layout import Layout, with_layout_constraint
from jax.experimental.pallas import tpu as pltpu
from jax.sharding import Mesh
from jax.sharding import PartitionSpec as P

NH = 16
DN = 128
DR = 64
DV = 128
KVR = 512
FFE = 1408
FFS = 2816
TOP = 6
PLANE = 4

BF = jnp.bfloat16
F32 = jnp.float32

epsilon = 1e-06


def rms_norm(values, gain_row):
    return (
        values * lax.rsqrt(jnp.mean(values * values, axis=-1, keepdims=True) + epsilon) * gain_row
    )


def norm_back(values, gain_row, incoming):
    factor = lax.rsqrt(jnp.mean(values * values, axis=-1, keepdims=True) + epsilon)
    scaled = incoming * gain_row
    grad_values = factor * scaled - values * (factor * factor * factor) * jnp.mean(
        scaled * values, axis=-1, keepdims=True
    )
    grad_gain = jnp.sum(incoming * values * factor, axis=0)
    return (grad_values, grad_gain)


def tables(position, rot_width):
    half_width = rot_width // 2
    frequency = 10000.0 ** (-2.0 * jnp.arange(half_width, dtype=F32) / rot_width)
    angles = position.astype(F32)[:, None] * frequency[None, :]
    return (jnp.cos(angles), jnp.sin(angles))


def unrotate(values, cosine, sine_table):
    half_width = values.shape[-1] // 2
    first_half = values[..., :half_width]
    second = values[..., half_width:]
    return jnp.concatenate(
        [first_half * cosine + second * sine_table, second * cosine - first_half * sine_table],
        axis=-1,
    )


def dot_plain(left_side, right_side):
    return jnp.dot(left_side, right_side, preferred_element_type=F32)


def dot_last(left_side, right_side):
    return lax.dot_general(
        left_side, right_side, (((1,), (1,)), ((), ())), preferred_element_type=F32
    )


def dot_first(left_side, right_side):
    return lax.dot_general(
        left_side, right_side, (((0,), (0,)), ((), ())), preferred_element_type=F32
    )


def straight(values):
    return with_layout_constraint(values, Layout(tuple(range(values.ndim))))


def after(values, *others):
    return lax.optimization_barrier((values,) + others)[0]


def stage(*values):
    return lax.optimization_barrier(values)


def hop(values, axis, distance):
    size = lax.axis_size(axis)
    moves = [(i, i ^ distance) for i in range(size)]
    return straight(lax.ppermute(straight(values), axis, moves))


def gather_plane(values):
    return [values] + [hop(values, "r", j) for j in range(1, PLANE)]


def scatter_plane(parts):
    moved = [hop(parts[j].astype(BF), "r", j) for j in range(1, PLANE)]
    return parts[0].astype(F32) + sum(part.astype(F32) for part in moved)


def scatter_sides(own, given):
    total = straight((own.astype(F32) + given.astype(F32)).astype(BF))
    return scatter_plane([total[j] for j in range(PLANE)])


def column_order(axis):
    return jnp.arange(lax.axis_size(axis), dtype=jnp.int32) ^ lax.axis_index(axis)


def both_cores(values):
    other = hop(values, "fsdp", 1)
    first = lax.axis_index("fsdp") == 0
    return jnp.concatenate(
        [jnp.where(first, values, other), jnp.where(first, other, values)], axis=0
    )


def by_column(parts):
    return jnp.take(parts.astype(BF), column_order("z"), axis=0, mode="clip")


def sum_columns(parts):
    moved = [hop(parts[k], "z", k) for k in range(1, lax.axis_size("z"))]
    return parts[0].astype(F32) + sum(part.astype(F32) for part in moved)


def gather_columns(values):
    spread = jnp.broadcast_to(values[None], (lax.axis_size("z"),) + values.shape)
    return lax.all_to_all(spread, "z", split_axis=0, concat_axis=0, tiled=True)


def gather_columns_apart(values):
    column = [values] + [hop(values, "z", k) for k in range(1, lax.axis_size("z"))]
    return jnp.take(jnp.stack(column, axis=0), column_order("z"), axis=0, mode="clip")


def all_order():
    return (column_order("z")[:, None] * PLANE + column_order("r")[None, :]).reshape(-1)


def swap_plane(parts):
    shape = parts.shape[1:]
    parts = jnp.take(parts, all_order(), axis=0, mode="clip")
    parts = parts.reshape((lax.axis_size("z"), PLANE) + shape)
    plane = [parts[:, 0]] + [hop(parts[:, j], "r", j) for j in range(1, PLANE)]
    return jnp.stack(plane, axis=1)


def swap_column(plane):
    depth = lax.axis_size("z")
    column = [plane[0]] + [hop(plane[k], "z", k) for k in range(1, depth)]
    column = jnp.stack(column, axis=0).reshape((depth * PLANE,) + plane.shape[2:])
    return jnp.take(column, all_order(), axis=0, mode="clip")


ROOM = 56 * 1024 * 1024


def whole(array):
    return pl.BlockSpec(array.shape, lambda *_: (0,) * array.ndim)


def sums_of_products(lefts, rights, tall, wide=None, kind=F32):
    height, width = lefts[0].shape[1], rights[0].shape[1]
    depth = sum(left.shape[0] for left in lefts)
    wide = width if wide is None else wide

    def stack(refs, into):
        start = 0
        for ref in refs:
            into[start : start + ref.shape[0], :] = ref[...]
            start += ref.shape[0]

    def body(*refs):
        out_ref, left_ref, right_ref = refs[-3:]

        @pl.when(pl.program_id(1) == 0)
        def _():
            stack(refs[len(lefts) : len(lefts) + len(rights)], right_ref)

        stack(refs[: len(lefts)], left_ref)
        out_ref[...] = dot_first(left_ref[...], right_ref[...]).astype(kind)

    return pl.pallas_call(
        body,
        grid=(width // wide, height // tall),
        in_specs=[pl.BlockSpec((left.shape[0], tall), lambda j, i: (0, i)) for left in lefts]
        + [pl.BlockSpec((right.shape[0], wide), lambda j, i: (0, j)) for right in rights],
        out_specs=pl.BlockSpec((tall, wide), lambda j, i: (i, j)),
        out_shape=jax.ShapeDtypeStruct((height, width), kind),
        scratch_shapes=[pltpu.VMEM((depth, tall), BF), pltpu.VMEM((depth, wide), BF)],
        compiler_params=pltpu.CompilerParams(vmem_limit_bytes=ROOM),
        cost_estimate=pl.CostEstimate(
            flops=2 * depth * height * width,
            bytes_accessed=2 * depth * (height + width) + 4 * height * width,
            transcendentals=0,
        ),
    )(*lefts, *rights)


def swiglu_parts(gate, up, incoming):
    sigmoid = jax.nn.sigmoid(gate)
    return (
        (incoming * up * sigmoid * (1.0 + gate * (1.0 - sigmoid))).astype(BF),
        (incoming * gate * sigmoid).astype(BF),
    )


TILE = 256
STRIP = 512
PARTS = 4


def spans(size, width):
    return [slice(start, min(start + width, size)) for start in range(0, size, width)]


class Copies:
    def __init__(self, semaphores):
        self.semaphores = semaphores
        self.used = 0

    def start(self, source, target):
        copy = pltpu.make_async_copy(source, target, self.semaphores.at[self.used])
        self.used += 1
        copy.start()
        return [copy]

    def start_rows(self, source, target):
        rows = source.shape[0]
        step = rows // PARTS
        copies = []
        for part in range(PARTS):
            span = pl.ds(part * step, step)
            copies += self.start(source.at[span, :], target.at[span, :])
        return copies


def wait(copies):
    for copy in copies:
        copy.wait()


def expert_forward(pieces, chosen, masks, mine, shared_router, both, down, shared_down):
    planes, rows, width = pieces[0].shape
    blocks, capacity = chosen.shape[:2]
    slots, flat_rows = blocks * capacity, blocks * rows
    hidden, units, experts = down.shape[0], shared_down.shape[0], mine.shape[1]
    strips = spans(width, STRIP)
    shapes = [
        ((slots, width), BF), ((slots, 2 * hidden), BF), ((slots, hidden), BF), ((slots, width), BF),
        ((flat_rows, 2 * units), BF), ((flat_rows, units), BF),
    ] + [((planes, rows, width), F32 if j == 0 else BF) for j in range(PLANE)]
    gate_shape = jax.ShapeDtypeStruct((flat_rows, 128), F32)

    def body(
        chosen_ref, masks_ref, mine_ref, piece_0, piece_1, piece_2, piece_3, router_hbm, both_hbm,
        down_hbm, shared_down_hbm,
        gates_ref, in_hbm, gu_hbm, act_hbm, out_hbm, shared_gu_hbm, shared_act_hbm,
        total_0, total_1, total_2, total_3,
        rows_ref, router_ref, both_ref, down_ref, shared_down_ref,
        in_ref, gu_ref, act_ref, out_ref, shared_gu_ref, shared_act_ref,
        sum_0, sum_1, sum_2, sum_3, semaphores,
    ):
        copies = Copies(semaphores)
        totals, sums = (total_0, total_1, total_2, total_3), (sum_0, sum_1, sum_2, sum_3)
        coming = []
        for j, piece in enumerate((piece_0, piece_1, piece_2, piece_3)):
            for k in range(planes):
                target = rows_ref.at[pl.ds((j * planes + k) * rows, rows), :]
                coming.append(copies.start(piece.at[k], target))
        router_in = copies.start_rows(router_hbm, router_ref)
        both_in = copies.start_rows(both_hbm, both_ref)
        down_in = copies.start_rows(down_hbm, down_ref)
        down_in += copies.start(shared_down_hbm, shared_down_ref)
        for block in range(blocks):
            wait(coming[block])
            in_ref[block * capacity : (block + 1) * capacity, :] = dot_plain(
                chosen_ref[block], rows_ref[block * rows : (block + 1) * rows, :]
            ).astype(BF)
        leaving = copies.start(in_ref, in_hbm)
        wait(router_in)
        joined = dot_plain(rows_ref[...], router_ref[...])
        gate, up = joined[:, :units], joined[:, units : 2 * units]
        shared_gu_ref[...] = joined[:, : 2 * units].astype(BF)
        shared_act_ref[...] = (gate * jax.nn.sigmoid(gate) * up).astype(BF)
        leaving += copies.start(shared_gu_ref, shared_gu_hbm)
        leaving += copies.start(shared_act_ref, shared_act_hbm)
        mask = masks_ref[...] > 0.0
        logits = jnp.where(mask, joined[:, 2 * units : 2 * units + experts], -1e30)
        odds = jnp.exp(logits - jnp.max(logits, axis=1, keepdims=True))
        odds = jnp.where(mask, odds, 0.0)
        own = jnp.sum(odds * mine_ref[...], axis=1, keepdims=True)
        own = own / jnp.sum(odds, axis=1, keepdims=True)
        gates_ref[...] = jnp.broadcast_to(own, gates_ref.shape)
        wait(both_in)
        for span in spans(hidden, TILE):
            above = slice(hidden + span.start, hidden + span.stop)
            gate = dot_plain(in_ref[...], both_ref[:, span])
            up = dot_plain(in_ref[...], both_ref[:, above])
            gu_ref[:, span] = gate.astype(BF)
            gu_ref[:, above] = up.astype(BF)
            act_ref[:, span] = (gate * jax.nn.sigmoid(gate) * up).astype(BF)
        leaving += copies.start(gu_ref, gu_hbm)
        leaving += copies.start(act_ref, act_hbm)
        wait(down_in)
        for strip in strips:
            out_ref[:, strip] = dot_plain(act_ref[...], down_ref[:, strip]).astype(BF)
            shared = dot_plain(shared_act_ref[...], shared_down_ref[:, strip])
            for j in range(PLANE):
                for k in range(planes):
                    block = j * planes + k
                    span = slice(block * rows, (block + 1) * rows)
                    picked = dot_first(
                        chosen_ref[block], out_ref[block * capacity : (block + 1) * capacity, strip]
                    )
                    sums[j][k, :, strip] = (gates_ref[span, 0:1] * picked + shared[span, :]).astype(
                        sums[j].dtype
                    )
                place = pl.ds(strip.start, strip.stop - strip.start)
                leaving += copies.start(sums[j].at[:, :, place], totals[j].at[:, :, place])
        leaving += copies.start(out_ref, out_hbm)
        wait(leaving)

    anywhere = pl.BlockSpec(memory_space=pl.ANY)
    moved = [shared_router, both, down, shared_down]
    scratch = [pltpu.VMEM((flat_rows, width), BF)]
    scratch += [pltpu.VMEM(array.shape, BF) for array in moved]
    scratch += [pltpu.VMEM(*shape) for shape in shapes]
    count = blocks + 3 * PARTS + 1 + 6 + PLANE * len(strips)
    return pl.pallas_call(
        body,
        in_specs=[pl.BlockSpec(memory_space=pltpu.VMEM)] * 3 + [anywhere] * (PLANE + len(moved)),
        out_specs=[pl.BlockSpec(memory_space=pltpu.VMEM)] + [anywhere] * len(shapes),
        out_shape=[gate_shape] + [jax.ShapeDtypeStruct(*shape) for shape in shapes],
        scratch_shapes=scratch + [pltpu.SemaphoreType.DMA((count,))],
        compiler_params=pltpu.CompilerParams(vmem_limit_bytes=ROOM),
        cost_estimate=pl.CostEstimate(
            flops=2 * width * (3 * slots * hidden + flat_rows * 4 * units),
            bytes_accessed=2 * width * (3 * hidden + 4 * units + 4 * flat_rows) + 12 * slots * hidden,
            transcendentals=slots * hidden,
        ),
    )(chosen, masks, mine, *pieces, *moved)


def expert_backward(pieces, chosen, gates, gu, out, shared_gu, shared_router, both, down, shared_down):
    planes, rows, width = pieces[0].shape
    blocks, capacity = chosen.shape[:2]
    slots, flat_rows = blocks * capacity, blocks * rows
    hidden, units = down.shape[0], shared_down.shape[0]
    strips = spans(width, STRIP)
    shapes = [
        ((slots, width), BF), ((slots, 2 * hidden), BF), ((flat_rows, 2 * units), BF),
    ] + [((planes, rows, width), F32 if j == 0 else BF) for j in range(PLANE)]
    gate_shape = jax.ShapeDtypeStruct((flat_rows, 128), F32)

    def body(
        chosen_ref, gates_ref, piece_0, piece_1, piece_2, piece_3, out_hbm, shared_gu_hbm, shared_down_hbm,
        gu_hbm, down_hbm, router_hbm, both_hbm,
        grad_gate_ref, slots_hbm, grad_gu_hbm, grad_shared_hbm, total_0, total_1, total_2, total_3,
        rows_ref, out_ref, shared_gu_ref, shared_down_ref, gu_ref, down_ref, router_ref, both_ref,
        slots_ref, grad_gu_ref, grad_shared_ref, sum_0, sum_1, sum_2, sum_3, semaphores,
    ):
        copies = Copies(semaphores)
        totals, sums = (total_0, total_1, total_2, total_3), (sum_0, sum_1, sum_2, sum_3)
        coming = []
        for j, piece in enumerate((piece_0, piece_1, piece_2, piece_3)):
            for k in range(planes):
                target = rows_ref.at[pl.ds((j * planes + k) * rows, rows), :]
                coming.append(copies.start(piece.at[k], target))
        out_in = copies.start_rows(out_hbm, out_ref)
        shared_in = copies.start(shared_gu_hbm, shared_gu_ref)
        shared_in += copies.start(shared_down_hbm, shared_down_ref)
        down_in = copies.start_rows(down_hbm, down_ref)
        down_in += copies.start(gu_hbm, gu_ref)
        both_in = copies.start_rows(both_hbm, both_ref)
        both_in += copies.start_rows(router_hbm, router_ref)
        wait(out_in)
        for block in range(blocks):
            wait(coming[block])
            span = slice(block * rows, (block + 1) * rows)
            part = slice(block * capacity, (block + 1) * capacity)
            values = rows_ref[span, :].astype(F32)
            slots_ref[part, :] = dot_plain(
                chosen_ref[block], (gates_ref[span, 0:1] * values).astype(BF)
            ).astype(BF)
            picked = dot_first(chosen_ref[block], out_ref[part, :])
            own = jnp.sum(values * picked, axis=1, keepdims=True)
            grad_gate_ref[span, :] = jnp.broadcast_to(own, (rows, 128))
        leaving = copies.start(slots_ref, slots_hbm)
        wait(shared_in)
        grad_gate, grad_up = swiglu_parts(
            shared_gu_ref[:, :units].astype(F32),
            shared_gu_ref[:, units:].astype(F32),
            dot_last(rows_ref[...], shared_down_ref[...]),
        )
        grad_shared_ref[:, :units] = grad_gate
        grad_shared_ref[:, units:] = grad_up
        leaving += copies.start(grad_shared_ref, grad_shared_hbm)
        wait(down_in)
        for span in spans(hidden, TILE):
            above = slice(hidden + span.start, hidden + span.stop)
            grad_gate, grad_up = swiglu_parts(
                gu_ref[:, span].astype(F32),
                gu_ref[:, above].astype(F32),
                dot_last(slots_ref[...], down_ref[span, :]),
            )
            grad_gu_ref[:, span] = grad_gate
            grad_gu_ref[:, above] = grad_up
        leaving += copies.start(grad_gu_ref, grad_gu_hbm)
        wait(both_in)
        for strip in strips:
            grad_in = dot_last(grad_gu_ref[...], both_ref[strip, :]).astype(BF)
            shared = dot_last(grad_shared_ref[...], router_ref[strip, : 2 * units])
            for j in range(PLANE):
                for k in range(planes):
                    block = j * planes + k
                    moved = dot_first(
                        chosen_ref[block], grad_in[block * capacity : (block + 1) * capacity, :]
                    )
                    sums[j][k, :, strip] = (moved + shared[block * rows : (block + 1) * rows, :]).astype(
                        sums[j].dtype
                    )
                place = pl.ds(strip.start, strip.stop - strip.start)
                leaving += copies.start(sums[j].at[:, :, place], totals[j].at[:, :, place])
        wait(leaving)

    anywhere = pl.BlockSpec(memory_space=pl.ANY)
    moved = [out, shared_gu, shared_down, gu, down, shared_router, both]
    scratch = [pltpu.VMEM((flat_rows, width), BF)]
    scratch += [pltpu.VMEM(array.shape, BF) for array in moved]
    scratch += [pltpu.VMEM(*shape) for shape in shapes]
    count = blocks + 4 * PARTS + 3 + 3 + PLANE * len(strips)
    return pl.pallas_call(
        body,
        in_specs=[pl.BlockSpec(memory_space=pltpu.VMEM)] * 2 + [anywhere] * (PLANE + len(moved)),
        out_specs=[pl.BlockSpec(memory_space=pltpu.VMEM)] + [anywhere] * len(shapes),
        out_shape=[gate_shape] + [jax.ShapeDtypeStruct(*shape) for shape in shapes],
        scratch_shapes=scratch + [pltpu.SemaphoreType.DMA((count,))],
        compiler_params=pltpu.CompilerParams(vmem_limit_bytes=ROOM),
        cost_estimate=pl.CostEstimate(
            flops=2 * width * (3 * slots * hidden + flat_rows * 4 * units),
            bytes_accessed=2 * width * (3 * hidden + 4 * units + 6 * flat_rows) + 12 * slots * hidden,
            transcendentals=slots * hidden,
        ),
    )(chosen, gates, *pieces, *moved)


def turn(values, cosine, sine_table):
    lane = lax.broadcasted_iota(jnp.int32, values.shape, 1)
    wide = values.shape[1]
    swapped = jnp.where(
        lane % DR < DR // 2,
        pltpu.roll(values, wide - DR // 2, 1),
        pltpu.roll(values, DR // 2, 1),
    )
    return values * cosine + swapped * sine_table


def head_lanes(values, head):
    lane = lax.broadcasted_iota(jnp.int32, values.shape, 1)
    return jnp.where(lane // DR == head, values, jnp.zeros_like(values))


def attend(near, away, gain, down, latent_gain, query, up, heads, cosine, sine_table, place, places, early):
    sequences, rows, width = near.shape
    length = 2 * rows
    nope = heads * DN
    span = KVR + 2 * DR
    scaling = (DN + DR) ** (-0.5)

    def body(
        near_ref, away_ref, gain_ref, down_ref, latent_gain_ref, query_ref, up_ref, cos_ref, sin_ref, place_ref, places_ref, early_ref,
        normed_ref, latent_ref, compressed_ref, queries_ref, rope_ref, keyval_ref,
        attention_ref, context_ref,
    ):
        for side, ref in enumerate((near_ref, away_ref)):
            values = ref[0].astype(F32)
            normed_ref[side * rows : (side + 1) * rows, :] = rms_norm(values, gain_ref[...]).astype(BF)
        normed = normed_ref[...]
        latent = dot_plain(normed, down_ref[:, :span])
        latent_ref[...] = latent
        compressed = rms_norm(latent[:, :KVR], latent_gain_ref[...]).astype(BF)
        compressed_ref[...] = compressed
        key_rope = head_lanes(turn(latent[:, KVR:], cos_ref[...], sin_ref[...]), 0)
        key_rope = (key_rope + pltpu.roll(key_rope, DR, 1)).astype(BF)
        rope_ref[...] = key_rope
        query_raw = dot_plain(normed, query_ref[...])
        queries_ref[:, :nope] = query_raw[:, :nope].astype(BF)
        query_rope = turn(query_raw[:, nope:], cos_ref[...], sin_ref[...]).astype(BF)
        queries_ref[:, nope:] = query_rope
        keyval_ref[...] = dot_plain(compressed, up_ref[...]).astype(BF)
        visible = (places_ref[0:1, :] <= place_ref[:, 0:1]) | (early_ref[0, 0:1, :] > 0.0)
        for head in range(heads):
            start = head * (DN + DV)
            scores = dot_last(
                queries_ref[:, head * DN : (head + 1) * DN], keyval_ref[:, start : start + DN]
            ) + dot_last(head_lanes(query_rope, head), key_rope)
            scores = jnp.where(visible, scores * scaling, -1e30)
            weights = jnp.exp(scores - jnp.max(scores, axis=1, keepdims=True))
            attention = weights / jnp.sum(weights, axis=1, keepdims=True)
            attention_ref[0, head] = attention
            context_ref[:, head * DV : (head + 1) * DV] = dot_plain(
                attention.astype(BF), keyval_ref[:, start + DN : start + DN + DV]
            ).astype(BF)

    def by_rows(columns):
        return pl.BlockSpec((length, columns), lambda s: (s, 0))

    def halves():
        return pl.BlockSpec((1, rows, width), lambda s: (s, 0, 0))

    every = sequences * length
    fixed = (gain, down, latent_gain, query, up, cosine, sine_table, place, places)
    columns = (width, span, KVR, query.shape[1], 2 * DR, up.shape[1])
    kinds = (BF, F32, BF, BF, BF, BF)
    return pl.pallas_call(
        body,
        grid=(sequences,),
        in_specs=[halves(), halves()]
        + [whole(array) for array in fixed]
        + [pl.BlockSpec((1,) + early.shape[1:], lambda s: (s, 0, 0))],
        out_specs=[by_rows(c) for c in columns]
        + [
            pl.BlockSpec((1, heads, length, length), lambda s: (s, 0, 0, 0)),
            by_rows(heads * DV),
        ],
        out_shape=[jax.ShapeDtypeStruct((every, c), k) for c, k in zip(columns, kinds)]
        + [
            jax.ShapeDtypeStruct((sequences, heads, length, length), F32),
            jax.ShapeDtypeStruct((every, heads * DV), BF),
        ],
        compiler_params=pltpu.CompilerParams(vmem_limit_bytes=ROOM),
        cost_estimate=pl.CostEstimate(
            flops=2 * every * (width * (span + query.shape[1]) + KVR * up.shape[1]),
            bytes_accessed=32 * 1024 * 1024,
            transcendentals=every * length * heads,
        ),
    )(near, away, *fixed, early)


def attend_back(
    near, away, out, queries, rope, keyval, attention, normed, compressed, query, up, cosine, sine_table
):
    sequences, rows, width = near.shape
    length = 2 * rows
    heads = out.shape[0] // DV
    nope = heads * DN
    span = KVR + 2 * DR
    scaling = (DN + DR) ** (-0.5)

    def body(
        near_ref, away_ref, queries_ref, rope_ref, keyval_ref, attention_ref,
        normed_ref, compressed_ref, out_ref, query_ref, up_ref, cos_ref, sin_ref,
        grad_query_out, grad_up_out, own_ref, given_ref,
        grad_query_ref, grad_up_ref, incoming_ref, columns_ref, pairs_ref,
    ):
        @pl.when(pl.program_id(0) == 0)
        def _():
            grad_query_ref[...] = jnp.zeros_like(grad_query_ref)
            grad_up_ref[...] = jnp.zeros_like(grad_up_ref)

        incoming_ref[:rows, :] = near_ref[0]
        incoming_ref[rows:, :] = away_ref[0]
        incoming = incoming_ref[...]
        grad_context = dot_last(incoming, out_ref[...]).astype(BF)
        key_rope = rope_ref[...]
        query_rope = queries_ref[:, nope:]
        grad_query_rope = jnp.zeros((length, 2 * DR), F32)
        grad_key_rope = jnp.zeros((length, 2 * DR), F32)
        for head in range(heads):
            start = head * (DN + DV)
            attention = attention_ref[0, head]
            grad_head = grad_context[:, head * DV : (head + 1) * DV]
            grad_attention = dot_last(grad_head, keyval_ref[:, start + DN : start + DN + DV])
            grad_scores = attention * (
                grad_attention - jnp.sum(attention * grad_attention, axis=1, keepdims=True)
            )
            grad_scores = grad_scores.astype(BF)
            columns_ref[:, head * DN : (head + 1) * DN] = (
                dot_plain(grad_scores, keyval_ref[:, start : start + DN]) * scaling
            ).astype(BF)
            grad_query_rope += head_lanes(dot_plain(grad_scores, key_rope) * scaling, head)
            pairs_ref[:, start : start + DN] = (
                dot_first(grad_scores, queries_ref[:, head * DN : (head + 1) * DN]) * scaling
            ).astype(BF)
            pairs_ref[:, start + DN : start + DN + DV] = dot_first(
                attention.astype(BF), grad_head
            ).astype(BF)
            grad_key_rope += dot_first(grad_scores, head_lanes(query_rope, head)) * scaling
        columns_ref[:, nope:] = turn(grad_query_rope, cos_ref[...], -sin_ref[...]).astype(BF)
        grad_key_rope += pltpu.roll(grad_key_rope, DR, 1)
        columns = columns_ref[...]
        pairs = pairs_ref[...]
        grad_query_ref[...] += dot_first(normed_ref[...], columns)
        grad_up_ref[...] += dot_first(compressed_ref[...], pairs)
        latent = dot_last(pairs, up_ref[...])
        total = dot_last(columns, query_ref[...])
        own_ref[0, :, :width] = total[:rows].astype(BF)
        given_ref[0, :, :width] = total[rows:].astype(BF)
        own_ref[0, :, width : width + KVR] = latent[:rows].astype(BF)
        given_ref[0, :, width : width + KVR] = latent[rows:].astype(BF)
        own_ref[0, :, width + KVR :] = grad_key_rope[:rows].astype(BF)

        @pl.when(pl.program_id(0) == sequences - 1)
        def _():
            grad_query_out[...] = grad_query_ref[...].astype(BF)
            grad_up_out[...] = grad_up_ref[...].astype(BF)

        given_ref[0, :, width + KVR :] = grad_key_rope[rows:].astype(BF)

    def by_rows(columns):
        return pl.BlockSpec((length, columns), lambda s: (s, 0))

    def halves(columns):
        return pl.BlockSpec((1, rows, columns), lambda s: (s, 0, 0))

    every = sequences * length
    moving = (queries, rope, keyval)
    fixed = (out, query, up, cosine, sine_table)
    shapes = (
        (query.shape, BF), (up.shape, BF),
        ((sequences, rows, width + span), BF), ((sequences, rows, width + span), BF),
    )
    return pl.pallas_call(
        body,
        grid=(sequences,),
        in_specs=[halves(width), halves(width)]
        + [by_rows(array.shape[1]) for array in moving]
        + [pl.BlockSpec((1, heads, length, length), lambda s: (s, 0, 0, 0))]
        + [by_rows(normed.shape[1]), by_rows(compressed.shape[1])]
        + [whole(array) for array in fixed],
        out_specs=[whole(query), whole(up)]
        + [halves(width + span), halves(width + span)],
        out_shape=[jax.ShapeDtypeStruct(shape, kind) for shape, kind in shapes],
        scratch_shapes=[
            pltpu.VMEM(query.shape, F32),
            pltpu.VMEM(up.shape, F32),
            pltpu.VMEM((length, width), BF),
            pltpu.VMEM((length, query.shape[1]), BF),
            pltpu.VMEM((length, up.shape[1]), BF),
        ],
        compiler_params=pltpu.CompilerParams(vmem_limit_bytes=ROOM),
        cost_estimate=pl.CostEstimate(
            flops=4 * every * (width * (query.shape[1] + heads * DV) + KVR * up.shape[1]),
            bytes_accessed=48 * 1024 * 1024,
            transcendentals=0,
        ),
    )(near, away, *moving, attention, normed, compressed, *fixed)


def on_device(
    tokens,
    norm1_gain,
    q_weight,
    kv_down,
    latent_gain,
    kv_up,
    o_weight,
    norm2_gain,
    router,
    shared_gate_up,
    shared_down,
    expert_gate_up,
    expert_down,
    teacher,
    routes,
    prefix,
    token_count,
):
    cores = lax.axis_size("fsdp")
    depth = lax.axis_size("z")
    experts = depth * PLANE
    group = cores * PLANE
    heads = NH // group
    core = lax.axis_index("fsdp")
    plane_index = lax.axis_index("z")
    spot = lax.axis_index("r")
    own_expert = plane_index * PLANE + spot
    token_rows = tokens.shape[1]
    model_width = tokens.shape[2]
    seq_length = token_rows * cores
    capacity = -(-max(2, token_rows * TOP * 5 // (experts * 3)) // 16) * 16
    weight_rows = q_weight.shape[0]
    latent_rows = kv_up.shape[0]
    wide_q = heads * (DN + DR)
    wide_kv = heads * (DN + DV)
    scaling = (DN + DR) ** (-0.5)
    devices = cores * experts
    every = PLANE * seq_length
    everywhere = jnp.arange(devices, dtype=jnp.int32) ^ (core * experts + own_expert)

    sub = depth // PLANE
    shard_moves = [
        (z * PLANE + r, ((z % sub) * PLANE + r) * PLANE + z // sub)
        for z in range(depth)
        for r in range(PLANE)
    ]

    moved_o = lax.ppermute(o_weight, ("z", "r"), shard_moves)
    first_rows = tokens[0]

    fold = weight_rows // latent_rows
    up_fold = wide_kv // fold
    up_packed = kv_up.reshape(latent_rows, group, fold, up_fold)
    up_packed = up_packed.swapaxes(1, 2).reshape(weight_rows, group, up_fold)
    by_head = q_weight.reshape(weight_rows, group, heads, DN + DR)
    packed = jnp.concatenate(
        [
            by_head[..., :DN].reshape(weight_rows, group, heads * DN),
            by_head[..., DN:].reshape(weight_rows, group, heads * DR),
            up_packed,
        ],
        axis=2,
    )
    packed = lax.all_to_all(
        packed.swapaxes(0, 1), ("fsdp", "r"), split_axis=0, concat_axis=0, tiled=True
    )
    packed = packed.reshape(cores, PLANE * weight_rows, wide_q + up_fold)

    own_mask = jnp.any(
        routes[0][:, :, None] == jnp.arange(experts, dtype=jnp.int32)[None, None, :], axis=1
    )
    small = jnp.concatenate(
        [
            kv_down,
            router,
            norm1_gain[:, None],
            norm2_gain[:, None],
            jnp.pad(latent_gain, (0, weight_rows - latent_rows))[:, None],
            jnp.broadcast_to(prefix.astype(BF)[None, :], (weight_rows, 1)),
            own_mask.astype(BF).reshape(weight_rows, -1),
        ],
        axis=1,
    )
    small_width = -(-small.shape[1] // 128) * 128
    small = jnp.pad(small, ((0, 0), (0, small_width - small.shape[1])))
    small = jnp.stack([small] + [hop(small, "z", k) for k in range(1, depth)], axis=0)
    shared_both = shared_gate_up.reshape(weight_rows, 2 * cores, experts, shared_down.shape[0])
    shared_both = shared_both.transpose(2, 0, 1, 3).reshape(experts, weight_rows, -1)
    near_rows = jnp.stack(gather_plane(first_rows), axis=0)
    packed, small, near_rows, shared_both = stage(packed, small, near_rows, shared_both)
    packed = gather_columns(packed)
    away_rows = hop(near_rows, "fsdp", 1)
    small = jnp.stack(gather_plane(small), axis=1)
    small = jnp.stack([small, hop(small, "fsdp", 1)], axis=0)
    shared_both = swap_plane(after(shared_both, small))
    packed, shared_both, moved_o = stage(packed, shared_both, moved_o, small, away_rows)[:3]
    output_weight = gather_columns_apart(moved_o).reshape(heads * DV, model_width)
    small = small.reshape(devices, weight_rows, small_width)
    prefixes = small[:PLANE, 0, KVR + DR + experts + 3].astype(F32)
    masks = small[:experts, :, KVR + DR + experts + 4 :][:, :, : token_rows * experts // weight_rows]
    masks = masks.astype(F32).reshape(experts, token_rows, experts)
    small = jnp.take(small, everywhere, axis=0, mode="clip").reshape(model_width, small_width)
    down_weight = small[:, : KVR + DR]
    router_weight = small[:, KVR + DR : KVR + DR + experts]
    gains = small[:, KVR + DR + experts : KVR + DR + experts + 3].astype(F32).T
    gain_one_f = gains[0]
    gain_two_f = gains[1]
    latent_gain_f = gains[2].reshape(-1, weight_rows)[:, :latent_rows].reshape(KVR)

    half = jnp.arange(token_rows, dtype=jnp.int32)
    position = jnp.concatenate([core * token_rows + half, (1 - core) * token_rows + half])
    cosine, sine_table = tables(position, DR)
    spread_cos = jnp.tile(cosine, (1, 4))
    spread_sin = jnp.tile(jnp.concatenate([-sine_table, sine_table], axis=1), (1, 2))
    places = position.astype(F32)
    early = (places[None, :] < prefixes[:, None]).astype(F32)
    early = jnp.broadcast_to(early[:, None, :], (PLANE, 8, seq_length))
    packed = packed.swapaxes(0, 1).reshape(model_width, wide_q + up_fold)
    query_weight = packed[:, :wide_q]
    up_weight = packed[:, wide_q:].reshape(KVR, fold * up_fold)


    normed, latent, compressed, queries, key_rope, keyval, attention, context = attend(
        near_rows, away_rows, gain_one_f[None], small, latent_gain_f[None], query_weight,
        up_weight, heads, spread_cos, spread_sin,
        jnp.broadcast_to(places[:, None], (seq_length, 128)),
        jnp.broadcast_to(places[None, :], (8, seq_length)), early,
    )
    expert_both_weight = lax.all_gather(expert_gate_up, "fsdp", axis=1, tiled=True)[0]
    expert_down_weight = lax.all_gather(expert_down, "fsdp", axis=2, tiled=True)[0]
    unit = shared_down.shape[0]
    shared_units = cores * unit
    masks = after(masks, packed)
    order = jnp.arange(experts, dtype=jnp.int32) ^ own_expert
    mine = (jnp.arange(experts, dtype=jnp.int32) == own_expert).astype(F32)
    taken = jnp.sum(masks * mine[None, None, :], axis=2)
    rank = jnp.cumsum(taken, axis=1) - taken
    select = taken[:, None, :] * (
        rank[:, None, :] == jnp.arange(capacity, dtype=F32)[None, :, None]
    ).astype(F32)
    select_low = select.astype(BF)
    steps = depth
    lots = [[k] for k in range(depth)]
    lots = lots[:1] + lots[2:] + lots[1:2]
    block_order = np.array(
        [k * PLANE + j for planes in lots for j in range(PLANE) for k in planes], dtype=np.int32
    )
    chunk_select = jnp.take(select_low, block_order, axis=0, mode="clip")
    chunk_select = chunk_select.reshape(steps, PLANE, capacity, token_rows)
    chunk_masks = jnp.take(masks, block_order, axis=0, mode="clip")
    chunk_masks = chunk_masks.reshape(steps, PLANE * token_rows, experts)
    context, output_weight, chunk_select, chunk_masks = stage(
        context, output_weight, chunk_select, chunk_masks
    )
    sides = context.reshape(PLANE, cores, token_rows, heads * DV)

    def project(side):
        flat = sides[:, side].reshape(PLANE * token_rows, heads * DV)
        return dot_plain(flat, output_weight).reshape(PLANE, token_rows, model_width)

    given_part = hop(project(1).astype(BF), "fsdp", 1)
    own_part = project(0).astype(BF)
    shared_down_weight = both_cores(shared_down)
    own_part, given_part, shared_both, shared_down_weight = stage(
        own_part, given_part, shared_both, shared_down_weight
    )
    shared_both = swap_column(shared_both).reshape(experts * weight_rows, 2 * shared_units)
    own_rows = tokens[0].astype(F32)
    hidden = own_rows + scatter_sides(own_part, given_part)
    hidden, shared_both = stage(hidden, shared_both)
    shared_both_weight = both_cores(shared_both)
    normed2 = rms_norm(hidden, gain_two_f).astype(BF)

    def gates_of(logits, mask):
        logits = jnp.where(mask, logits, -1e30)
        odds = jnp.where(mask, jnp.exp(logits - jnp.max(logits, axis=-1, keepdims=True)), 0.0)
        return odds / jnp.sum(odds, axis=-1, keepdims=True)

    own_gates = gates_of(dot_plain(normed2, router_weight), own_mask)
    wide_unit = -(-unit // 128) * 128
    padded = cores * wide_unit

    def pad_columns(values, columns):
        return jnp.pad(values, ((0, 0), (0, columns - values.shape[1])))

    shared_router = jnp.concatenate(
        [
            pad_columns(shared_both_weight[:, start : start + unit], wide_unit)
            for start in range(0, 2 * shared_units, unit)
        ]
        + [
            pad_columns(router_weight, -(-experts // 128) * 128),
        ],
        axis=1,
    )
    shared_rows = jnp.pad(
        shared_down_weight.reshape(cores, unit, model_width),
        ((0, 0), (0, wide_unit - unit), (0, 0)),
    ).reshape(padded, model_width)

    def passes(values, compute, besides):
        def fetch(values, number):
            return jnp.stack([hop(values, "z", k) if k else values for k in lots[number]], axis=0)

        source, pieces, totals, summed = fetch(values, 0), None, None, None
        returned, results = [], []
        for step in range(steps + 3):
            later = [values, None, None, None, None, None]
            if step + 1 < steps:
                later[1] = fetch(values, step + 1)
            if pieces is not None:
                later[3] = compute(step - 1, pieces, results)
            if source is not None and totals is not None:
                count, half = source.shape[0], source.shape[1] // 2
                along, across = [
                    hop(jnp.concatenate([source, totals[j]], axis=0), "r", j) for j in (1, 2)
                ]
                opposite = hop(totals[3], "r", 3)
                behind = later[3][1]
                far = jnp.concatenate(
                    [
                        hop(after(along[:count, :half], behind), "r", 2),
                        hop(after(across[:count, half:], behind), "r", 1),
                    ],
                    axis=1,
                )
                later[2] = [source, along[:count], across[:count], far]
                later[4] = totals[0] + sum(
                    part.astype(F32) for part in (along[count:], across[count:], opposite)
                )
            elif source is not None:
                later[2] = gather_plane(source)
            elif totals is not None:
                later[4] = scatter_plane(totals)
            if summed is not None:
                later[5] = [
                    hop(summed[i].astype(BF), "z", k) if k else summed[i]
                    for i, k in enumerate(lots[step - 3])
                ]
            later.append(besides(step, summed if totals is None else totals[0], results))
            values, source, pieces, totals, summed, back, beside = lax.optimization_barrier(later)
            if beside is not None:
                results.append(beside)
            if back is not None:
                returned += [part.astype(F32) for part in back]
        return sum(returned), results

    def forward_chunk(number, pieces, results):
        values = expert_forward(
            pieces, chunk_select[number], chunk_masks[number], mine[None], results[0][0],
            expert_both_weight, expert_down_weight, results[0][1],
        )
        arrived.append([piece.reshape(-1, model_width) for piece in pieces])
        saved.append(values[:7])
        return list(values[7:])

    def backward_chunk(number, pieces, results):
        gates, expert_in, expert_gu, expert_act, expert_out, shared_gu, shared_act = saved[number]
        values = expert_backward(
            pieces, chunk_select[number], gates, expert_gu, expert_out, shared_gu, shared_router,
            expert_both_weight, expert_down_weight, shared_rows,
        )
        grad_arrived.append([piece.reshape(-1, model_width) for piece in pieces])
        grads.append(values[:4])
        return list(values[4:])

    arrived, saved, grad_arrived, grads = [], [], [], []
    routed, results = passes(
        normed2,
        forward_chunk,
        lambda step, behind, results: (shared_router, shared_rows, chunk_select, chunk_masks)
        if step == 0
        else None,
    )
    shared_router, shared_rows = results[0][:2]
    output = hidden + routed
    misfit = output - teacher[0].astype(F32)
    misfit_low = misfit.astype(BF)

    def products(lefts, rights, behind, tall, wide=None):
        return sums_of_products([after(lefts[0], behind)] + lefts[1:], rights, tall, wide)

    def kept(lists, entry):
        return [values[entry] for values in lists]

    def joined(lists):
        return [piece for pieces in lists for piece in pieces]

    def weight_grads(step, behind, results):
        if step == steps + 1:
            grad_gate = jnp.concatenate([values[0][:, 0] for values in grads], axis=0)
            grad_gate = jnp.take(
                after(grad_gate.reshape(experts, token_rows), behind),
                np.argsort(block_order), axis=0, mode="clip",
            )
            squares = jnp.broadcast_to(jnp.sum(misfit * misfit)[None, None], (experts, 128))
            notes = jnp.concatenate([jnp.take(grad_gate, order, axis=0, mode="clip"), squares], axis=1)
            return (
                products(joined(arrived), kept(grads, 3), behind, 512),
                products(kept(saved, 6), joined(grad_arrived), behind, padded, 512),
                notes,
            )
        if step == steps + 2:
            notes = lax.all_to_all(results[0][2], ("z", "r"), split_axis=0, concat_axis=0, tiled=True)
            return products(kept(saved, 3), kept(grads, 1), behind, FFE, 512), notes
        return None

    grad_returned, results = passes(misfit_low, backward_chunk, weight_grads)
    grad_shared, (grad_expert_down, notes) = results
    grad_shared_both, grad_shared_down = grad_shared[:2]
    grad_expert_down = lax.psum_scatter(
        grad_expert_down[None], "fsdp", scatter_dimension=2, tiled=True
    )
    grad_shared_down = lax.psum_scatter(
        grad_shared_down, "fsdp", scatter_dimension=0, tiled=True
    )[:unit]
    grad_shared_both = lax.psum_scatter(
        grad_shared_both, "fsdp", scatter_dimension=0, tiled=True
    )
    grad_shared_both = jnp.concatenate(
        [
            grad_shared_both[:, start : start + unit].astype(BF)
            for start in range(0, 2 * padded, wide_unit)
        ],
        axis=1,
    )
    grad_shared_both = lax.all_to_all(
        grad_shared_both.reshape(experts, weight_rows, 2 * shared_units),
        ("z", "r"),
        split_axis=0,
        concat_axis=0,
        tiled=True,
    )

    grad_gates = notes[:, :token_rows].T
    all_squares = jnp.sum(notes[:, token_rows])[None]
    all_squares = all_squares + hop(jnp.broadcast_to(all_squares, (8, 128)), "fsdp", 1)[0, :1]
    loss_value = all_squares / (token_count.astype(F32) * model_width)
    grad_logits = (
        own_gates * (grad_gates - jnp.sum(own_gates * grad_gates, axis=1, keepdims=True))
    ).astype(BF)
    grad_normed2 = grad_returned + dot_last(grad_logits, router_weight)
    grad_hidden_norm, grad_gain_two = norm_back(hidden, gain_two_f, grad_normed2)
    grad_hidden = misfit + grad_hidden_norm
    near_grad = jnp.stack(gather_plane(grad_hidden.astype(BF)), axis=0)
    grad_expert_gate_up = products(kept(saved, 1), kept(grads, 2), grad_hidden, 256)
    near_grad, grad_expert_gate_up, grad_shared_both = stage(
        near_grad, grad_expert_gate_up, grad_shared_both
    )
    grad_expert_gate_up = lax.psum_scatter(
        grad_expert_gate_up[None], "fsdp", scatter_dimension=1, tiled=True
    )
    away_grad = hop(near_grad, "fsdp", 1)
    flat = (PLANE * token_rows, model_width)
    grad_output_weight = sums_of_products(
        [sides[:, 0].reshape(flat[0], -1), sides[:, 1].reshape(flat[0], -1)],
        [near_grad.reshape(flat), away_grad.reshape(flat)],
        heads * DV,
        512,
        BF,
    )
    grad_output_weight = by_column(grad_output_weight.reshape(depth, weight_rows, model_width))
    grad_router = dot_first(normed2, grad_logits)
    grad_output_weight, away_grad, grad_router = stage(grad_output_weight, away_grad, grad_router)
    grad_output_weight = sum_columns(grad_output_weight).astype(BF)
    grad_query_weight, grad_up, own_part, given_part = attend_back(
        near_grad, away_grad, output_weight, queries, key_rope, keyval, attention,
        normed, compressed, query_weight, up_weight, spread_cos, spread_sin,
    )
    grad_query_weight, grad_up, own_part, given_part, grad_output_weight = stage(
        grad_query_weight, grad_up, own_part, given_part, grad_output_weight
    )
    grad_packed = jnp.concatenate([grad_query_weight, grad_up.reshape(model_width, up_fold)], axis=1)
    grad_packed = grad_packed.reshape(cores, depth, PLANE * weight_rows, wide_q + up_fold)
    grad_packed = grad_packed.swapaxes(0, 1)
    given_part = hop(given_part, "fsdp", 1)
    own_part, given_part, grad_packed = stage(own_part, given_part, grad_packed)
    grad_packed = lax.all_to_all(grad_packed, "z", split_axis=0, concat_axis=0, tiled=True)
    normed_sum = scatter_sides(own_part, given_part)
    latent_sum = normed_sum[:, model_width:]
    own_latent = latent[:token_rows]
    grad_latent_norm, grad_latent_gain = norm_back(
        own_latent[:, :KVR], latent_gain_f, latent_sum[:, :KVR]
    )
    grad_latent = jnp.concatenate(
        [
            grad_latent_norm,
            unrotate(latent_sum[:, KVR : KVR + DR], cosine[:token_rows], sine_table[:token_rows]),
        ],
        axis=1,
    ).astype(BF)
    own_normed = normed[:token_rows]
    grad_normed = normed_sum[:, :model_width] + dot_last(grad_latent, down_weight)
    grad_flat_norm, grad_gain_one = norm_back(own_rows, gain_one_f, grad_normed)
    grad_tokens = grad_hidden + grad_flat_norm
    grad_latent_gain = jnp.pad(
        grad_latent_gain.reshape(-1, latent_rows), ((0, 0), (0, weight_rows - latent_rows))
    ).reshape(model_width)
    base = KVR + DR + experts
    columns = jnp.arange(small_width, dtype=jnp.int32)[None, :]

    def widen(values, start):
        return jnp.pad(values, ((0, 0), (start, small_width - start - values.shape[1])))

    grad_small = (
        dot_first(own_normed, widen(grad_latent, 0))
        + widen(grad_router, KVR + DR)
        + jnp.where(columns == base, grad_gain_one[:, None], 0.0)
        + jnp.where(columns == base + 1, grad_gain_two[:, None], 0.0)
        + jnp.where(columns == base + 2, grad_latent_gain[:, None], 0.0)
    )
    grad_small = straight(grad_small.astype(BF)).reshape(devices, weight_rows, small_width)
    grad_small = jnp.take(grad_small, everywhere, axis=0, mode="clip")
    grad_small = grad_small.reshape(cores, depth, PLANE, weight_rows, small_width)
    grad_tail = grad_small[0].astype(F32) + hop(grad_small[1], "fsdp", 1).astype(F32)
    grad_tail, grad_packed, grad_output_weight = stage(
        straight(grad_tail.astype(BF)), grad_packed, grad_output_weight
    )
    grad_packed = jnp.sum(grad_packed.astype(F32), axis=0).astype(BF)
    grad_shared_gate_up = (
        after(grad_shared_both, grad_tail)
        .reshape(experts, weight_rows, 2 * cores, unit)
        .transpose(1, 2, 0, 3)
        .reshape(weight_rows, 2 * FFS)
        .astype(F32)
    )
    grad_packed = lax.all_to_all(
        grad_packed.reshape(group, weight_rows, wide_q + up_fold),
        ("fsdp", "r"),
        split_axis=0,
        concat_axis=0,
        tiled=True,
    )
    grad_small = scatter_plane([grad_tail[:, j] for j in range(PLANE)])
    grad_output_weight = lax.ppermute(
        grad_output_weight, ("z", "r"), [(b, a) for a, b in shard_moves]
    )
    grad_small, grad_packed, grad_output_weight = stage(
        grad_small, grad_packed, grad_output_weight
    )
    grad_output_weight = grad_output_weight.astype(F32)
    grad_packed = grad_packed.swapaxes(0, 1)
    grad_small = grad_small[0] + sum(
        hop(grad_small[k].astype(BF), "z", k).astype(F32) for k in range(1, depth)
    )
    grad_q_weight = jnp.concatenate(
        [
            grad_packed[:, :, : heads * DN].reshape(weight_rows, group, heads, DN),
            grad_packed[:, :, heads * DN : wide_q].reshape(weight_rows, group, heads, DR),
        ],
        axis=3,
    )
    grad_q_weight = grad_q_weight.reshape(weight_rows, -1).astype(F32)
    grad_kv_up = (
        grad_packed[:, :, wide_q:]
        .reshape(latent_rows, fold, group, up_fold)
        .swapaxes(1, 2)
        .reshape(latent_rows, -1)
        .astype(F32)
    )
    return (
        output.astype(BF)[None],
        loss_value,
        grad_tokens[None],
        grad_small[:, base],
        grad_q_weight,
        grad_small[:, : KVR + DR],
        grad_small[:latent_rows, base + 2],
        grad_kv_up,
        grad_output_weight,
        grad_small[:, base + 1],
        grad_small[:, KVR + DR : base],
        grad_shared_gate_up,
        grad_shared_down,
        grad_expert_gate_up,
        grad_expert_down,
    )


def solution(mesh):
    cores = mesh.shape["fsdp"]
    experts = mesh.shape["expert"]
    grid = Mesh(mesh.devices.reshape(cores, experts // PLANE, PLANE), ("fsdp", "z", "r"))
    expert = ("z", "r")
    every = ("fsdp", "z", "r")
    return jax.shard_map(
        on_device,
        mesh=grid,
        in_specs=(
            P(expert, "fsdp", None),
            P(every),
            P(every, None),
            P(every, None),
            P(every),
            P(every, None),
            P(every, None),
            P(every),
            P(every, None),
            P(every, None),
            P(every, None),
            P(expert, "fsdp", None),
            P(expert, None, "fsdp"),
            P(expert, "fsdp", None),
            P(expert, "fsdp", None),
            P(expert),
            P(),
        ),
        out_specs=(
            P(expert, "fsdp", None),
            P(),
            P(expert, "fsdp", None),
            P(every),
            P(every, None),
            P(every, None),
            P(every),
            P(every, None),
            P(every, None),
            P(every),
            P(every, None),
            P(every, None),
            P(every, None),
            P(expert, "fsdp", None),
            P(expert, None, "fsdp"),
        ),
        check_vma=False,
    )
```

```python
import math

import jax
import jax.numpy as jnp
import numpy as np
from jax import lax
from jax.experimental import pallas as pl
from jax.experimental.layout import Layout, with_layout_constraint
from jax.experimental.pallas import tpu as pltpu
from jax.sharding import Mesh
from jax.sharding import PartitionSpec as P

NH = 16
DN = 128
DR = 64
DV = 128
KVR = 512
FFE = 1408
FFS = 2816
TOP = 6
PLANE = 4

BF = jnp.bfloat16
F32 = jnp.float32

epsilon = 1e-06


def rms_norm(values, gain_row):
    return (
        values * lax.rsqrt(jnp.mean(values * values, axis=-1, keepdims=True) + epsilon) * gain_row
    )


def norm_back(values, gain_row, incoming):
    factor = lax.rsqrt(jnp.mean(values * values, axis=-1, keepdims=True) + epsilon)
    scaled = incoming * gain_row
    grad_values = factor * scaled - values * (factor * factor * factor) * jnp.mean(
        scaled * values, axis=-1, keepdims=True
    )
    grad_gain = jnp.sum(incoming * values * factor, axis=0)
    return (grad_values, grad_gain)


def tables(position, rot_width):
    half_width = rot_width // 2
    frequency = 10000.0 ** (-2.0 * jnp.arange(half_width, dtype=F32) / rot_width)
    angles = position.astype(F32)[:, None] * frequency[None, :]
    return (jnp.cos(angles), jnp.sin(angles))


def unrotate(values, cosine, sine_table):
    half_width = values.shape[-1] // 2
    first_half = values[..., :half_width]
    second = values[..., half_width:]
    return jnp.concatenate(
        [first_half * cosine + second * sine_table, second * cosine - first_half * sine_table],
        axis=-1,
    )


def dot_plain(left_side, right_side):
    return jnp.dot(left_side, right_side, preferred_element_type=F32)


def dot_last(left_side, right_side):
    return lax.dot_general(
        left_side, right_side, (((1,), (1,)), ((), ())), preferred_element_type=F32
    )


def dot_first(left_side, right_side):
    return lax.dot_general(
        left_side, right_side, (((0,), (0,)), ((), ())), preferred_element_type=F32
    )


def straight(values):
    return with_layout_constraint(values, Layout(tuple(range(values.ndim))))


def after(values, *others):
    return lax.optimization_barrier((values,) + others)[0]


def stage(*values):
    return lax.optimization_barrier(values)


def hop(values, axis, distance):
    size = lax.axis_size(axis)
    moves = [(i, i ^ distance) for i in range(size)]
    return straight(lax.ppermute(straight(values), axis, moves))


def gather_plane(values):
    return [values] + [hop(values, "r", j) for j in range(1, PLANE)]


def scatter_plane(parts):
    moved = [hop(parts[j].astype(BF), "r", j) for j in range(1, PLANE)]
    return parts[0].astype(F32) + sum(part.astype(F32) for part in moved)


def scatter_sides(own, given):
    total = straight((own.astype(F32) + given.astype(F32)).astype(BF))
    return scatter_plane([total[j] for j in range(PLANE)])


def column_order(axis):
    return jnp.arange(lax.axis_size(axis), dtype=jnp.int32) ^ lax.axis_index(axis)


def both_cores(values):
    other = hop(values, "fsdp", 1)
    first = lax.axis_index("fsdp") == 0
    return jnp.concatenate(
        [jnp.where(first, values, other), jnp.where(first, other, values)], axis=0
    )


def by_column(parts):
    return jnp.take(parts.astype(BF), column_order("z"), axis=0, mode="clip")


def sum_columns(parts):
    moved = [hop(parts[k], "z", k) for k in range(1, lax.axis_size("z"))]
    return parts[0].astype(F32) + sum(part.astype(F32) for part in moved)


def gather_columns(values):
    spread = jnp.broadcast_to(values[None], (lax.axis_size("z"),) + values.shape)
    return lax.all_to_all(spread, "z", split_axis=0, concat_axis=0, tiled=True)


def gather_columns_apart(values):
    column = [values] + [hop(values, "z", k) for k in range(1, lax.axis_size("z"))]
    return jnp.take(jnp.stack(column, axis=0), column_order("z"), axis=0, mode="clip")


def all_order():
    return (column_order("z")[:, None] * PLANE + column_order("r")[None, :]).reshape(-1)


def swap_plane(parts):
    shape = parts.shape[1:]
    parts = jnp.take(parts, all_order(), axis=0, mode="clip")
    parts = parts.reshape((lax.axis_size("z"), PLANE) + shape)
    plane = [parts[:, 0]] + [hop(parts[:, j], "r", j) for j in range(1, PLANE)]
    return jnp.stack(plane, axis=1)


def swap_column(plane):
    depth = lax.axis_size("z")
    column = [plane[0]] + [hop(plane[k], "z", k) for k in range(1, depth)]
    column = jnp.stack(column, axis=0).reshape((depth * PLANE,) + plane.shape[2:])
    return jnp.take(column, all_order(), axis=0, mode="clip")


ROOM = 56 * 1024 * 1024


def whole(array):
    return pl.BlockSpec(array.shape, lambda *_: (0,) * array.ndim)


def sums_of_products(lefts, rights, tall, wide=None, kind=F32):
    height, width = lefts[0].shape[1], rights[0].shape[1]
    depth = sum(left.shape[0] for left in lefts)
    wide = width if wide is None else wide

    def stack(refs, into):
        start = 0
        for ref in refs:
            into[start : start + ref.shape[0], :] = ref[...]
            start += ref.shape[0]

    def body(*refs):
        out_ref, left_ref, right_ref = refs[-3:]

        @pl.when(pl.program_id(1) == 0)
        def _():
            stack(refs[len(lefts) : len(lefts) + len(rights)], right_ref)

        stack(refs[: len(lefts)], left_ref)
        out_ref[...] = dot_first(left_ref[...], right_ref[...]).astype(kind)

    return pl.pallas_call(
        body,
        grid=(width // wide, height // tall),
        in_specs=[pl.BlockSpec((left.shape[0], tall), lambda j, i: (0, i)) for left in lefts]
        + [pl.BlockSpec((right.shape[0], wide), lambda j, i: (0, j)) for right in rights],
        out_specs=pl.BlockSpec((tall, wide), lambda j, i: (i, j)),
        out_shape=jax.ShapeDtypeStruct((height, width), kind),
        scratch_shapes=[pltpu.VMEM((depth, tall), BF), pltpu.VMEM((depth, wide), BF)],
        compiler_params=pltpu.CompilerParams(vmem_limit_bytes=ROOM),
        cost_estimate=pl.CostEstimate(
            flops=2 * depth * height * width,
            bytes_accessed=2 * depth * (height + width) + 4 * height * width,
            transcendentals=0,
        ),
    )(*lefts, *rights)


def swiglu_parts(gate, up, incoming):
    sigmoid = jax.nn.sigmoid(gate)
    return (
        (incoming * up * sigmoid * (1.0 + gate * (1.0 - sigmoid))).astype(BF),
        (incoming * gate * sigmoid).astype(BF),
    )


TILE = 256
STRIP = 512
PARTS = 4


def spans(size, width):
    return [slice(start, min(start + width, size)) for start in range(0, size, width)]


class Copies:
    def __init__(self, semaphores):
        self.semaphores = semaphores
        self.used = 0

    def start(self, source, target):
        copy = pltpu.make_async_copy(source, target, self.semaphores.at[self.used])
        self.used += 1
        copy.start()
        return [copy]

    def start_rows(self, source, target):
        rows = source.shape[0]
        step = rows // PARTS
        copies = []
        for part in range(PARTS):
            span = pl.ds(part * step, step)
            copies += self.start(source.at[span, :], target.at[span, :])
        return copies


def wait(copies):
    for copy in copies:
        copy.wait()


def expert_forward(pieces, chosen, masks, mine, shared_router, both, down, shared_down):
    planes, rows, width = pieces[0].shape
    blocks, capacity = chosen.shape[:2]
    slots, flat_rows = blocks * capacity, blocks * rows
    hidden, units, experts = down.shape[0], shared_down.shape[0], mine.shape[1]
    strips = spans(width, STRIP)
    shapes = [
        ((slots, width), BF), ((slots, 2 * hidden), BF), ((slots, hidden), BF), ((slots, width), BF),
        ((flat_rows, 2 * units), BF), ((flat_rows, units), BF),
    ] + [((planes, rows, width), F32 if j == 0 else BF) for j in range(PLANE)]
    gate_shape = jax.ShapeDtypeStruct((flat_rows, 128), F32)

    def body(
        chosen_ref, masks_ref, mine_ref, piece_0, piece_1, piece_2, piece_3, router_hbm, both_hbm,
        down_hbm, shared_down_hbm,
        gates_ref, in_hbm, gu_hbm, act_hbm, out_hbm, shared_gu_hbm, shared_act_hbm,
        total_0, total_1, total_2, total_3,
        rows_ref, router_ref, both_ref, down_ref, shared_down_ref,
        in_ref, gu_ref, act_ref, out_ref, shared_gu_ref, shared_act_ref,
        sum_0, sum_1, sum_2, sum_3, semaphores,
    ):
        copies = Copies(semaphores)
        totals, sums = (total_0, total_1, total_2, total_3), (sum_0, sum_1, sum_2, sum_3)
        coming = []
        for j, piece in enumerate((piece_0, piece_1, piece_2, piece_3)):
            for k in range(planes):
                target = rows_ref.at[pl.ds((j * planes + k) * rows, rows), :]
                coming.append(copies.start(piece.at[k], target))
        router_in = copies.start_rows(router_hbm, router_ref)
        both_in = copies.start_rows(both_hbm, both_ref)
        down_in = copies.start_rows(down_hbm, down_ref)
        down_in += copies.start(shared_down_hbm, shared_down_ref)
        for block in range(blocks):
            wait(coming[block])
            in_ref[block * capacity : (block + 1) * capacity, :] = dot_plain(
                chosen_ref[block], rows_ref[block * rows : (block + 1) * rows, :]
            ).astype(BF)
        leaving = copies.start(in_ref, in_hbm)
        wait(router_in)
        joined = dot_plain(rows_ref[...], router_ref[...])
        gate, up = joined[:, :units], joined[:, units : 2 * units]
        shared_gu_ref[...] = joined[:, : 2 * units].astype(BF)
        shared_act_ref[...] = (gate * jax.nn.sigmoid(gate) * up).astype(BF)
        leaving += copies.start(shared_gu_ref, shared_gu_hbm)
        leaving += copies.start(shared_act_ref, shared_act_hbm)
        mask = masks_ref[...] > 0.0
        logits = jnp.where(mask, joined[:, 2 * units : 2 * units + experts], -1e30)
        odds = jnp.exp(logits - jnp.max(logits, axis=1, keepdims=True))
        odds = jnp.where(mask, odds, 0.0)
        own = jnp.sum(odds * mine_ref[...], axis=1, keepdims=True)
        own = own / jnp.sum(odds, axis=1, keepdims=True)
        gates_ref[...] = jnp.broadcast_to(own, gates_ref.shape)
        wait(both_in)
        for span in spans(hidden, TILE):
            above = slice(hidden + span.start, hidden + span.stop)
            gate = dot_plain(in_ref[...], both_ref[:, span])
            up = dot_plain(in_ref[...], both_ref[:, above])
            gu_ref[:, span] = gate.astype(BF)
            gu_ref[:, above] = up.astype(BF)
            act_ref[:, span] = (gate * jax.nn.sigmoid(gate) * up).astype(BF)
        leaving += copies.start(gu_ref, gu_hbm)
        leaving += copies.start(act_ref, act_hbm)
        wait(down_in)
        for strip in strips:
            out_ref[:, strip] = dot_plain(act_ref[...], down_ref[:, strip]).astype(BF)
            shared = dot_plain(shared_act_ref[...], shared_down_ref[:, strip])
            for j in range(PLANE):
                for k in range(planes):
                    block = j * planes + k
                    span = slice(block * rows, (block + 1) * rows)
                    picked = dot_first(
                        chosen_ref[block], out_ref[block * capacity : (block + 1) * capacity, strip]
                    )
                    sums[j][k, :, strip] = (gates_ref[span, 0:1] * picked + shared[span, :]).astype(
                        sums[j].dtype
                    )
                place = pl.ds(strip.start, strip.stop - strip.start)
                leaving += copies.start(sums[j].at[:, :, place], totals[j].at[:, :, place])
        leaving += copies.start(out_ref, out_hbm)
        wait(leaving)

    anywhere = pl.BlockSpec(memory_space=pl.ANY)
    moved = [shared_router, both, down, shared_down]
    scratch = [pltpu.VMEM((flat_rows, width), BF)]
    scratch += [pltpu.VMEM(array.shape, BF) for array in moved]
    scratch += [pltpu.VMEM(*shape) for shape in shapes]
    count = blocks + 3 * PARTS + 1 + 6 + PLANE * len(strips)
    return pl.pallas_call(
        body,
        in_specs=[pl.BlockSpec(memory_space=pltpu.VMEM)] * 3 + [anywhere] * (PLANE + len(moved)),
        out_specs=[pl.BlockSpec(memory_space=pltpu.VMEM)] + [anywhere] * len(shapes),
        out_shape=[gate_shape] + [jax.ShapeDtypeStruct(*shape) for shape in shapes],
        scratch_shapes=scratch + [pltpu.SemaphoreType.DMA((count,))],
        compiler_params=pltpu.CompilerParams(vmem_limit_bytes=ROOM),
        cost_estimate=pl.CostEstimate(
            flops=2 * width * (3 * slots * hidden + flat_rows * 4 * units),
            bytes_accessed=2 * width * (3 * hidden + 4 * units + 4 * flat_rows) + 12 * slots * hidden,
            transcendentals=slots * hidden,
        ),
    )(chosen, masks, mine, *pieces, *moved)


def expert_backward(pieces, chosen, gates, gu, out, shared_gu, shared_router, both, down, shared_down):
    planes, rows, width = pieces[0].shape
    blocks, capacity = chosen.shape[:2]
    slots, flat_rows = blocks * capacity, blocks * rows
    hidden, units = down.shape[0], shared_down.shape[0]
    strips = spans(width, STRIP)
    shapes = [
        ((slots, width), BF), ((slots, 2 * hidden), BF), ((flat_rows, 2 * units), BF),
    ] + [((planes, rows, width), F32 if j == 0 else BF) for j in range(PLANE)]
    gate_shape = jax.ShapeDtypeStruct((flat_rows, 128), F32)

    def body(
        chosen_ref, gates_ref, piece_0, piece_1, piece_2, piece_3, out_hbm, shared_gu_hbm, shared_down_hbm,
        gu_hbm, down_hbm, router_hbm, both_hbm,
        grad_gate_ref, slots_hbm, grad_gu_hbm, grad_shared_hbm, total_0, total_1, total_2, total_3,
        rows_ref, out_ref, shared_gu_ref, shared_down_ref, gu_ref, down_ref, router_ref, both_ref,
        slots_ref, grad_gu_ref, grad_shared_ref, sum_0, sum_1, sum_2, sum_3, semaphores,
    ):
        copies = Copies(semaphores)
        totals, sums = (total_0, total_1, total_2, total_3), (sum_0, sum_1, sum_2, sum_3)
        coming = []
        for j, piece in enumerate((piece_0, piece_1, piece_2, piece_3)):
            for k in range(planes):
                target = rows_ref.at[pl.ds((j * planes + k) * rows, rows), :]
                coming.append(copies.start(piece.at[k], target))
        out_in = copies.start_rows(out_hbm, out_ref)
        shared_in = copies.start(shared_gu_hbm, shared_gu_ref)
        shared_in += copies.start(shared_down_hbm, shared_down_ref)
        down_in = copies.start_rows(down_hbm, down_ref)
        down_in += copies.start(gu_hbm, gu_ref)
        both_in = copies.start_rows(both_hbm, both_ref)
        both_in += copies.start_rows(router_hbm, router_ref)
        wait(out_in)
        for block in range(blocks):
            wait(coming[block])
            span = slice(block * rows, (block + 1) * rows)
            part = slice(block * capacity, (block + 1) * capacity)
            values = rows_ref[span, :].astype(F32)
            slots_ref[part, :] = dot_plain(
                chosen_ref[block], (gates_ref[span, 0:1] * values).astype(BF)
            ).astype(BF)
            picked = dot_first(chosen_ref[block], out_ref[part, :])
            own = jnp.sum(values * picked, axis=1, keepdims=True)
            grad_gate_ref[span, :] = jnp.broadcast_to(own, (rows, 128))
        leaving = copies.start(slots_ref, slots_hbm)
        wait(shared_in)
        grad_gate, grad_up = swiglu_parts(
            shared_gu_ref[:, :units].astype(F32),
            shared_gu_ref[:, units:].astype(F32),
            dot_last(rows_ref[...], shared_down_ref[...]),
        )
        grad_shared_ref[:, :units] = grad_gate
        grad_shared_ref[:, units:] = grad_up
        leaving += copies.start(grad_shared_ref, grad_shared_hbm)
        wait(down_in)
        for span in spans(hidden, TILE):
            above = slice(hidden + span.start, hidden + span.stop)
            grad_gate, grad_up = swiglu_parts(
                gu_ref[:, span].astype(F32),
                gu_ref[:, above].astype(F32),
                dot_last(slots_ref[...], down_ref[span, :]),
            )
            grad_gu_ref[:, span] = grad_gate
            grad_gu_ref[:, above] = grad_up
        leaving += copies.start(grad_gu_ref, grad_gu_hbm)
        wait(both_in)
        for strip in strips:
            grad_in = dot_last(grad_gu_ref[...], both_ref[strip, :]).astype(BF)
            shared = dot_last(grad_shared_ref[...], router_ref[strip, : 2 * units])
            for j in range(PLANE):
                for k in range(planes):
                    block = j * planes + k
                    moved = dot_first(
                        chosen_ref[block], grad_in[block * capacity : (block + 1) * capacity, :]
                    )
                    sums[j][k, :, strip] = (moved + shared[block * rows : (block + 1) * rows, :]).astype(
                        sums[j].dtype
                    )
                place = pl.ds(strip.start, strip.stop - strip.start)
                leaving += copies.start(sums[j].at[:, :, place], totals[j].at[:, :, place])
        wait(leaving)

    anywhere = pl.BlockSpec(memory_space=pl.ANY)
    moved = [out, shared_gu, shared_down, gu, down, shared_router, both]
    scratch = [pltpu.VMEM((flat_rows, width), BF)]
    scratch += [pltpu.VMEM(array.shape, BF) for array in moved]
    scratch += [pltpu.VMEM(*shape) for shape in shapes]
    count = blocks + 4 * PARTS + 3 + 3 + PLANE * len(strips)
    return pl.pallas_call(
        body,
        in_specs=[pl.BlockSpec(memory_space=pltpu.VMEM)] * 2 + [anywhere] * (PLANE + len(moved)),
        out_specs=[pl.BlockSpec(memory_space=pltpu.VMEM)] + [anywhere] * len(shapes),
        out_shape=[gate_shape] + [jax.ShapeDtypeStruct(*shape) for shape in shapes],
        scratch_shapes=scratch + [pltpu.SemaphoreType.DMA((count,))],
        compiler_params=pltpu.CompilerParams(vmem_limit_bytes=ROOM),
        cost_estimate=pl.CostEstimate(
            flops=2 * width * (3 * slots * hidden + flat_rows * 4 * units),
            bytes_accessed=2 * width * (3 * hidden + 4 * units + 6 * flat_rows) + 12 * slots * hidden,
            transcendentals=slots * hidden,
        ),
    )(chosen, gates, *pieces, *moved)


def turn(values, cosine, sine_table):
    lane = lax.broadcasted_iota(jnp.int32, values.shape, 1)
    wide = values.shape[1]
    swapped = jnp.where(
        lane % DR < DR // 2,
        pltpu.roll(values, wide - DR // 2, 1),
        pltpu.roll(values, DR // 2, 1),
    )
    return values * cosine + swapped * sine_table


def head_lanes(values, head):
    lane = lax.broadcasted_iota(jnp.int32, values.shape, 1)
    return jnp.where(lane // DR == head, values, jnp.zeros_like(values))


def attend(near, away, gain, down, latent_gain, query, up, heads, cosine, sine_table, place, places, early):
    sequences, rows, width = near.shape
    length = 2 * rows
    nope = heads * DN
    span = KVR + 2 * DR
    scaling = (DN + DR) ** (-0.5)

    def body(
        near_ref, away_ref, gain_ref, down_ref, latent_gain_ref, query_ref, up_ref, cos_ref, sin_ref, place_ref, places_ref, early_ref,
        normed_ref, latent_ref, compressed_ref, queries_ref, rope_ref, keyval_ref,
        attention_ref, near_context_ref, away_context_ref,
    ):
        for side, ref in enumerate((near_ref, away_ref)):
            values = ref[0].astype(F32)
            normed_ref[side * rows : (side + 1) * rows, :] = rms_norm(values, gain_ref[...]).astype(BF)
        normed = normed_ref[...]
        latent = dot_plain(normed, down_ref[:, :span])
        latent_ref[...] = latent
        compressed = rms_norm(latent[:, :KVR], latent_gain_ref[...]).astype(BF)
        compressed_ref[...] = compressed
        key_rope = head_lanes(turn(latent[:, KVR:], cos_ref[...], sin_ref[...]), 0)
        key_rope = (key_rope + pltpu.roll(key_rope, DR, 1)).astype(BF)
        rope_ref[...] = key_rope
        query_raw = dot_plain(normed, query_ref[...])
        queries_ref[:, :nope] = query_raw[:, :nope].astype(BF)
        query_rope = turn(query_raw[:, nope:], cos_ref[...], sin_ref[...]).astype(BF)
        queries_ref[:, nope:] = query_rope
        keyval_ref[...] = dot_plain(compressed, up_ref[...]).astype(BF)
        visible = (places_ref[0:1, :] <= place_ref[:, 0:1]) | (early_ref[0, 0:1, :] > 0.0)
        for head in range(heads):
            start = head * (DN + DV)
            scores = dot_last(
                queries_ref[:, head * DN : (head + 1) * DN], keyval_ref[:, start : start + DN]
            ) + dot_last(head_lanes(query_rope, head), key_rope)
            scores = jnp.where(visible, scores * scaling, -1e30)
            weights = jnp.exp(scores - jnp.max(scores, axis=1, keepdims=True))
            attention = weights / jnp.sum(weights, axis=1, keepdims=True)
            attention_ref[0, head] = attention
            context = dot_plain(
                attention.astype(BF), keyval_ref[:, start + DN : start + DN + DV]
            ).astype(BF)
            near_context_ref[0, :, head * DV : (head + 1) * DV] = context[:rows]
            away_context_ref[0, :, head * DV : (head + 1) * DV] = context[rows:]

    def by_rows(columns):
        return pl.BlockSpec((length, columns), lambda s: (s, 0))

    def halves():
        return pl.BlockSpec((1, rows, width), lambda s: (s, 0, 0))

    every = sequences * length
    fixed = (gain, down, latent_gain, query, up, cosine, sine_table, place, places)
    columns = (width, span, KVR, query.shape[1], 2 * DR, up.shape[1])
    kinds = (BF, F32, BF, BF, BF, BF)
    return pl.pallas_call(
        body,
        grid=(sequences,),
        in_specs=[halves(), halves()]
        + [whole(array) for array in fixed]
        + [pl.BlockSpec((1,) + early.shape[1:], lambda s: (s, 0, 0))],
        out_specs=[by_rows(c) for c in columns]
        + [
            pl.BlockSpec((1, heads, length, length), lambda s: (s, 0, 0, 0)),
            pl.BlockSpec((1, rows, heads * DV), lambda s: (s, 0, 0)),
            pl.BlockSpec((1, rows, heads * DV), lambda s: (s, 0, 0)),
        ],
        out_shape=[jax.ShapeDtypeStruct((every, c), k) for c, k in zip(columns, kinds)]
        + [
            jax.ShapeDtypeStruct((sequences, heads, length, length), F32),
            jax.ShapeDtypeStruct((sequences, rows, heads * DV), BF),
            jax.ShapeDtypeStruct((sequences, rows, heads * DV), BF),
        ],
        compiler_params=pltpu.CompilerParams(vmem_limit_bytes=ROOM),
        cost_estimate=pl.CostEstimate(
            flops=2 * every * (width * (span + query.shape[1]) + KVR * up.shape[1]),
            bytes_accessed=32 * 1024 * 1024,
            transcendentals=every * length * heads,
        ),
    )(near, away, *fixed, early)


def attend_back(
    near, away, out, queries, rope, keyval, attention, normed, compressed, query, up, cosine, sine_table
):
    sequences, rows, width = near.shape
    length = 2 * rows
    heads = out.shape[0] // DV
    nope = heads * DN
    span = KVR + 2 * DR
    scaling = (DN + DR) ** (-0.5)

    def body(
        near_ref, away_ref, queries_ref, rope_ref, keyval_ref, attention_ref,
        normed_ref, compressed_ref, out_ref, query_ref, up_ref, cos_ref, sin_ref,
        grad_query_out, grad_up_out, own_ref, given_ref,
        grad_query_ref, grad_up_ref, incoming_ref, columns_ref, pairs_ref,
    ):
        @pl.when(pl.program_id(0) == 0)
        def _():
            grad_query_ref[...] = jnp.zeros_like(grad_query_ref)
            grad_up_ref[...] = jnp.zeros_like(grad_up_ref)

        incoming_ref[:rows, :] = near_ref[0]
        incoming_ref[rows:, :] = away_ref[0]
        incoming = incoming_ref[...]
        grad_context = dot_last(incoming, out_ref[...]).astype(BF)
        key_rope = rope_ref[...]
        query_rope = queries_ref[:, nope:]
        grad_query_rope = jnp.zeros((length, 2 * DR), F32)
        grad_key_rope = jnp.zeros((length, 2 * DR), F32)
        for head in range(heads):
            start = head * (DN + DV)
            attention = attention_ref[0, head]
            grad_head = grad_context[:, head * DV : (head + 1) * DV]
            grad_attention = dot_last(grad_head, keyval_ref[:, start + DN : start + DN + DV])
            grad_scores = attention * (
                grad_attention - jnp.sum(attention * grad_attention, axis=1, keepdims=True)
            )
            grad_scores = grad_scores.astype(BF)
            columns_ref[:, head * DN : (head + 1) * DN] = (
                dot_plain(grad_scores, keyval_ref[:, start : start + DN]) * scaling
            ).astype(BF)
            grad_query_rope += head_lanes(dot_plain(grad_scores, key_rope) * scaling, head)
            pairs_ref[:, start : start + DN] = (
                dot_first(grad_scores, queries_ref[:, head * DN : (head + 1) * DN]) * scaling
            ).astype(BF)
            pairs_ref[:, start + DN : start + DN + DV] = dot_first(
                attention.astype(BF), grad_head
            ).astype(BF)
            grad_key_rope += dot_first(grad_scores, head_lanes(query_rope, head)) * scaling
        columns_ref[:, nope:] = turn(grad_query_rope, cos_ref[...], -sin_ref[...]).astype(BF)
        grad_key_rope += pltpu.roll(grad_key_rope, DR, 1)
        columns = columns_ref[...]
        pairs = pairs_ref[...]
        grad_query_ref[...] += dot_first(normed_ref[...], columns)
        grad_up_ref[...] += dot_first(compressed_ref[...], pairs)
        latent = dot_last(pairs, up_ref[...])
        total = dot_last(columns, query_ref[...])
        own_ref[0, :, :width] = total[:rows].astype(BF)
        given_ref[0, :, :width] = total[rows:].astype(BF)
        own_ref[0, :, width : width + KVR] = latent[:rows].astype(BF)
        given_ref[0, :, width : width + KVR] = latent[rows:].astype(BF)
        own_ref[0, :, width + KVR :] = grad_key_rope[:rows].astype(BF)

        @pl.when(pl.program_id(0) == sequences - 1)
        def _():
            grad_query_out[...] = grad_query_ref[...].astype(BF)
            grad_up_out[...] = grad_up_ref[...].astype(BF)

        given_ref[0, :, width + KVR :] = grad_key_rope[rows:].astype(BF)

    def by_rows(columns):
        return pl.BlockSpec((length, columns), lambda s: (s, 0))

    def halves(columns):
        return pl.BlockSpec((1, rows, columns), lambda s: (s, 0, 0))

    every = sequences * length
    moving = (queries, rope, keyval)
    fixed = (out, query, up, cosine, sine_table)
    shapes = (
        (query.shape, BF), (up.shape, BF),
        ((sequences, rows, width + span), BF), ((sequences, rows, width + span), BF),
    )
    return pl.pallas_call(
        body,
        grid=(sequences,),
        in_specs=[halves(width), halves(width)]
        + [by_rows(array.shape[1]) for array in moving]
        + [pl.BlockSpec((1, heads, length, length), lambda s: (s, 0, 0, 0))]
        + [by_rows(normed.shape[1]), by_rows(compressed.shape[1])]
        + [whole(array) for array in fixed],
        out_specs=[whole(query), whole(up)]
        + [halves(width + span), halves(width + span)],
        out_shape=[jax.ShapeDtypeStruct(shape, kind) for shape, kind in shapes],
        scratch_shapes=[
            pltpu.VMEM(query.shape, F32),
            pltpu.VMEM(up.shape, F32),
            pltpu.VMEM((length, width), BF),
            pltpu.VMEM((length, query.shape[1]), BF),
            pltpu.VMEM((length, up.shape[1]), BF),
        ],
        compiler_params=pltpu.CompilerParams(vmem_limit_bytes=ROOM),
        cost_estimate=pl.CostEstimate(
            flops=4 * every * (width * (query.shape[1] + heads * DV) + KVR * up.shape[1]),
            bytes_accessed=48 * 1024 * 1024,
            transcendentals=0,
        ),
    )(near, away, *moving, attention, normed, compressed, *fixed)


def on_device(
    tokens,
    norm1_gain,
    q_weight,
    kv_down,
    latent_gain,
    kv_up,
    o_weight,
    norm2_gain,
    router,
    shared_gate_up,
    shared_down,
    expert_gate_up,
    expert_down,
    teacher,
    routes,
    prefix,
    token_count,
):
    cores = lax.axis_size("fsdp")
    depth = lax.axis_size("z")
    experts = depth * PLANE
    group = cores * PLANE
    heads = NH // group
    core = lax.axis_index("fsdp")
    plane_index = lax.axis_index("z")
    spot = lax.axis_index("r")
    own_expert = plane_index * PLANE + spot
    token_rows = tokens.shape[1]
    model_width = tokens.shape[2]
    seq_length = token_rows * cores
    capacity = -(-max(2, token_rows * TOP * 5 // (experts * 3)) // 16) * 16
    weight_rows = q_weight.shape[0]
    latent_rows = kv_up.shape[0]
    wide_q = heads * (DN + DR)
    wide_kv = heads * (DN + DV)
    scaling = (DN + DR) ** (-0.5)
    devices = cores * experts
    every = PLANE * seq_length
    everywhere = jnp.arange(devices, dtype=jnp.int32) ^ (core * experts + own_expert)

    sub = depth // PLANE
    shard_moves = [
        (z * PLANE + r, ((z % sub) * PLANE + r) * PLANE + z // sub)
        for z in range(depth)
        for r in range(PLANE)
    ]

    moved_o = lax.ppermute(o_weight, ("z", "r"), shard_moves)
    first_rows = tokens[0]

    fold = weight_rows // latent_rows
    up_fold = wide_kv // fold
    up_packed = kv_up.reshape(latent_rows, group, fold, up_fold)
    up_packed = up_packed.swapaxes(1, 2).reshape(weight_rows, group, up_fold)
    by_head = q_weight.reshape(weight_rows, group, heads, DN + DR)
    packed = jnp.concatenate(
        [
            by_head[..., :DN].reshape(weight_rows, group, heads * DN),
            by_head[..., DN:].reshape(weight_rows, group, heads * DR),
            up_packed,
        ],
        axis=2,
    )
    packed = lax.all_to_all(
        packed.swapaxes(0, 1), ("fsdp", "r"), split_axis=0, concat_axis=0, tiled=True
    )
    packed = packed.reshape(cores, PLANE * weight_rows, wide_q + up_fold)

    own_mask = jnp.any(
        routes[0][:, :, None] == jnp.arange(experts, dtype=jnp.int32)[None, None, :], axis=1
    )
    small = jnp.concatenate(
        [
            kv_down,
            router,
            norm1_gain[:, None],
            norm2_gain[:, None],
            jnp.pad(latent_gain, (0, weight_rows - latent_rows))[:, None],
            jnp.broadcast_to(prefix.astype(BF)[None, :], (weight_rows, 1)),
            own_mask.astype(BF).reshape(weight_rows, -1),
        ],
        axis=1,
    )
    small_width = -(-small.shape[1] // 128) * 128
    small = jnp.pad(small, ((0, 0), (0, small_width - small.shape[1])))
    small = jnp.stack([small] + [hop(small, "z", k) for k in range(1, depth)], axis=0)
    shared_both = shared_gate_up.reshape(weight_rows, 2 * cores, experts, shared_down.shape[0])
    shared_both = shared_both.transpose(2, 0, 1, 3).reshape(experts, weight_rows, -1)
    near_rows = jnp.stack(gather_plane(first_rows), axis=0)
    packed, small, near_rows, shared_both = stage(packed, small, near_rows, shared_both)
    packed = gather_columns(packed)
    away_rows = hop(near_rows, "fsdp", 1)
    small = jnp.stack(gather_plane(small), axis=1)
    small = jnp.stack([small, hop(small, "fsdp", 1)], axis=0)
    shared_both = swap_plane(after(shared_both, small))
    packed, shared_both, moved_o = stage(packed, shared_both, moved_o, small, away_rows)[:3]
    output_weight = gather_columns_apart(moved_o).reshape(heads * DV, model_width)
    small = small.reshape(devices, weight_rows, small_width)
    prefixes = small[:PLANE, 0, KVR + DR + experts + 3].astype(F32)
    masks = small[:experts, :, KVR + DR + experts + 4 :][:, :, : token_rows * experts // weight_rows]
    masks = masks.astype(F32).reshape(experts, token_rows, experts)
    small = jnp.take(small, everywhere, axis=0, mode="clip").reshape(model_width, small_width)
    down_weight = small[:, : KVR + DR]
    router_weight = small[:, KVR + DR : KVR + DR + experts]
    gains = small[:, KVR + DR + experts : KVR + DR + experts + 3].astype(F32).T
    gain_one_f = gains[0]
    gain_two_f = gains[1]
    latent_gain_f = gains[2].reshape(-1, weight_rows)[:, :latent_rows].reshape(KVR)

    half = jnp.arange(token_rows, dtype=jnp.int32)
    position = jnp.concatenate([core * token_rows + half, (1 - core) * token_rows + half])
    cosine, sine_table = tables(position, DR)
    spread_cos = jnp.tile(cosine, (1, 4))
    spread_sin = jnp.tile(jnp.concatenate([-sine_table, sine_table], axis=1), (1, 2))
    places = position.astype(F32)
    early = (places[None, :] < prefixes[:, None]).astype(F32)
    early = jnp.broadcast_to(early[:, None, :], (PLANE, 8, seq_length))
    packed = packed.swapaxes(0, 1).reshape(model_width, wide_q + up_fold)
    query_weight = packed[:, :wide_q]
    up_weight = packed[:, wide_q:].reshape(KVR, fold * up_fold)


    normed, latent, compressed, queries, key_rope, keyval, attention, *context = attend(
        near_rows, away_rows, gain_one_f[None], small, latent_gain_f[None], query_weight,
        up_weight, heads, spread_cos, spread_sin,
        jnp.broadcast_to(places[:, None], (seq_length, 128)),
        jnp.broadcast_to(places[None, :], (8, seq_length)), early,
    )
    expert_both_weight = lax.all_gather(expert_gate_up, "fsdp", axis=1, tiled=True)[0]
    expert_down_weight = lax.all_gather(expert_down, "fsdp", axis=2, tiled=True)[0]
    unit = shared_down.shape[0]
    shared_units = cores * unit
    masks = after(masks, packed)
    order = jnp.arange(experts, dtype=jnp.int32) ^ own_expert
    mine = (jnp.arange(experts, dtype=jnp.int32) == own_expert).astype(F32)
    taken = jnp.sum(masks * mine[None, None, :], axis=2)
    rank = jnp.cumsum(taken, axis=1) - taken
    select = taken[:, None, :] * (
        rank[:, None, :] == jnp.arange(capacity, dtype=F32)[None, :, None]
    ).astype(F32)
    select_low = select.astype(BF)
    steps = depth
    lots = [[k] for k in range(depth)]
    lots = lots[:1] + lots[2:] + lots[1:2]
    block_order = np.array(
        [k * PLANE + j for planes in lots for j in range(PLANE) for k in planes], dtype=np.int32
    )
    chunk_select = jnp.take(select_low, block_order, axis=0, mode="clip")
    chunk_select = chunk_select.reshape(steps, PLANE, capacity, token_rows)
    chunk_masks = jnp.take(masks, block_order, axis=0, mode="clip")
    chunk_masks = chunk_masks.reshape(steps, PLANE * token_rows, experts)
    context, output_weight, chunk_select, chunk_masks = stage(
        context, output_weight, chunk_select, chunk_masks
    )
    sides = [side.reshape(PLANE * token_rows, heads * DV) for side in context]

    def project(side):
        flat = sides[side]
        return dot_plain(flat, output_weight).reshape(PLANE, token_rows, model_width)

    given_part = hop(project(1).astype(BF), "fsdp", 1)
    own_part = project(0).astype(BF)
    shared_down_weight = both_cores(shared_down)
    own_part, given_part, shared_both, shared_down_weight = stage(
        own_part, given_part, shared_both, shared_down_weight
    )
    shared_both = swap_column(shared_both).reshape(experts * weight_rows, 2 * shared_units)
    own_rows = tokens[0].astype(F32)
    hidden = own_rows + scatter_sides(own_part, given_part)
    hidden, shared_both = stage(hidden, shared_both)
    shared_both_weight = both_cores(shared_both)
    normed2 = rms_norm(hidden, gain_two_f).astype(BF)

    def gates_of(logits, mask):
        logits = jnp.where(mask, logits, -1e30)
        odds = jnp.where(mask, jnp.exp(logits - jnp.max(logits, axis=-1, keepdims=True)), 0.0)
        return odds / jnp.sum(odds, axis=-1, keepdims=True)

    own_gates = gates_of(dot_plain(normed2, router_weight), own_mask)
    wide_unit = -(-unit // 128) * 128
    padded = cores * wide_unit

    def pad_columns(values, columns):
        return jnp.pad(values, ((0, 0), (0, columns - values.shape[1])))

    shared_router = jnp.concatenate(
        [
            pad_columns(shared_both_weight[:, start : start + unit], wide_unit)
            for start in range(0, 2 * shared_units, unit)
        ]
        + [
            pad_columns(router_weight, -(-experts // 128) * 128),
        ],
        axis=1,
    )
    shared_rows = jnp.pad(
        shared_down_weight.reshape(cores, unit, model_width),
        ((0, 0), (0, wide_unit - unit), (0, 0)),
    ).reshape(padded, model_width)

    def passes(values, compute, besides):
        def fetch(values, number):
            return jnp.stack([hop(values, "z", k) if k else values for k in lots[number]], axis=0)

        source, pieces, totals, summed = fetch(values, 0), None, None, None
        returned, results = [], []
        for step in range(steps + 3):
            later = [values, None, None, None, None, None]
            if step + 1 < steps:
                later[1] = fetch(values, step + 1)
            if pieces is not None:
                later[3] = compute(step - 1, pieces, results)
            if source is not None and totals is not None:
                count, half = source.shape[0], source.shape[1] // 2
                along, across = [
                    hop(jnp.concatenate([source, totals[j]], axis=0), "r", j) for j in (1, 2)
                ]
                opposite = hop(totals[3], "r", 3)
                behind = later[3][1]
                far = jnp.concatenate(
                    [
                        hop(after(along[:count, :half], behind), "r", 2),
                        hop(after(across[:count, half:], behind), "r", 1),
                    ],
                    axis=1,
                )
                later[2] = [source, along[:count], across[:count], far]
                later[4] = totals[0] + sum(
                    part.astype(F32) for part in (along[count:], across[count:], opposite)
                )
            elif source is not None:
                later[2] = gather_plane(source)
            elif totals is not None:
                later[4] = scatter_plane(totals)
            if summed is not None:
                later[5] = [
                    hop(summed[i].astype(BF), "z", k) if k else summed[i]
                    for i, k in enumerate(lots[step - 3])
                ]
            later.append(besides(step, summed if totals is None else totals[0], results))
            values, source, pieces, totals, summed, back, beside = lax.optimization_barrier(later)
            if beside is not None:
                results.append(beside)
            if back is not None:
                returned += [part.astype(F32) for part in back]
        return sum(returned), results

    def forward_chunk(number, pieces, results):
        values = expert_forward(
            pieces, chunk_select[number], chunk_masks[number], mine[None], results[0][0],
            expert_both_weight, expert_down_weight, results[0][1],
        )
        arrived.append([piece.reshape(-1, model_width) for piece in pieces])
        saved.append(values[:7])
        return list(values[7:])

    def backward_chunk(number, pieces, results):
        gates, expert_in, expert_gu, expert_act, expert_out, shared_gu, shared_act = saved[number]
        values = expert_backward(
            pieces, chunk_select[number], gates, expert_gu, expert_out, shared_gu, shared_router,
            expert_both_weight, expert_down_weight, shared_rows,
        )
        grad_arrived.append([piece.reshape(-1, model_width) for piece in pieces])
        grads.append(values[:4])
        return list(values[4:])

    arrived, saved, grad_arrived, grads = [], [], [], []
    routed, results = passes(
        normed2,
        forward_chunk,
        lambda step, behind, results: (shared_router, shared_rows, chunk_select, chunk_masks)
        if step == 0
        else None,
    )
    shared_router, shared_rows = results[0][:2]
    output = hidden + routed
    misfit = output - teacher[0].astype(F32)
    misfit_low = misfit.astype(BF)

    def products(lefts, rights, behind, tall, wide=None):
        return sums_of_products([after(lefts[0], behind)] + lefts[1:], rights, tall, wide)

    def kept(lists, entry):
        return [values[entry] for values in lists]

    def joined(lists):
        return [piece for pieces in lists for piece in pieces]

    def weight_grads(step, behind, results):
        if step == steps + 1:
            grad_gate = jnp.concatenate([values[0][:, 0] for values in grads], axis=0)
            grad_gate = jnp.take(
                after(grad_gate.reshape(experts, token_rows), behind),
                np.argsort(block_order), axis=0, mode="clip",
            )
            squares = jnp.broadcast_to(jnp.sum(misfit * misfit)[None, None], (experts, 128))
            notes = jnp.concatenate([jnp.take(grad_gate, order, axis=0, mode="clip"), squares], axis=1)
            return (
                products(joined(arrived), kept(grads, 3), behind, 512),
                products(kept(saved, 6), joined(grad_arrived), behind, padded, 512),
                notes,
            )
        if step == steps + 2:
            notes = lax.all_to_all(results[0][2], ("z", "r"), split_axis=0, concat_axis=0, tiled=True)
            return products(kept(saved, 3), kept(grads, 1), behind, FFE, 512), notes
        return None

    grad_returned, results = passes(misfit_low, backward_chunk, weight_grads)
    grad_shared, (grad_expert_down, notes) = results
    grad_shared_both, grad_shared_down = grad_shared[:2]
    grad_expert_down = lax.psum_scatter(
        grad_expert_down[None], "fsdp", scatter_dimension=2, tiled=True
    )
    grad_shared_down = lax.psum_scatter(
        grad_shared_down, "fsdp", scatter_dimension=0, tiled=True
    )[:unit]
    grad_shared_both = lax.psum_scatter(
        grad_shared_both, "fsdp", scatter_dimension=0, tiled=True
    )
    grad_shared_both = jnp.concatenate(
        [
            grad_shared_both[:, start : start + unit].astype(BF)
            for start in range(0, 2 * padded, wide_unit)
        ],
        axis=1,
    )
    grad_shared_both = lax.all_to_all(
        grad_shared_both.reshape(experts, weight_rows, 2 * shared_units),
        ("z", "r"),
        split_axis=0,
        concat_axis=0,
        tiled=True,
    )

    grad_gates = notes[:, :token_rows].T
    all_squares = jnp.sum(notes[:, token_rows])[None]
    all_squares = all_squares + hop(jnp.broadcast_to(all_squares, (8, 128)), "fsdp", 1)[0, :1]
    loss_value = all_squares / (token_count.astype(F32) * model_width)
    grad_logits = (
        own_gates * (grad_gates - jnp.sum(own_gates * grad_gates, axis=1, keepdims=True))
    ).astype(BF)
    grad_normed2 = grad_returned + dot_last(grad_logits, router_weight)
    grad_hidden_norm, grad_gain_two = norm_back(hidden, gain_two_f, grad_normed2)
    grad_hidden = misfit + grad_hidden_norm
    near_grad = jnp.stack(gather_plane(grad_hidden.astype(BF)), axis=0)
    grad_expert_gate_up = products(kept(saved, 1), kept(grads, 2), grad_hidden, 256)
    near_grad, grad_expert_gate_up, grad_shared_both = stage(
        near_grad, grad_expert_gate_up, grad_shared_both
    )
    grad_expert_gate_up = lax.psum_scatter(
        grad_expert_gate_up[None], "fsdp", scatter_dimension=1, tiled=True
    )
    away_grad = hop(near_grad, "fsdp", 1)
    flat = (PLANE * token_rows, model_width)
    grad_output_weight = sums_of_products(
        sides,
        [near_grad.reshape(flat), away_grad.reshape(flat)],
        heads * DV,
        512,
        BF,
    )
    grad_output_weight = by_column(grad_output_weight.reshape(depth, weight_rows, model_width))
    grad_router = dot_first(normed2, grad_logits)
    grad_output_weight, away_grad, grad_router = stage(grad_output_weight, away_grad, grad_router)
    grad_output_weight = sum_columns(grad_output_weight).astype(BF)
    grad_query_weight, grad_up, own_part, given_part = attend_back(
        near_grad, away_grad, output_weight, queries, key_rope, keyval, attention,
        normed, compressed, query_weight, up_weight, spread_cos, spread_sin,
    )
    grad_query_weight, grad_up, own_part, given_part, grad_output_weight = stage(
        grad_query_weight, grad_up, own_part, given_part, grad_output_weight
    )
    grad_packed = jnp.concatenate([grad_query_weight, grad_up.reshape(model_width, up_fold)], axis=1)
    grad_packed = grad_packed.reshape(cores, depth, PLANE * weight_rows, wide_q + up_fold)
    grad_packed = grad_packed.swapaxes(0, 1)
    given_part = hop(given_part, "fsdp", 1)
    own_part, given_part, grad_packed = stage(own_part, given_part, grad_packed)
    grad_packed = lax.all_to_all(grad_packed, "z", split_axis=0, concat_axis=0, tiled=True)
    normed_sum = scatter_sides(own_part, given_part)
    latent_sum = normed_sum[:, model_width:]
    own_latent = latent[:token_rows]
    grad_latent_norm, grad_latent_gain = norm_back(
        own_latent[:, :KVR], latent_gain_f, latent_sum[:, :KVR]
    )
    grad_latent = jnp.concatenate(
        [
            grad_latent_norm,
            unrotate(latent_sum[:, KVR : KVR + DR], cosine[:token_rows], sine_table[:token_rows]),
        ],
        axis=1,
    ).astype(BF)
    own_normed = normed[:token_rows]
    grad_normed = normed_sum[:, :model_width] + dot_last(grad_latent, down_weight)
    grad_flat_norm, grad_gain_one = norm_back(own_rows, gain_one_f, grad_normed)
    grad_tokens = grad_hidden + grad_flat_norm
    grad_latent_gain = jnp.pad(
        grad_latent_gain.reshape(-1, latent_rows), ((0, 0), (0, weight_rows - latent_rows))
    ).reshape(model_width)
    base = KVR + DR + experts
    columns = jnp.arange(small_width, dtype=jnp.int32)[None, :]

    def widen(values, start):
        return jnp.pad(values, ((0, 0), (start, small_width - start - values.shape[1])))

    grad_small = (
        dot_first(own_normed, widen(grad_latent, 0))
        + widen(grad_router, KVR + DR)
        + jnp.where(columns == base, grad_gain_one[:, None], 0.0)
        + jnp.where(columns == base + 1, grad_gain_two[:, None], 0.0)
        + jnp.where(columns == base + 2, grad_latent_gain[:, None], 0.0)
    )
    grad_small = straight(grad_small.astype(BF)).reshape(devices, weight_rows, small_width)
    grad_small = jnp.take(grad_small, everywhere, axis=0, mode="clip")
    grad_small = grad_small.reshape(cores, depth, PLANE, weight_rows, small_width)
    grad_tail = grad_small[0].astype(F32) + hop(grad_small[1], "fsdp", 1).astype(F32)
    grad_tail, grad_packed, grad_output_weight = stage(
        straight(grad_tail.astype(BF)), grad_packed, grad_output_weight
    )
    grad_packed = jnp.sum(grad_packed.astype(F32), axis=0).astype(BF)
    grad_shared_gate_up = (
        after(grad_shared_both, grad_tail)
        .reshape(experts, weight_rows, 2 * cores, unit)
        .transpose(1, 2, 0, 3)
        .reshape(weight_rows, 2 * FFS)
        .astype(F32)
    )
    grad_packed = lax.all_to_all(
        grad_packed.reshape(group, weight_rows, wide_q + up_fold),
        ("fsdp", "r"),
        split_axis=0,
        concat_axis=0,
        tiled=True,
    )
    grad_small = scatter_plane([grad_tail[:, j] for j in range(PLANE)])
    grad_output_weight = lax.ppermute(
        grad_output_weight, ("z", "r"), [(b, a) for a, b in shard_moves]
    )
    grad_small, grad_packed, grad_output_weight = stage(
        grad_small, grad_packed, grad_output_weight
    )
    grad_output_weight = grad_output_weight.astype(F32)
    grad_packed = grad_packed.swapaxes(0, 1)
    grad_small = grad_small[0] + sum(
        hop(grad_small[k].astype(BF), "z", k).astype(F32) for k in range(1, depth)
    )
    grad_q_weight = jnp.concatenate(
        [
            grad_packed[:, :, : heads * DN].reshape(weight_rows, group, heads, DN),
            grad_packed[:, :, heads * DN : wide_q].reshape(weight_rows, group, heads, DR),
        ],
        axis=3,
    )
    grad_q_weight = grad_q_weight.reshape(weight_rows, -1).astype(F32)
    grad_kv_up = (
        grad_packed[:, :, wide_q:]
        .reshape(latent_rows, fold, group, up_fold)
        .swapaxes(1, 2)
        .reshape(latent_rows, -1)
        .astype(F32)
    )
    return (
        output.astype(BF)[None],
        loss_value,
        grad_tokens[None],
        grad_small[:, base],
        grad_q_weight,
        grad_small[:, : KVR + DR],
        grad_small[:latent_rows, base + 2],
        grad_kv_up,
        grad_output_weight,
        grad_small[:, base + 1],
        grad_small[:, KVR + DR : base],
        grad_shared_gate_up,
        grad_shared_down,
        grad_expert_gate_up,
        grad_expert_down,
    )


def solution(mesh):
    cores = mesh.shape["fsdp"]
    experts = mesh.shape["expert"]
    grid = Mesh(mesh.devices.reshape(cores, experts // PLANE, PLANE), ("fsdp", "z", "r"))
    expert = ("z", "r")
    every = ("fsdp", "z", "r")
    return jax.shard_map(
        on_device,
        mesh=grid,
        in_specs=(
            P(expert, "fsdp", None),
            P(every),
            P(every, None),
            P(every, None),
            P(every),
            P(every, None),
            P(every, None),
            P(every),
            P(every, None),
            P(every, None),
            P(every, None),
            P(expert, "fsdp", None),
            P(expert, None, "fsdp"),
            P(expert, "fsdp", None),
            P(expert, "fsdp", None),
            P(expert),
            P(),
        ),
        out_specs=(
            P(expert, "fsdp", None),
            P(),
            P(expert, "fsdp", None),
            P(every),
            P(every, None),
            P(every, None),
            P(every),
            P(every, None),
            P(every, None),
            P(every),
            P(every, None),
            P(every, None),
            P(every, None),
            P(expert, "fsdp", None),
            P(expert, None, "fsdp"),
        ),
        check_vma=False,
    )
```
